128 devices in a mesh: sample: 16 (over x, z_hi, core), tok: 8 (over z_lo, y).
Axes of the slice: x: 4, y: 4, z: 4 (z_hi: 2, z_lo: 2; z = z_hi * 2 + z_lo), core: 2. Of those that a mesh axis runs over, the one named last changes fastest.
Arguments:
- act: bfloat16 [32, 1024, 768], P('sample', 'tok'), may hold values from -500 to 500, as said below
- pair_bias: bfloat16 [16, 1024, 1024], P(None, 'tok'), may hold values from -12 to 260
- ln_gain: float32 [768], replicated, may hold values from 0.5 to 1.5
- w_in: bfloat16 [768, 3072], replicated, may hold values from -0.21875 to 0.21875
- w_out: bfloat16 [768, 768], replicated, may hold values from -0.21875 to 0.21875
- d_out: bfloat16 [32, 1024, 768], P('sample', 'tok'), may hold values from -6 to 6
Outputs:
- result: bfloat16 [32, 1024, 768], P('sample', 'tok')
- grad_act: bfloat16 [32, 1024, 768], P('sample', 'tok')
- grad_bias: float32 [16, 1024, 1024], P(None, 'tok', 'sample')
- grad_gain: float32 [768], replicated
- grad_win: float32 [768, 3072], P(None, ('sample', 'tok'))
- grad_wout: float32 [768, 768], P(None, ('sample', 'tok'))
The draws below stay inside these ranges and needn't reach their ends.
Inputs may be any that keep to these rules, and one draw needn't show every extreme that they name: `act`: activations of order one to some hundreds; channels and tokens have scales of their own.
All inputs are finite; a program needn't handle non-finite values.
Results may differ from the reference program's by a relative error of at most 0.017.
Values may be sent and summed in bfloat16 or wider, within the bound.
No kernel may reach another device: no remote copies, remote signals or barrier semaphores. Data moves between devices by JAX's collectives and lax.ppermute only.
A program may use at most 192 MiB of HBM per device.

```python
import math
import jax
import jax.numpy as jnp
from jax import lax

C = 768
H = 16
DH = 48
SAMPLES = 32
TOKENS = 1024


def draw_act(key, part):
    key = jax.random.fold_in(key, 1)
    first, second, third = jax.random.split(key, 3)
    shape = (SAMPLES, TOKENS, C)
    base = jnp.clip(jax.random.normal(first, shape, jnp.float32), -5.0, 5.0)
    column_scale = jnp.exp(jax.random.uniform(second, (1, 1, C), jnp.float32) * math.log(10.0))
    row_scale = jnp.exp(jax.random.uniform(third, (SAMPLES, TOKENS, 1), jnp.float32) * math.log(10.0))
    return (base * column_scale * row_scale).astype(jnp.bfloat16)


def draw_pair_bias(key, part):
    key = jax.random.fold_in(key, 2)
    first = jax.random.fold_in(key, 0)
    shape = (H, TOKENS, TOKENS)
    base = jnp.clip(jax.random.normal(first, shape, jnp.float32) * 2.0, -8.0, 8.0)
    return base.astype(jnp.bfloat16)


def with_spikes(result, key, source, target, blocks, factor):
    def block_of(axis_at):
        return (jnp.arange(result.shape[axis_at]) // (result.shape[axis_at] // blocks)).reshape((-1,) + (1,) * (result.ndim - 1 - axis_at))

    near = jax.random.permutation(key, blocks)[block_of(target)]
    far = (block_of(target) + blocks // 2) % blocks
    return jnp.where((block_of(source) == near) | (block_of(source) == far), factor * result, result)


def steps_of(own_key, shape, pieces, smallest, largest):
    gain = 1.0
    for position, parts in pieces:
        steps = jax.random.uniform(jax.random.fold_in(jax.random.fold_in(own_key, 6), position), (parts,), jnp.float32, smallest / len(pieces), largest / len(pieces))
        gain = gain * jnp.repeat(jnp.exp(steps), shape[position] // parts).reshape((-1,) + (1,) * (len(shape) - 1 - position))
    return gain


def centred(key, dims, width, limit, shards=(), kind=jnp.bfloat16):
    entries = jax.random.normal(key, dims, jnp.float32) * width
    if len(shards) > 0:
        entries = steps_of(key, dims, shards, -0.22, 0.18) * entries
    return jnp.clip(entries, min=-limit, max=limit).astype(kind)


def heavy_noise(key, shape, scale, limit, shards, heavy, kind=jnp.bfloat16):
    drawn = scale * jax.random.normal(key, shape, jnp.float32)
    if shards:
        drawn = drawn * steps_of(key, shape, shards, -0.22, 0.18)
    return jnp.clip(with_spikes(drawn, jax.random.fold_in(key, 3), *heavy), -limit, limit).astype(kind)


def setup_inputs(seed: int = 0) -> dict:
    key_of = jax.random.split(jax.random.key(seed), 7)
    act = draw_act(jax.random.fold_in(key_of[6], 71), 0)
    pair_bias = draw_pair_bias(jax.random.fold_in(key_of[6], 71), 0)
    ln_gain = jnp.clip(1.0 + 0.1 * jax.random.normal(key_of[2], (C,), jnp.float32), 0.5, 1.5)
    w_in = centred(key_of[3], (C, 4 * C), C ** -0.5, 0.21875)
    w_out = centred(key_of[4], (C, C), C ** -0.5, 0.21875)
    d_out = heavy_noise(key_of[5], (SAMPLES, TOKENS, C), 1.0, 6.0, ((0, 16), (1, 8)), (0, 2, 16, 2.0))
    return {"act": act, "pair_bias": pair_bias, "ln_gain": ln_gain, "w_in": w_in, "w_out": w_out, "d_out": d_out}


EPS = 1e-05

def reference(act, pair_bias, ln_gain, w_in, w_out, d_out):
    score_scale = 1.0 / math.sqrt(DH)
    bias_float = pair_bias.astype(jnp.float32)

    def one_sample(carry, inputs):
        bias_total, gain_total, win_total, wout_total = carry
        act_rows, cotangent = inputs
        values_f = act_rows.astype(jnp.float32)
        center = lax.optimization_barrier(jnp.mean(values_f, -1, keepdims=True))
        spread = lax.optimization_barrier(jnp.mean((values_f - center) ** 2, -1, keepdims=True))
        inv_std = lax.rsqrt(spread + EPS)
        normed = (values_f - center) * inv_std
        scaled = (normed * ln_gain).astype(jnp.bfloat16)
        projected = jnp.dot(scaled, w_in, preferred_element_type=jnp.float32)
        query_rows = projected[:, :C].astype(jnp.bfloat16)
        key_part = projected[:, C:2 * C].astype(jnp.bfloat16)
        value_part = projected[:, 2 * C:3 * C].astype(jnp.bfloat16)
        gate_open = jax.nn.sigmoid(projected[:, 3 * C:])
        query_heads = query_rows.astype(jnp.float32).reshape(TOKENS, H, DH)
        key_heads = key_part.astype(jnp.float32).reshape(TOKENS, H, DH)
        value_heads = value_part.astype(jnp.float32).reshape(TOKENS, H, DH)
        scores = jnp.einsum('qhd,khd->hqk', query_heads, key_heads) * score_scale + bias_float
        attn_probs = jax.nn.softmax(scores, axis=-1)
        probs_low = attn_probs.astype(jnp.bfloat16)
        attended = jnp.einsum('hqk,khd->qhd', probs_low.astype(jnp.float32), value_heads).reshape(TOKENS, C)
        gated = (attended * gate_open).astype(jnp.bfloat16)
        output = jnp.dot(gated, w_out, preferred_element_type=jnp.float32).astype(jnp.bfloat16)
        grad_gated = jnp.dot(cotangent, w_out.T, preferred_element_type=jnp.float32).astype(jnp.bfloat16)
        gated_float = grad_gated.astype(jnp.float32)
        wout_total = wout_total + jnp.dot(gated.T, cotangent, preferred_element_type=jnp.float32)
        grad_attended = (gated_float * gate_open).astype(jnp.bfloat16)
        grad_gatepre = gated_float * attended * gate_open * (1.0 - gate_open)
        attended_heads = grad_attended.astype(jnp.float32).reshape(TOKENS, H, DH)
        grad_probs = jnp.einsum('qhd,khd->hqk', attended_heads, value_heads)
        delta_sum = lax.optimization_barrier(jnp.sum(attn_probs * grad_probs, -1, keepdims=True))
        grad_scores = attn_probs * (grad_probs - delta_sum)
        bias_total = bias_total + grad_scores
        scores_low = grad_scores.astype(jnp.bfloat16).astype(jnp.float32)
        grad_query = jnp.einsum('hqk,khd->qhd', scores_low, key_heads).reshape(TOKENS, C) * score_scale
        grad_key = jnp.einsum('hqk,qhd->khd', scores_low, query_heads).reshape(TOKENS, C) * score_scale
        grad_value = jnp.einsum('hqk,qhd->khd', probs_low.astype(jnp.float32), attended_heads).reshape(TOKENS, C)
        grad_proj = jnp.concatenate([grad_query, grad_key, grad_value, grad_gatepre], -1).astype(jnp.bfloat16)
        win_total = win_total + jnp.dot(scaled.T, grad_proj, preferred_element_type=jnp.float32)
        grad_scaled = jnp.dot(grad_proj, w_in.T, preferred_element_type=jnp.float32)
        gain_total = gain_total + lax.optimization_barrier(jnp.sum(grad_scaled * normed, 0))
        grad_normed = grad_scaled * ln_gain
        grad_rows = inv_std * (grad_normed - lax.optimization_barrier(jnp.mean(grad_normed, -1, keepdims=True)) - normed * lax.optimization_barrier(jnp.mean(grad_normed * normed, -1, keepdims=True)))
        return ((bias_total, gain_total, win_total, wout_total), (output, grad_rows.astype(jnp.bfloat16)))
    start = (jnp.zeros((H, TOKENS, TOKENS), jnp.float32), jnp.zeros((C,), jnp.float32), jnp.zeros((C, 4 * C), jnp.float32), jnp.zeros((C, C), jnp.float32))
    totals, stacked = lax.scan(one_sample, start, (act, d_out))
    return (stacked[0], stacked[1], totals[0], totals[1], totals[2], totals[3])
```

```python
import functools
import math

import jax
import jax.numpy as jnp
from jax import lax
from jax.experimental import pallas as pl
from jax.experimental.pallas import tpu as pltpu
from jax.sharding import Mesh
from jax.sharding import PartitionSpec as P

EPS = 1e-05
LOG2E = math.log2(math.e)
BF = jnp.bfloat16
F32 = jnp.float32
HEADS = 16
DH = 48
TOK = 128
KEYS = 1024
PLANE = ("zh", "zl", "y")


def dot(a, b):
    return jnp.dot(a, b, preferred_element_type=F32)


def attention_kernel(
    x_ref, bias_ref, out_ref, gbias_ref, qa_s, ka_s, va_s, vt_s, kn_s, gn_s, qt_s, dk_s, dv_s, gb_s, *, rows
):
    sample = pl.program_id(0)
    block = pl.program_id(1)
    last_block = pl.num_programs(1) - 1
    half = sample // 2
    lane0 = pl.multiple_of((sample % 2) * TOK, TOK)
    scale = 1.0 / math.sqrt(DH)
    per_block = rows // TOK

    @pl.when(block == 0)
    def _():
        whole = jnp.concatenate(
            [x_ref[half * 8 + t, :, pl.ds(lane0, TOK)] for t in range(8)], axis=1
        )
        qt, kt, vt, gt = (whole[i * DH : (i + 1) * DH] for i in range(4))
        qs = qt.astype(F32) * (scale * LOG2E)
        q_hi = qs.astype(BF)
        q_lo = (qs - q_hi.astype(F32)).astype(BF)
        zeros32 = jnp.zeros((32, KEYS), BF)
        zeros64 = jnp.zeros((64, KEYS), BF)
        zeros80 = jnp.zeros((80, KEYS), BF)
        ones16 = jnp.ones((16, KEYS), BF)
        qa_s[...] = jnp.concatenate([q_hi, q_lo, zeros32], axis=0).T
        ka_s[...] = jnp.concatenate([kt, kt, zeros32], axis=0)
        v_one = jnp.concatenate([vt, ones16, zeros64], axis=0)
        va_s[...] = v_one
        vt_s[...] = v_one.T
        kn_s[...] = jnp.concatenate([kt, zeros80], axis=0).T
        gn_s[...] = jnp.concatenate([gt, zeros80], axis=0).T
        qt_s[...] = qt
        dk_s[...] = jnp.zeros_like(dk_s)
        dv_s[...] = jnp.zeros_like(dv_s)

    row0 = pl.multiple_of(block * rows, rows)
    these = pl.ds(row0, rows)
    scores = dot(qa_s[these, :], ka_s[...]) + bias_ref[these, :].astype(F32) * LOG2E
    top = jnp.max(scores, axis=1, keepdims=True)
    expd = jnp.exp2(scores - top)
    expd_low = expd.astype(BF)
    summed = dot(expd_low, vt_s[...])
    inv = 1.0 / summed[:, DH : DH + 1]
    out = summed * inv
    gscaled = (gn_s[these, :].astype(F32) * inv).astype(BF)
    gscaled_f = gscaled.astype(F32)
    delta = jnp.sum(out * gscaled_f, axis=1, keepdims=True)
    delta_hi = delta.astype(BF).astype(F32)
    delta_lo = delta - delta_hi
    lane = lax.broadcasted_iota(jnp.int32, (rows, 128), 1)
    left = jnp.where(
        lane == DH, -delta_hi, jnp.where(lane == DH + 1, -delta_lo, gscaled_f)
    ).astype(BF)
    dscores = expd * dot(left, va_s[...])
    dscores_low = dscores.astype(BF)

    @pl.when(sample == 0)
    def _():
        gb_s[these, :] = dscores

    @pl.when(sample > 0)
    def _():
        gb_s[these, :] = gb_s[these, :] + dscores

    @pl.when(sample == pl.num_programs(0) - 1)
    def _():
        gbias_ref[these, :] = gb_s[these, :].astype(BF)

    dquery = dot(dscores_low, kn_s[...]) * scale
    dk_s[...] += dot(qt_s[:, these], dscores_low)
    gscaled_t = gscaled_f.T.astype(BF)
    dv_s[...] += dot(gscaled_t[:DH], expd_low)
    out_t = out.T
    dquery_t = dquery.T
    for t in range(per_block):
        cols = slice(t * TOK, (t + 1) * TOK)
        where = half * 8 + block * per_block + t
        out_ref[where, 0:DH, pl.ds(lane0, TOK)] = out_t[:DH, cols].astype(BF)
        out_ref[where, DH : 2 * DH, pl.ds(lane0, TOK)] = dquery_t[:DH, cols].astype(BF)

    @pl.when(block == last_block)
    def _():
        for t in range(8):
            cols = slice(t * TOK, (t + 1) * TOK)
            out_ref[half * 8 + t, 2 * DH : 3 * DH, pl.ds(lane0, TOK)] = (
                dk_s[:, cols] * scale
            ).astype(BF)
            out_ref[half * 8 + t, 3 * DH : 4 * DH, pl.ds(lane0, TOK)] = dv_s[:, cols].astype(BF)


def attention(x, bias, rows=256):
    whole3 = pl.BlockSpec(x.shape, lambda s, b: (0, 0, 0))
    whole2 = pl.BlockSpec(bias.shape, lambda s, b: (0, 0))
    return pl.pallas_call(
        functools.partial(attention_kernel, rows=rows),
        grid=(4, KEYS // rows),
        in_specs=[whole3, whole2],
        out_specs=[whole3, whole2],
        out_shape=[
            jax.ShapeDtypeStruct(x.shape, BF),
            jax.ShapeDtypeStruct(bias.shape, BF),
        ],
        scratch_shapes=[
            pltpu.VMEM((KEYS, 128), BF),
            pltpu.VMEM((128, KEYS), BF),
            pltpu.VMEM((128, KEYS), BF),
            pltpu.VMEM((KEYS, 128), BF),
            pltpu.VMEM((KEYS, 128), BF),
            pltpu.VMEM((KEYS, 128), BF),
            pltpu.VMEM((DH, KEYS), BF),
            pltpu.VMEM((DH, KEYS), F32),
            pltpu.VMEM((DH, KEYS), F32),
            pltpu.VMEM((KEYS, KEYS), F32),
        ],
        compiler_params=pltpu.CompilerParams(vmem_limit_bytes=48 * 1024 * 1024),
        cost_estimate=pl.CostEstimate(
            flops=4 * 6 * 2 * KEYS * KEYS * 128, bytes_accessed=8 * 2**20, transcendentals=4 * KEYS * KEYS
        ),
        name="attention",
    )(x, bias)


def split_pair(values):
    high = lax.reduce_precision(values, 8, 7)
    return high.astype(BF), (values - high).astype(BF)


def per_device(act, pair_bias, ln_gain, w_in, w_out, d_out):
    sample_count, row_count, channels = act.shape
    flat = sample_count * row_count
    core = lax.axis_index("core")
    zh = lax.axis_index("zh")

    bias_own = lax.dynamic_slice(pair_bias, (zh * 8, core * 64, 0), (8, 64, KEYS))
    bias_own = lax.all_to_all(bias_own, ("zl", "y"), 0, 0, tiled=True)
    bias_other = lax.ppermute(bias_own, "core", [(0, 1), (1, 0)])
    first = core == 0
    bias_head = jnp.stack(
        [jnp.where(first, bias_own, bias_other), jnp.where(first, bias_other, bias_own)], axis=1
    ).reshape(KEYS, KEYS)

    values_f = act.reshape(flat, channels).astype(F32)
    center = jnp.mean(values_f, -1, keepdims=True)
    spread = jnp.mean((values_f - center) ** 2, -1, keepdims=True)
    inv_std = lax.rsqrt(spread + EPS)
    normed = (values_f - center) * inv_std
    scaled = (normed * ln_gain).astype(BF)
    rows_out = d_out.reshape(flat, channels)

    proj_t = jnp.einsum("cd,rc->dr", w_in, scaled, preferred_element_type=F32)
    gate_t = jax.nn.sigmoid(proj_t[3 * channels :])
    ggated_t = (
        jnp.einsum("cd,rd->cr", w_out, rows_out, preferred_element_type=F32).astype(BF).astype(F32)
    )
    gatt_t = (ggated_t * gate_t).astype(BF)
    send = jnp.concatenate(
        [
            proj_t[: 3 * channels].astype(BF).reshape(3, HEADS, DH, flat).transpose(1, 0, 2, 3).reshape(HEADS, 3 * DH, flat),
            gatt_t.reshape(HEADS, DH, flat),
        ],
        axis=1,
    )
    received = lax.all_to_all(send, PLANE, 0, 0, tiled=True)
    result, gbias = attention(received, bias_head)
    back = lax.all_to_all(result, PLANE, 0, 0, tiled=True)

    gb = gbias.reshape(KEYS, 4, 2, 2, 64).transpose(1, 3, 2, 0, 4).reshape(8 * 2 * KEYS, 64)
    gb = lax.psum_scatter(gb, ("x", "core"), scatter_dimension=0, tiled=True)
    gb = gb.reshape(2, 2, 4, TOK, 64).reshape(HEADS, TOK, 64)
    grad_bias = lax.all_to_all(gb, PLANE, 0, 0, tiled=True).astype(F32)

    att_t = back[:, :DH].reshape(channels, flat).astype(F32)
    gated_t = (att_t * gate_t).astype(BF)
    output = jnp.einsum("cr,cd->rd", gated_t, w_out, preferred_element_type=F32).astype(BF)
    gatepre_t = (ggated_t * att_t * gate_t * (1.0 - gate_t)).astype(BF)
    gproj_t = jnp.concatenate(
        [
            back[:, DH:].reshape(HEADS, 3, DH, flat).transpose(1, 0, 2, 3).reshape(3 * channels, flat),
            gatepre_t,
        ],
        axis=0,
    )
    win_t = dot(gproj_t, scaled).astype(BF)
    wout_t = jnp.einsum("rd,cr->dc", rows_out, gated_t, preferred_element_type=F32).astype(BF)
    grad_scaled = jnp.einsum("dr,cd->rc", gproj_t, w_in, preferred_element_type=F32)
    gain = jnp.sum(grad_scaled * normed, 0)
    grad_normed = grad_scaled * ln_gain
    grad_act = inv_std * (
        grad_normed
        - jnp.mean(grad_normed, -1, keepdims=True)
        - normed * jnp.mean(grad_normed * normed, -1, keepdims=True)
    )
    high, low = split_pair(gain)
    parts = jnp.concatenate(
        [
            win_t.reshape(128, 24, channels),
            wout_t.reshape(128, 6, channels),
            jnp.broadcast_to(high, (128, 1, channels)),
            jnp.broadcast_to(low, (128, 1, channels)),
        ],
        axis=1,
    )
    parts = parts.reshape(8, 2, 8, 32, channels).transpose(1, 0, 2, 3, 4).reshape(2, 64, 32, channels)
    parts = lax.all_to_all(parts, "core", 0, 0, tiled=True)
    pair = parts[0].astype(F32) + parts[1].astype(F32)
    high, low = split_pair(pair[:, 30:31] + pair[:, 31:32])
    parts = jnp.concatenate([pair[:, :30].astype(BF), high, low], axis=1)
    parts = lax.all_to_all(parts, ("x", "zh", "zl", "y"), 0, 0, tiled=True)
    total = jnp.sum(parts.astype(F32), axis=0)
    return (
        output.reshape(sample_count, row_count, channels),
        grad_act.astype(BF).reshape(sample_count, row_count, channels),
        grad_bias,
        total[30] + total[31],
        total[:24].T,
        total[24:30].T,
    )


def solution(mesh):
    fine = Mesh(mesh.devices.reshape(4, 2, 2, 2, 4), ("x", "zh", "core", "zl", "y"))
    sample = ("x", "zh", "core")
    tok = ("zl", "y")
    return jax.shard_map(
        per_device,
        mesh=fine,
        in_specs=(
            P(sample, tok, None),
            P(None, tok, None),
            P(),
            P(),
            P(),
            P(sample, tok, None),
        ),
        out_specs=(
            P(sample, tok, None),
            P(sample, tok, None),
            P(None, tok, sample),
            P(),
            P(None, sample + tok),
            P(None, sample + tok),
        ),
        check_vma=False,
    )
```

```python
import functools
import math

import jax
import jax.numpy as jnp
from jax import lax
from jax.experimental import pallas as pl
from jax.experimental.pallas import tpu as pltpu
from jax.sharding import Mesh
from jax.sharding import PartitionSpec as P

EPS = 1e-05
LOG2E = math.log2(math.e)
BF = jnp.bfloat16
F32 = jnp.float32
C = 768
HEADS = 16
DH = 48
TOK = 128
KEYS = 1024
PLANE = ("zh", "zl", "y")
SWAP = [(0, 1), (1, 0)]
SCALE = 1.0 / math.sqrt(DH)
VMEM_LIMIT = 48 * 1024 * 1024


def dot(a, b):
    return jnp.dot(a, b, preferred_element_type=F32)


def dot_nt(a, b):
    return lax.dot_general(a, b, (((1,), (1,)), ((), ())), preferred_element_type=F32)


def params():
    return pltpu.CompilerParams(vmem_limit_bytes=VMEM_LIMIT)


def front_kernel(
    act_ref, gain_ref, w_ref, wout_ref, dout_ref,
    scaled_ref, normed_ref, inv_ref, send0_ref, send1_ref, gate0_ref, gate1_ref, gg0_ref, gg1_ref,
):
    step = pl.program_id(0)
    sends = (send0_ref, send1_ref)

    @pl.when(step == 0)
    def _():
        values = act_ref[...].astype(F32)
        center = jnp.mean(values, -1, keepdims=True)
        shifted = values - center
        spread = jnp.mean(shifted * shifted, -1, keepdims=True)
        inv_std = lax.rsqrt(spread + EPS)
        normed = shifted * inv_std
        normed_ref[...] = normed
        inv_ref[...] = inv_std
        scaled_ref[...] = (normed * gain_ref[...]).astype(BF)

    block = dot(scaled_ref[...], w_ref[...])

    for kind in range(3):

        @pl.when(step == kind)
        def _(kind=kind):
            low = block.astype(BF).T
            for j in range(2):
                sends[j][:, kind * DH : (kind + 1) * DH, :] = low[:, j * TOK : (j + 1) * TOK].reshape(
                    HEADS, DH, TOK
                )

    @pl.when(step == 3)
    def _():
        gate = jax.nn.sigmoid(block.T)
        ggated = dot_nt(wout_ref[...], dout_ref[...]).astype(BF)
        gatt = (ggated.astype(F32) * gate).astype(BF)
        for j, gate_ref, gg_ref in ((0, gate0_ref, gg0_ref), (1, gate1_ref, gg1_ref)):
            cols = slice(j * TOK, (j + 1) * TOK)
            gate_ref[...] = gate[:, cols]
            gg_ref[...] = ggated[:, cols]
            sends[j][:, 3 * DH : 4 * DH, :] = gatt[:, cols].reshape(HEADS, DH, TOK)


def front(act, ln_gain, w_in, w_out, d_out):
    flat = act.shape[0]
    shapes = [
        ((flat, C), BF),
        ((flat, C), F32),
        ((flat, 1), F32),
        ((HEADS, 4 * DH, TOK), BF),
        ((HEADS, 4 * DH, TOK), BF),
        ((C, TOK), F32),
        ((C, TOK), F32),
        ((C, TOK), BF),
        ((C, TOK), BF),
    ]

    def whole(shape):
        return pl.BlockSpec(shape, lambda t: (0,) * len(shape))

    return pl.pallas_call(
        front_kernel,
        grid=(4,),
        in_specs=[
            whole((flat, C)),
            whole((1, C)),
            pl.BlockSpec((C, C), lambda t: (0, t)),
            whole((C, C)),
            whole((flat, C)),
        ],
        out_specs=[whole(s) for s, _ in shapes],
        out_shape=[jax.ShapeDtypeStruct(s, d) for s, d in shapes],
        compiler_params=params(),
        cost_estimate=pl.CostEstimate(
            flops=2 * flat * C * 5 * C, bytes_accessed=11 * 2**20, transcendentals=flat * C
        ),
        name="front",
    )(act, ln_gain, w_in, w_out, d_out)


def attention_kernel(*refs, rows, first):
    if first:
        x_ref, bias_ref, out_ref, gsum_ref = refs[:4]
        gin_ref = None
    else:
        x_ref, bias_ref, gin_ref, out_ref, gsum_ref = refs[:5]
    qa_s, ka_s, va_s, vt_s, kn_s, gn_s, qt_s, dk_s, dv_s, gb_s = refs[-10:]
    half = pl.program_id(0)
    block = pl.program_id(1)
    last_block = pl.num_programs(1) - 1
    per_block = rows // TOK

    @pl.when(block == 0)
    def _():
        whole = jnp.concatenate([x_ref[half * 8 + t] for t in range(8)], axis=1)
        qt, kt, vt, gt = (whole[i * DH : (i + 1) * DH] for i in range(4))
        qs = qt.astype(F32) * (SCALE * LOG2E)
        q_hi = qs.astype(BF)
        q_lo = (qs - q_hi.astype(F32)).astype(BF)
        zeros32 = jnp.zeros((32, KEYS), BF)
        zeros64 = jnp.zeros((64, KEYS), BF)
        zeros80 = jnp.zeros((80, KEYS), BF)
        ones16 = jnp.ones((16, KEYS), BF)
        qa_s[...] = jnp.concatenate([q_hi, q_lo, zeros32], axis=0).T
        ka_s[...] = jnp.concatenate([kt, kt, zeros32], axis=0)
        v_one = jnp.concatenate([vt, ones16, zeros64], axis=0)
        va_s[...] = v_one
        vt_s[...] = v_one.T
        kn_s[...] = jnp.concatenate([kt, zeros80], axis=0).T
        gn_s[...] = jnp.concatenate([gt, zeros80], axis=0).T
        qt_s[...] = qt
        dk_s[...] = jnp.zeros_like(dk_s)
        dv_s[...] = jnp.zeros_like(dv_s)

    row0 = pl.multiple_of(block * rows, rows)
    these = pl.ds(row0, rows)
    scores = dot(qa_s[these, :], ka_s[...]) + bias_ref[these, :].astype(F32) * LOG2E
    top = jnp.max(scores, axis=1, keepdims=True)
    expd = jnp.exp2(scores - top)
    expd_low = expd.astype(BF)
    summed = dot(expd_low, vt_s[...])
    inv = 1.0 / summed[:, DH : DH + 1]
    out = summed * inv
    gscaled = (gn_s[these, :].astype(F32) * inv).astype(BF)
    gscaled_f = gscaled.astype(F32)
    delta = jnp.sum(out * gscaled_f, axis=1, keepdims=True)
    delta_hi = delta.astype(BF).astype(F32)
    delta_lo = delta - delta_hi
    lane = lax.broadcasted_iota(jnp.int32, (rows, 128), 1)
    left = jnp.where(
        lane == DH, -delta_hi, jnp.where(lane == DH + 1, -delta_lo, gscaled_f)
    ).astype(BF)
    dscores = expd * dot(left, va_s[...])
    dscores_low = dscores.astype(BF)

    if first:

        @pl.when(half == 0)
        def _():
            gsum_ref[these, :] = dscores

        @pl.when(half == 1)
        def _():
            gsum_ref[these, :] = gsum_ref[these, :] + dscores

    else:

        @pl.when(half == 0)
        def _():
            gb_s[these, :] = gin_ref[these, :] + dscores

        @pl.when(half == 1)
        def _():
            total = (gb_s[these, :] + dscores).astype(BF)
            for x in range(4):
                even = total[:, x * 256 : x * 256 + 128]
                odd = total[:, x * 256 + 128 : x * 256 + 256]
                gsum_ref[2 * x, these, :] = jnp.concatenate([even[:, :64], odd[:, :64]], axis=1)
                gsum_ref[2 * x + 1, these, :] = jnp.concatenate([even[:, 64:], odd[:, 64:]], axis=1)

    dquery = dot(dscores_low, kn_s[...]) * SCALE
    dk_s[...] += dot(qt_s[:, these], dscores_low)
    gscaled_t = gscaled_f.T.astype(BF)
    dv_s[...] += dot(gscaled_t[:DH], expd_low)
    out_t = out.T
    dquery_t = dquery.T
    for t in range(per_block):
        cols = slice(t * TOK, (t + 1) * TOK)
        where = half * 8 + block * per_block + t
        out_ref[where, 0:DH, :] = out_t[:DH, cols].astype(BF)
        out_ref[where, DH : 2 * DH, :] = dquery_t[:DH, cols].astype(BF)

    @pl.when(block == last_block)
    def _():
        for t in range(8):
            cols = slice(t * TOK, (t + 1) * TOK)
            out_ref[half * 8 + t, 2 * DH : 3 * DH, :] = (dk_s[:, cols] * SCALE).astype(BF)
            out_ref[half * 8 + t, 3 * DH : 4 * DH, :] = dv_s[:, cols].astype(BF)


def attention(x, bias, gsum=None, rows=256):
    first = gsum is None

    def whole(shape):
        return pl.BlockSpec(shape, lambda s, b: (0,) * len(shape))

    sum_shape, sum_type = ((KEYS, KEYS), F32) if first else ((8, KEYS, 128), BF)
    operands = [x, bias] + ([] if first else [gsum])
    return pl.pallas_call(
        functools.partial(attention_kernel, rows=rows, first=first),
        grid=(2, KEYS // rows),
        in_specs=[whole(o.shape) for o in operands],
        out_specs=[whole(x.shape), whole(sum_shape)],
        out_shape=[jax.ShapeDtypeStruct(x.shape, BF), jax.ShapeDtypeStruct(sum_shape, sum_type)],
        scratch_shapes=[
            pltpu.VMEM((KEYS, 128), BF),
            pltpu.VMEM((128, KEYS), BF),
            pltpu.VMEM((128, KEYS), BF),
            pltpu.VMEM((KEYS, 128), BF),
            pltpu.VMEM((KEYS, 128), BF),
            pltpu.VMEM((KEYS, 128), BF),
            pltpu.VMEM((DH, KEYS), BF),
            pltpu.VMEM((DH, KEYS), F32),
            pltpu.VMEM((DH, KEYS), F32),
            pltpu.VMEM((8, 128) if first else (KEYS, KEYS), F32),
        ],
        compiler_params=params(),
        cost_estimate=pl.CostEstimate(
            flops=2 * 6 * 2 * KEYS * KEYS * 256, bytes_accessed=8 * 2**20, transcendentals=2 * KEYS * KEYS
        ),
        name="attention",
    )(*operands)


def gate_kernel(core_ref, back_ref, gate_ref, gg_ref, gproj_ref, gated_ref, send_ref):
    other = 1 - core_ref[0]
    att = back_ref[:, :DH, :].astype(F32).reshape(C, TOK)
    gate = gate_ref[...]
    opened = att * gate
    gated = opened.astype(BF)
    gated_ref[...] = gated
    send_ref[8] = gated[: C // 4]
    send_ref[9] = gated[C // 4 : C // 2]
    send_ref[10] = gated[C // 2 : 3 * C // 4]
    send_ref[11] = gated[3 * C // 4 :]
    for kind in range(3):
        gproj_ref[kind * 4 : kind * 4 + 4] = back_ref[:, (kind + 1) * DH : (kind + 2) * DH, :].reshape(
            4, 4 * DH, TOK
        )
    gproj_ref[12:16] = (gg_ref[...].astype(F32) * opened * (1.0 - gate)).astype(BF).reshape(4, 4 * DH, TOK)
    for n in range(8):
        send_ref[n] = gproj_ref[2 * n + other]


def gate_step(core, back, gate, ggated):
    def whole(shape):
        return pl.BlockSpec(shape, lambda t, core: (0,) * len(shape))

    shapes = [(16, 4 * DH, TOK), (C, TOK), (12, 4 * DH, TOK)]
    return pl.pallas_call(
        gate_kernel,
        grid_spec=pltpu.PrefetchScalarGridSpec(
            num_scalar_prefetch=1,
            grid=(1,),
            in_specs=[whole(back.shape), whole(gate.shape), whole(ggated.shape)],
            out_specs=[whole(s) for s in shapes],
        ),
        out_shape=[jax.ShapeDtypeStruct(s, BF) for s in shapes],
        compiler_params=params(),
        cost_estimate=pl.CostEstimate(flops=6 * C * TOK, bytes_accessed=4 * 2**20, transcendentals=0),
        name="gate",
    )(core, back, gate, ggated)


def weight_kernel(
    core_ref, g0_ref, g1_ref, o0_ref, o1_ref, gated0_ref, gated1_ref, sc_ref, sco_ref, do_ref, doo_ref,
    a_ref, b_ref, c_ref, scaled_s, gated_s,
):
    core = core_ref[0]
    n = pl.program_id(0)
    x = n // 2
    zh = n % 2

    @pl.when(n == 0)
    def _():
        scaled_s[: 2 * TOK] = sc_ref[...]
        scaled_s[2 * TOK :] = sco_ref[...]
        gated_s[:TOK] = gated0_ref[...].T
        gated_s[TOK : 2 * TOK] = gated1_ref[...].T
        for q in range(4):
            lanes = slice(q * 192, (q + 1) * 192)
            gated_s[2 * TOK : 3 * TOK, lanes] = o0_ref[8 + q].T
            gated_s[3 * TOK :, lanes] = o1_ref[8 + q].T

    mine = 2 * n + core
    left = jnp.concatenate([g0_ref[mine], g1_ref[mine], o0_ref[n], o1_ref[n]], axis=1)
    win = dot(left, scaled_s[...])
    wout = dot(jnp.concatenate([do_ref[n], doo_ref[n]], axis=1), gated_s[...])
    for k in range(8):
        zl, y = k // 4, k % 4
        z = zh * 2 + zl
        chunk = jnp.concatenate([win[k * 24 : k * 24 + 24], wout[k * 8 : k * 8 + 8]], axis=0).astype(BF)
        a_ref[y, z, x] = chunk[:, :256]
        b_ref[z, x, y] = chunk[:, 256:512]
        c_ref[x, y, z] = chunk[:, 512:]


def weight_grads(core, operands):
    def whole(shape):
        return pl.BlockSpec(shape, lambda t, core: (0,) * len(shape))

    shape = (4, 4, 4, 32, 256)
    return pl.pallas_call(
        weight_kernel,
        grid_spec=pltpu.PrefetchScalarGridSpec(
            num_scalar_prefetch=1,
            grid=(8,),
            in_specs=[whole(o.shape) for o in operands],
            out_specs=[whole(shape)] * 3,
            scratch_shapes=[pltpu.VMEM((4 * TOK, C), BF), pltpu.VMEM((4 * TOK, C), BF)],
        ),
        out_shape=[jax.ShapeDtypeStruct(shape, BF)] * 3,
        compiler_params=params(),
        cost_estimate=pl.CostEstimate(
            flops=2 * 4 * TOK * C * 2048, bytes_accessed=8 * 2**20, transcendentals=0
        ),
        name="weight_grads",
    )(core, *operands)


def reduce_parts(parts):
    axes = {"x": "x", "y": "y", "z": ("zh", "zl")}
    orders = ("yzx", "zxy", "xyz")
    for stage in range(3):
        sent = [
            lax.all_to_all(p, axes[order[stage]], 0, 0, tiled=True) for p, order in zip(parts, orders)
        ]
        parts = [jnp.sum(p.astype(F32), axis=0) for p in sent]
        if stage < 2:
            parts = [p.astype(BF) for p in parts]
    return jnp.concatenate(parts, axis=-1)


def sum_everywhere(vector):
    tile = jnp.pad(vector, (0, 1024 - C)).reshape(8, 128)
    tile = jnp.sum(
        lax.all_to_all(jnp.broadcast_to(tile, (8, 8, 128)), ("x", "core"), 0, 0, tiled=True), axis=0
    )
    tile = jnp.sum(
        lax.all_to_all(jnp.broadcast_to(tile, (16, 8, 128)), PLANE, 0, 0, tiled=True), axis=0
    )
    return tile.reshape(1024)[:C]


def per_device(act, pair_bias, ln_gain, w_in, w_out, d_out):
    sample_count, row_count, channels = act.shape
    flat = sample_count * row_count
    core = lax.axis_index("core")
    core_arg = jnp.full((1,), core, jnp.int32)
    zh = lax.axis_index("zh")

    bias_own = lax.dynamic_slice(pair_bias, (zh * 8, core * 64, 0), (8, 64, KEYS))
    bias_own = lax.all_to_all(bias_own, ("zl", "y"), 0, 0, tiled=True)
    bias_other = lax.ppermute(bias_own, "core", SWAP)
    is_first = core == 0
    bias_head = jnp.stack(
        [jnp.where(is_first, bias_own, bias_other), jnp.where(is_first, bias_other, bias_own)], axis=1
    ).reshape(KEYS, KEYS)

    rows_out = d_out.reshape(flat, channels)
    scaled, normed, inv_std, send0, send1, gate0, gate1, gg0, gg1 = front(
        act.reshape(flat, channels), ln_gain.reshape(1, C), w_in, w_out, rows_out
    )
    in0 = lax.all_to_all(send0, PLANE, 0, 0, tiled=True)
    send1, in0 = lax.optimization_barrier((send1, in0))
    in1 = lax.all_to_all(send1, PLANE, 0, 0, tiled=True)

    dout_t = jnp.pad(rows_out.T.reshape(128, 6, flat), ((0, 0), (0, 2), (0, 0)))
    dout_t = dout_t.reshape(8, 2, 64, flat)
    dout_mine = lax.dynamic_index_in_dim(dout_t, core, 1, keepdims=False)
    dout_send = lax.dynamic_index_in_dim(dout_t, 1 - core, 1, keepdims=False)
    dout_other = lax.ppermute(dout_send, "core", SWAP)
    scaled_other = lax.ppermute(scaled, "core", SWAP)

    result0, gsum = attention(in0, bias_head)
    back0 = lax.all_to_all(result0, PLANE, 0, 0, tiled=True)
    result1, gsum = attention(in1, bias_head, gsum)
    back1 = lax.all_to_all(result1, PLANE, 0, 0, tiled=True)

    gb = lax.psum_scatter(gsum, ("x", "core"), scatter_dimension=0, tiled=False)
    gb = gb.reshape(8, TOK, 2, 64).transpose(2, 0, 1, 3).reshape(HEADS, TOK, 64)
    grad_bias = lax.all_to_all(gb, PLANE, 0, 0, tiled=True).astype(F32)

    gproj0, gated0, half0 = gate_step(core_arg, back0, gate0, gg0)
    other0 = lax.ppermute(half0, "core", SWAP)
    gproj1, gated1, half1 = gate_step(core_arg, back1, gate1, gg1)
    other1 = lax.ppermute(half1, "core", SWAP)
    parts = weight_grads(
        core_arg,
        (gproj0, gproj1, other0, other1, gated0, gated1, scaled, scaled_other, dout_mine, dout_other),
    )
    total = reduce_parts(parts)

    outputs = []
    grad_acts = []
    gain = jnp.zeros((C,), F32)
    for j, gproj, gated in ((0, gproj0, gated0), (1, gproj1, gated1)):
        rows = slice(j * TOK, (j + 1) * TOK)
        outputs.append(jnp.einsum("cr,cd->rd", gated, w_out, preferred_element_type=F32).astype(BF))
        grad_scaled = jnp.einsum(
            "dr,cd->rc", gproj.reshape(4 * C, TOK), w_in, preferred_element_type=F32
        )
        gain = gain + jnp.sum(grad_scaled * normed[rows], 0)
        grad_normed = grad_scaled * ln_gain
        grad_acts.append(
            (
                inv_std[rows]
                * (
                    grad_normed
                    - jnp.mean(grad_normed, -1, keepdims=True)
                    - normed[rows] * jnp.mean(grad_normed * normed[rows], -1, keepdims=True)
                )
            ).astype(BF)
        )
    return (
        jnp.stack(outputs),
        jnp.stack(grad_acts),
        grad_bias,
        sum_everywhere(gain),
        total[:24].T,
        total[24:30].T,
    )


def solution(mesh):
    fine = Mesh(mesh.devices.reshape(4, 2, 2, 2, 4), ("x", "zh", "core", "zl", "y"))
    sample = ("x", "zh", "core")
    tok = ("zl", "y")
    return jax.shard_map(
        per_device,
        mesh=fine,
        in_specs=(
            P(sample, tok, None),
            P(None, tok, None),
            P(),
            P(),
            P(),
            P(sample, tok, None),
        ),
        out_specs=(
            P(sample, tok, None),
            P(sample, tok, None),
            P(None, tok, sample),
            P(),
            P(None, sample + tok),
            P(None, sample + tok),
        ),
        check_vma=False,
    )
```

```python
import functools
import math

import jax
import jax.numpy as jnp
from jax import lax
from jax.experimental import pallas as pl
from jax.experimental.pallas import tpu as pltpu
from jax.sharding import Mesh
from jax.sharding import PartitionSpec as P

EPS = 1e-05
LOG2E = math.log2(math.e)
BF = jnp.bfloat16
F32 = jnp.float32
C = 768
HEADS = 16
DH = 48
TOK = 128
KEYS = 1024
PLANE = ("zh", "zl", "y")
SWAP = [(0, 1), (1, 0)]
SCALE = 1.0 / math.sqrt(DH)
VMEM_LIMIT = 48 * 1024 * 1024


def dot(a, b):
    return jnp.dot(a, b, preferred_element_type=F32)


def dot_nt(a, b):
    return lax.dot_general(a, b, (((1,), (1,)), ((), ())), preferred_element_type=F32)


def params():
    return pltpu.CompilerParams(vmem_limit_bytes=VMEM_LIMIT)


def front_kernel(
    act_ref, gain_ref, w_ref, wout_ref, dout_ref, scaled_ref, normed_ref, inv_ref, send_ref, gate_ref, gg_ref
):
    step = pl.program_id(0)
    flat = act_ref.shape[0]

    @pl.when(step == 0)
    def _():
        values = act_ref[...].astype(F32)
        center = jnp.mean(values, -1, keepdims=True)
        shifted = values - center
        spread = jnp.mean(shifted * shifted, -1, keepdims=True)
        inv_std = lax.rsqrt(spread + EPS)
        normed = shifted * inv_std
        normed_ref[...] = normed
        inv_ref[...] = inv_std
        scaled_ref[...] = (normed * gain_ref[...]).astype(BF)

    block = dot(scaled_ref[...], w_ref[...])

    for kind in range(3):

        @pl.when(step == kind)
        def _(kind=kind):
            send_ref[:, kind * DH : (kind + 1) * DH, :] = block.astype(BF).T.reshape(HEADS, DH, flat)

    @pl.when(step == 3)
    def _():
        gate = jax.nn.sigmoid(block.T)
        ggated = dot_nt(wout_ref[...], dout_ref[...]).astype(BF)
        gate_ref[...] = gate
        gg_ref[...] = ggated
        send_ref[:, 3 * DH : 4 * DH, :] = (ggated.astype(F32) * gate).astype(BF).reshape(HEADS, DH, flat)


def front(act, ln_gain, w_in, w_out, d_out):
    flat = act.shape[0]
    shapes = [
        ((flat, C), BF),
        ((flat, C), F32),
        ((flat, 1), F32),
        ((HEADS, 4 * DH, flat), BF),
        ((C, flat), F32),
        ((C, flat), BF),
    ]

    def whole(shape):
        return pl.BlockSpec(shape, lambda t: (0,) * len(shape))

    return pl.pallas_call(
        front_kernel,
        grid=(4,),
        in_specs=[
            whole((flat, C)),
            whole((1, C)),
            pl.BlockSpec((C, C), lambda t: (0, t)),
            whole((C, C)),
            whole((flat, C)),
        ],
        out_specs=[whole(s) for s, _ in shapes],
        out_shape=[jax.ShapeDtypeStruct(s, d) for s, d in shapes],
        compiler_params=params(),
        cost_estimate=pl.CostEstimate(
            flops=2 * flat * C * 5 * C, bytes_accessed=11 * 2**20, transcendentals=flat * C
        ),
        name="front",
    )(act, ln_gain, w_in, w_out, d_out)


def attention_kernel(
    core_ref, x_ref, bias_ref, out_ref, keep_ref, give_ref,
    qa_s, ka_s, va_s, vt_s, kn_s, gn_s, qt_s, dk_s, dv_s, gb_s, bias_s, *, rows,
):
    core = core_ref[0]
    sample = pl.program_id(0)
    block = pl.program_id(1)
    last_block = pl.num_programs(1) - 1
    half = sample // 2
    lane0 = pl.multiple_of((sample % 2) * TOK, TOK)
    per_block = rows // TOK

    @pl.when(block == 0)
    def _():
        whole = jnp.concatenate([x_ref[half * 8 + t, :, pl.ds(lane0, TOK)] for t in range(8)], axis=1)
        qt, kt, vt, gt = (whole[i * DH : (i + 1) * DH] for i in range(4))
        qs = qt.astype(F32) * (SCALE * LOG2E)
        q_hi = qs.astype(BF)
        q_lo = (qs - q_hi.astype(F32)).astype(BF)
        zeros32 = jnp.zeros((32, KEYS), BF)
        zeros64 = jnp.zeros((64, KEYS), BF)
        zeros80 = jnp.zeros((80, KEYS), BF)
        ones16 = jnp.ones((16, KEYS), BF)
        qa_s[...] = jnp.concatenate([q_hi, q_lo, zeros32], axis=0).T
        ka_s[...] = jnp.concatenate([kt, kt, zeros32], axis=0)
        v_one = jnp.concatenate([vt, ones16, zeros64], axis=0)
        va_s[...] = v_one
        vt_s[...] = v_one.T
        kn_s[...] = jnp.concatenate([kt, zeros80], axis=0).T
        gn_s[...] = jnp.concatenate([gt, zeros80], axis=0).T
        qt_s[...] = qt
        dk_s[...] = jnp.zeros_like(dk_s)
        dv_s[...] = jnp.zeros_like(dv_s)

    row0 = pl.multiple_of(block * rows, rows)
    these = pl.ds(row0, rows)

    @pl.when(sample == 0)
    def _():
        pieces = [bias_ref[p, block * per_block + t] for t in range(per_block) for p in range(8)]
        bias_s[these, :] = jnp.concatenate(pieces, axis=0).astype(F32) * LOG2E

    scores = dot(qa_s[these, :], ka_s[...]) + bias_s[these, :]
    top = jnp.max(scores, axis=1, keepdims=True)
    expd = jnp.exp2(scores - top)
    expd_low = expd.astype(BF)
    summed = dot(expd_low, vt_s[...])
    inv = 1.0 / summed[:, DH : DH + 1]
    out = summed * inv
    gscaled = (gn_s[these, :].astype(F32) * inv).astype(BF)
    gscaled_f = gscaled.astype(F32)
    delta = jnp.sum(out * gscaled_f, axis=1, keepdims=True)
    delta_hi = delta.astype(BF).astype(F32)
    delta_lo = delta - delta_hi
    lane = lax.broadcasted_iota(jnp.int32, (rows, 128), 1)
    left = jnp.where(
        lane == DH, -delta_hi, jnp.where(lane == DH + 1, -delta_lo, gscaled_f)
    ).astype(BF)
    dscores = expd * dot(left, va_s[...])
    dscores_low = dscores.astype(BF)

    @pl.when(sample == 0)
    def _():
        gb_s[these, :] = dscores

    @pl.when((sample > 0) & (sample < 3))
    def _():
        gb_s[these, :] = gb_s[these, :] + dscores

    @pl.when(sample == 3)
    def _():
        total = (gb_s[these, :] + dscores).astype(BF)
        for x in range(4):
            even = total[:, x * 256 : x * 256 + 128]
            odd = total[:, x * 256 + 128 : x * 256 + 256]
            low = jnp.concatenate([even[:, :64], odd[:, :64]], axis=1)
            high = jnp.concatenate([even[:, 64:], odd[:, 64:]], axis=1)
            keep_ref[x, these, :] = jnp.where(core == 0, low, high)
            give_ref[x, these, :] = jnp.where(core == 0, high, low)

    dquery = dot(dscores_low, kn_s[...]) * SCALE
    dk_s[...] += dot(qt_s[:, these], dscores_low)
    gscaled_t = gscaled_f.T.astype(BF)
    dv_s[...] += dot(gscaled_t[:DH], expd_low)
    out_t = out.T
    dquery_t = dquery.T
    for t in range(per_block):
        cols = slice(t * TOK, (t + 1) * TOK)
        where = half * 8 + block * per_block + t
        out_ref[where, 0:DH, pl.ds(lane0, TOK)] = out_t[:DH, cols].astype(BF)
        out_ref[where, DH : 2 * DH, pl.ds(lane0, TOK)] = dquery_t[:DH, cols].astype(BF)

    @pl.when(block == last_block)
    def _():
        for t in range(8):
            cols = slice(t * TOK, (t + 1) * TOK)
            out_ref[half * 8 + t, 2 * DH : 3 * DH, pl.ds(lane0, TOK)] = (dk_s[:, cols] * SCALE).astype(BF)
            out_ref[half * 8 + t, 3 * DH : 4 * DH, pl.ds(lane0, TOK)] = dv_s[:, cols].astype(BF)


def attention(core, x, bias, rows=256):
    def whole(shape):
        return pl.BlockSpec(shape, lambda s, b, core: (0,) * len(shape))

    half_sum = (4, KEYS, 128)
    return pl.pallas_call(
        functools.partial(attention_kernel, rows=rows),
        grid_spec=pltpu.PrefetchScalarGridSpec(
            num_scalar_prefetch=1,
            grid=(4, KEYS // rows),
            in_specs=[whole(x.shape), whole(bias.shape)],
            out_specs=[whole(x.shape), whole(half_sum), whole(half_sum)],
            scratch_shapes=[
                pltpu.VMEM((KEYS, 128), BF),
                pltpu.VMEM((128, KEYS), BF),
                pltpu.VMEM((128, KEYS), BF),
                pltpu.VMEM((KEYS, 128), BF),
                pltpu.VMEM((KEYS, 128), BF),
                pltpu.VMEM((KEYS, 128), BF),
                pltpu.VMEM((DH, KEYS), BF),
                pltpu.VMEM((DH, KEYS), F32),
                pltpu.VMEM((DH, KEYS), F32),
                pltpu.VMEM((KEYS, KEYS), F32),
                pltpu.VMEM((KEYS, KEYS), F32),
            ],
        ),
        out_shape=[
            jax.ShapeDtypeStruct(x.shape, BF),
            jax.ShapeDtypeStruct(half_sum, BF),
            jax.ShapeDtypeStruct(half_sum, BF),
        ],
        compiler_params=params(),
        cost_estimate=pl.CostEstimate(
            flops=4 * 6 * 2 * KEYS * KEYS * 256, bytes_accessed=8 * 2**20, transcendentals=4 * KEYS * KEYS
        ),
        name="attention",
    )(core, x, bias)


def gate_kernel(core_ref, back_ref, gate_ref, gg_ref, gproj_ref, gated_ref, send_ref):
    other = 1 - core_ref[0]
    flat = gate_ref.shape[1]
    att = back_ref[:, :DH, :].astype(F32).reshape(C, flat)
    gate = gate_ref[...]
    opened = att * gate
    gated = opened.astype(BF)
    gated_ref[...] = gated
    for q in range(4):
        send_ref[8 + q] = gated[q * 192 : (q + 1) * 192]
    for kind in range(3):
        gproj_ref[kind * 4 : kind * 4 + 4] = back_ref[:, (kind + 1) * DH : (kind + 2) * DH, :].reshape(
            4, 4 * DH, flat
        )
    gproj_ref[12:16] = (gg_ref[...].astype(F32) * opened * (1.0 - gate)).astype(BF).reshape(4, 4 * DH, flat)
    for n in range(8):
        send_ref[n] = gproj_ref[2 * n + other]


def gate_step(core, back, gate, ggated):
    def whole(shape):
        return pl.BlockSpec(shape, lambda t, core: (0,) * len(shape))

    flat = gate.shape[1]
    shapes = [(16, 4 * DH, flat), (C, flat), (12, 4 * DH, flat)]
    return pl.pallas_call(
        gate_kernel,
        grid_spec=pltpu.PrefetchScalarGridSpec(
            num_scalar_prefetch=1,
            grid=(1,),
            in_specs=[whole(back.shape), whole(gate.shape), whole(ggated.shape)],
            out_specs=[whole(s) for s in shapes],
        ),
        out_shape=[jax.ShapeDtypeStruct(s, BF) for s in shapes],
        compiler_params=params(),
        cost_estimate=pl.CostEstimate(flops=6 * C * flat, bytes_accessed=6 * 2**20, transcendentals=0),
        name="gate",
    )(core, back, gate, ggated)


def input_grad_kernel(g_ref, w_ref, normed_ref, inv_ref, gain_ref, grad_ref, ggain_ref, total_s):
    step = pl.program_id(0)
    flat = normed_ref.shape[0]
    part = dot(w_ref[...], g_ref[...].reshape(C, flat))

    @pl.when(step == 0)
    def _():
        total_s[...] = part

    @pl.when(step > 0)
    def _():
        total_s[...] += part

    @pl.when(step == 3)
    def _():
        grad_scaled = total_s[...].T
        normed = normed_ref[...]
        ggain_ref[...] = jnp.sum(grad_scaled * normed, axis=0, keepdims=True)
        grad_normed = grad_scaled * gain_ref[...]
        grad_ref[...] = (
            inv_ref[...]
            * (
                grad_normed
                - jnp.mean(grad_normed, -1, keepdims=True)
                - normed * jnp.mean(grad_normed * normed, -1, keepdims=True)
            )
        ).astype(BF)


def input_grad(gproj, w_in, normed, inv_std, ln_gain):
    flat = normed.shape[0]

    def whole(shape):
        return pl.BlockSpec(shape, lambda t: (0,) * len(shape))

    return pl.pallas_call(
        input_grad_kernel,
        grid=(4,),
        in_specs=[
            pl.BlockSpec((4, 4 * DH, flat), lambda t: (t, 0, 0)),
            pl.BlockSpec((C, C), lambda t: (0, t)),
            whole((flat, C)),
            whole((flat, 1)),
            whole((1, C)),
        ],
        out_specs=[whole((flat, C)), whole((1, C))],
        out_shape=[jax.ShapeDtypeStruct((flat, C), BF), jax.ShapeDtypeStruct((1, C), F32)],
        scratch_shapes=[pltpu.VMEM((C, flat), F32)],
        compiler_params=params(),
        cost_estimate=pl.CostEstimate(
            flops=2 * flat * C * 4 * C, bytes_accessed=8 * 2**20, transcendentals=0
        ),
        name="input_grad",
    )(gproj, w_in, normed, inv_std, ln_gain)


def weight_kernel(
    core_ref, g_ref, o_ref, gated_ref, sc_ref, sco_ref, do_ref, doo_ref, gain_ref, out_ref, scaled_s, gated_s
):
    core = core_ref[0]
    n = pl.program_id(0)
    flat = sc_ref.shape[0]

    @pl.when(n == 0)
    def _():
        scaled_s[:flat] = sc_ref[...]
        scaled_s[flat:] = sco_ref[...]
        gated_s[:flat] = gated_ref[...].T
        gated_s[flat:] = o_ref[8:12].reshape(C, flat).T

    left = jnp.concatenate([g_ref[2 * n + core], o_ref[n]], axis=1)
    win = dot(left, scaled_s[...])
    wout = dot(jnp.concatenate([do_ref[n], doo_ref[n]], axis=1), gated_s[...])
    gain = gain_ref[...]
    gain_hi = gain.astype(BF).astype(F32)
    gain_lo = gain - gain_hi
    row = lax.broadcasted_iota(jnp.int32, (8, C), 0)
    for k in range(8):
        tail = jnp.where(row == 6, gain_hi, jnp.where(row == 7, gain_lo, wout[k * 8 : k * 8 + 8]))
        out_ref[k] = jnp.concatenate([win[k * 24 : k * 24 + 24], tail], axis=0).astype(BF)


def weight_grads(core, operands):
    def whole(shape):
        return pl.BlockSpec(shape, lambda t, core: (0,) * len(shape))

    flat = operands[3].shape[0]
    return pl.pallas_call(
        weight_kernel,
        grid_spec=pltpu.PrefetchScalarGridSpec(
            num_scalar_prefetch=1,
            grid=(8,),
            in_specs=[whole(o.shape) for o in operands],
            out_specs=pl.BlockSpec((8, 32, C), lambda t, core: (t, 0, 0)),
            scratch_shapes=[pltpu.VMEM((2 * flat, C), BF), pltpu.VMEM((2 * flat, C), BF)],
        ),
        out_shape=jax.ShapeDtypeStruct((64, 32, C), BF),
        compiler_params=params(),
        cost_estimate=pl.CostEstimate(
            flops=2 * 2 * flat * C * 2048, bytes_accessed=8 * 2**20, transcendentals=0
        ),
        name="weight_grads",
    )(core, *operands)


def per_device(act, pair_bias, ln_gain, w_in, w_out, d_out):
    sample_count, row_count, channels = act.shape
    flat = sample_count * row_count
    core = lax.axis_index("core")
    core_arg = jnp.full((1,), core, jnp.int32)
    place = lax.axis_index("x") * 2 + core
    zh = lax.axis_index("zh")

    bias = lax.dynamic_slice(pair_bias, (zh * 8, place * 16, 0), (8, 16, KEYS))
    bias = lax.all_to_all(bias, ("zl", "y"), 0, 0, tiled=True)
    bias = lax.all_gather(bias, ("x", "core"))

    rows_out = d_out.reshape(flat, channels)
    scaled, normed, inv_std, send, gate, ggated = front(
        act.reshape(flat, channels), ln_gain.reshape(1, C), w_in, w_out, rows_out
    )
    received = lax.all_to_all(send, PLANE, 0, 0, tiled=True)

    dout_t = jnp.pad(rows_out.T.reshape(128, 6, flat), ((0, 0), (0, 2), (0, 0)))
    dout_t = dout_t.reshape(8, 2, 64, flat)
    dout_mine = lax.dynamic_index_in_dim(dout_t, core, 1, keepdims=False)
    dout_send = lax.dynamic_index_in_dim(dout_t, 1 - core, 1, keepdims=False)
    dout_other = lax.ppermute(dout_send, "core", SWAP)
    scaled_other = lax.ppermute(scaled, "core", SWAP)

    result, keep, give = attention(core_arg, received, bias)
    back = lax.all_to_all(result, PLANE, 0, 0, tiled=True)

    got = lax.ppermute(give, "core", SWAP)
    gb = (keep.astype(F32) + got.astype(F32)).astype(BF)
    gb = lax.psum_scatter(gb, "x", scatter_dimension=0, tiled=False)
    gb = gb.reshape(8, TOK, 2, 64).transpose(2, 0, 1, 3).reshape(HEADS, TOK, 64)
    grad_bias = lax.all_to_all(gb, PLANE, 0, 0, tiled=True).astype(F32)

    gproj, gated, half = gate_step(core_arg, back, gate, ggated)
    other = lax.ppermute(half, "core", SWAP)
    grad_act, gain = input_grad(gproj, w_in, normed, inv_std, ln_gain.reshape(1, C))
    chunks = weight_grads(
        core_arg, (gproj, other, gated, scaled, scaled_other, dout_mine, dout_other, gain)
    )
    chunks, gated = lax.optimization_barrier((chunks, gated))
    output = jnp.einsum("cr,cd->rd", gated, w_out, preferred_element_type=F32).astype(BF)
    chunks = lax.all_to_all(chunks, ("x", "zh", "zl", "y"), 0, 0, tiled=True)
    total = jnp.sum(chunks.astype(F32), axis=0)
    gain = total[30] + total[31]
    return (
        output.reshape(sample_count, row_count, channels),
        grad_act.reshape(sample_count, row_count, channels),
        grad_bias,
        gain + lax.ppermute(gain, "core", SWAP),
        total[:24].T,
        total[24:30].T,
    )


def solution(mesh):
    fine = Mesh(mesh.devices.reshape(4, 2, 2, 2, 4), ("x", "zh", "core", "zl", "y"))
    sample = ("x", "zh", "core")
    tok = ("zl", "y")
    return jax.shard_map(
        per_device,
        mesh=fine,
        in_specs=(
            P(sample, tok, None),
            P(None, tok, None),
            P(),
            P(),
            P(),
            P(sample, tok, None),
        ),
        out_specs=(
            P(sample, tok, None),
            P(sample, tok, None),
            P(None, tok, sample),
            P(),
            P(None, sample + tok),
            P(None, sample + tok),
        ),
        check_vma=False,
    )
```

```python
import functools
import math

import jax
import jax.numpy as jnp
from jax import lax
from jax.experimental import pallas as pl
from jax.experimental.pallas import tpu as pltpu
from jax.sharding import Mesh
from jax.sharding import PartitionSpec as P

EPS = 1e-05
LOG2E = math.log2(math.e)
BF = jnp.bfloat16
F32 = jnp.float32
C = 768
HEADS = 16
DH = 48
TOK = 128
KEYS = 1024
PLANE = ("zh", "zl", "y")
SWAP = [(0, 1), (1, 0)]
SCALE = 1.0 / math.sqrt(DH)
VMEM_LIMIT = 60 * 1024 * 1024


def dot(a, b):
    return jnp.dot(a, b, preferred_element_type=F32)


def dot_nt(a, b):
    return lax.dot_general(a, b, (((1,), (1,)), ((), ())), preferred_element_type=F32)


def params():
    return pltpu.CompilerParams(vmem_limit_bytes=VMEM_LIMIT)


def front_kernel(
    act_ref, gain_ref, w_ref, wout_ref, dout_ref, scaled_ref, normed_ref, inv_ref, send_ref, gate_ref, gg_ref
):
    step = pl.program_id(0)
    flat = act_ref.shape[0]

    @pl.when(step == 0)
    def _():
        values = act_ref[...].astype(F32)
        center = jnp.mean(values, -1, keepdims=True)
        shifted = values - center
        spread = jnp.mean(shifted * shifted, -1, keepdims=True)
        inv_std = lax.rsqrt(spread + EPS)
        normed = shifted * inv_std
        normed_ref[...] = normed
        inv_ref[...] = inv_std
        scaled_ref[...] = (normed * gain_ref[...]).astype(BF)

    block = dot(scaled_ref[...], w_ref[...])

    for kind in range(3):

        @pl.when(step == kind)
        def _(kind=kind):
            send_ref[:, kind * DH : (kind + 1) * DH, :] = block.astype(BF).T.reshape(HEADS, DH, flat)

    @pl.when(step == 3)
    def _():
        gate = jax.nn.sigmoid(block.T)
        ggated = dot_nt(wout_ref[...], dout_ref[...]).astype(BF)
        gate_ref[...] = gate
        gg_ref[...] = ggated
        send_ref[:, 3 * DH : 4 * DH, :] = (ggated.astype(F32) * gate).astype(BF).reshape(HEADS, DH, flat)


def front(act, ln_gain, w_in, w_out, d_out):
    flat = act.shape[0]
    shapes = [
        ((flat, C), BF),
        ((flat, C), F32),
        ((flat, 1), F32),
        ((HEADS, 4 * DH, flat), BF),
        ((C, flat), F32),
        ((C, flat), BF),
    ]

    def whole(shape):
        return pl.BlockSpec(shape, lambda t: (0,) * len(shape))

    return pl.pallas_call(
        front_kernel,
        grid=(4,),
        in_specs=[
            whole((flat, C)),
            whole((1, C)),
            pl.BlockSpec((C, C), lambda t: (0, t)),
            whole((C, C)),
            whole((flat, C)),
        ],
        out_specs=[whole(s) for s, _ in shapes],
        out_shape=[jax.ShapeDtypeStruct(s, d) for s, d in shapes],
        compiler_params=params(),
        cost_estimate=pl.CostEstimate(
            flops=2 * flat * C * 5 * C, bytes_accessed=11 * 2**20, transcendentals=flat * C
        ),
        name="front",
    )(act, ln_gain, w_in, w_out, d_out)


def attention_kernel(
    core_ref, x_ref, bias_ref, out_ref, keep_ref, give_ref,
    qa_s, ka_s, va_s, vt_s, kn_s, gn_s, gb_s, bias_s, *, blocks,
):
    core = core_ref[0]
    sample = pl.program_id(0)
    half = sample // 2
    lane0 = pl.multiple_of((sample % 2) * TOK, TOK)

    @pl.when(sample == 0)
    def _():
        for t in range(8):
            tile = jnp.concatenate([bias_ref[p, t] for p in range(8)], axis=0)
            bias_s[t * TOK : (t + 1) * TOK] = tile.astype(F32) * LOG2E

    whole = jnp.concatenate([x_ref[half * 8 + t, :, pl.ds(lane0, TOK)] for t in range(8)], axis=1)
    qt, kt, vt, gt = (whole[i * DH : (i + 1) * DH] for i in range(4))
    qs = qt.astype(F32) * (SCALE * LOG2E)
    q_hi = qs.astype(BF)
    q_lo = (qs - q_hi.astype(F32)).astype(BF)
    zeros32 = jnp.zeros((32, KEYS), BF)
    zeros64 = jnp.zeros((64, KEYS), BF)
    zeros80 = jnp.zeros((80, KEYS), BF)
    ones16 = jnp.ones((16, KEYS), BF)
    qa_s[...] = jnp.concatenate([q_hi, q_lo, zeros32], axis=0).T
    ka_s[...] = jnp.concatenate([kt, kt, zeros32], axis=0)
    v_one = jnp.concatenate([vt, ones16, zeros64], axis=0)
    va_s[...] = v_one
    vt_s[...] = v_one.T
    kn_s[...] = jnp.concatenate([kt, zeros80], axis=0).T
    gn_s[...] = jnp.concatenate([gt, zeros80], axis=0).T

    rows = KEYS // blocks
    every = [slice(i * rows, (i + 1) * rows) for i in range(blocks)]
    lane = lax.broadcasted_iota(jnp.int32, (rows, 128), 1)
    scores = [dot(qa_s[p], ka_s[...]) + bias_s[p] for p in every]
    expd = [jnp.exp2(s - jnp.max(s, axis=1, keepdims=True)) for s in scores]
    expd_low = [e.astype(BF) for e in expd]
    summed = [dot(e, vt_s[...]) for e in expd_low]
    inv = [1.0 / s[:, DH : DH + 1] for s in summed]
    out = [s * i for s, i in zip(summed, inv)]
    gscaled = [(gn_s[p].astype(F32) * i).astype(BF).astype(F32) for p, i in zip(every, inv)]
    left = []
    for o, g in zip(out, gscaled):
        delta = jnp.sum(o * g, axis=1, keepdims=True)
        delta_hi = delta.astype(BF).astype(F32)
        left.append(
            jnp.where(lane == DH, -delta_hi, jnp.where(lane == DH + 1, delta_hi - delta, g)).astype(BF)
        )
    dscores = [e * dot(l, va_s[...]) for e, l in zip(expd, left)]
    dscores_low = [d.astype(BF) for d in dscores]

    @pl.when(sample == 0)
    def _():
        for p, d in zip(every, dscores):
            gb_s[p] = d

    @pl.when((sample > 0) & (sample < 3))
    def _():
        for p, d in zip(every, dscores):
            gb_s[p] = gb_s[p] + d

    @pl.when(sample == 3)
    def _():
        for p, d in zip(every, dscores):
            total = (gb_s[p] + d).astype(BF)
            for x in range(4):
                even = total[:, x * 256 : x * 256 + 128]
                odd = total[:, x * 256 + 128 : x * 256 + 256]
                low = jnp.concatenate([even[:, :64], odd[:, :64]], axis=1)
                high = jnp.concatenate([even[:, 64:], odd[:, 64:]], axis=1)
                keep_ref[x, p] = jnp.where(core == 0, low, high)
                give_ref[x, p] = jnp.where(core == 0, high, low)

    all_low = jnp.concatenate(dscores_low, axis=0)
    gscaled_t = jnp.concatenate(gscaled, axis=0).T.astype(BF)
    out_t = jnp.concatenate(out, axis=0).T[:DH].astype(BF)
    dquery_t = (dot(all_low, kn_s[...]) * SCALE).T[:DH].astype(BF)
    dkey_t = (dot(qt, all_low) * SCALE).astype(BF)
    dvalue_t = dot(gscaled_t[:DH], jnp.concatenate(expd_low, axis=0)).astype(BF)
    for t in range(8):
        cols = slice(t * TOK, (t + 1) * TOK)
        for i, part in enumerate((out_t, dquery_t, dkey_t, dvalue_t)):
            out_ref[half * 8 + t, i * DH : (i + 1) * DH, pl.ds(lane0, TOK)] = part[:, cols]


def attention(core, x, bias, blocks=4):
    def whole(shape):
        return pl.BlockSpec(shape, lambda s, core: (0,) * len(shape))

    half_sum = (4, KEYS, 128)
    return pl.pallas_call(
        functools.partial(attention_kernel, blocks=blocks),
        grid_spec=pltpu.PrefetchScalarGridSpec(
            num_scalar_prefetch=1,
            grid=(4,),
            in_specs=[whole(x.shape), whole(bias.shape)],
            out_specs=[whole(x.shape), whole(half_sum), whole(half_sum)],
            scratch_shapes=[
                pltpu.VMEM((KEYS, 128), BF),
                pltpu.VMEM((128, KEYS), BF),
                pltpu.VMEM((128, KEYS), BF),
                pltpu.VMEM((KEYS, 128), BF),
                pltpu.VMEM((KEYS, 128), BF),
                pltpu.VMEM((KEYS, 128), BF),
                pltpu.VMEM((KEYS, KEYS), F32),
                pltpu.VMEM((KEYS, KEYS), F32),
            ],
        ),
        out_shape=[
            jax.ShapeDtypeStruct(x.shape, BF),
            jax.ShapeDtypeStruct(half_sum, BF),
            jax.ShapeDtypeStruct(half_sum, BF),
        ],
        compiler_params=params(),
        cost_estimate=pl.CostEstimate(
            flops=4 * 6 * 2 * KEYS * KEYS * 256, bytes_accessed=8 * 2**20, transcendentals=4 * KEYS * KEYS
        ),
        name="attention",
    )(core, x, bias)


def gate_kernel(core_ref, back_ref, gate_ref, gg_ref, gproj_ref, gated_ref, send_ref):
    other = 1 - core_ref[0]
    flat = gate_ref.shape[1]
    att = back_ref[:, :DH, :].astype(F32).reshape(C, flat)
    gate = gate_ref[...]
    opened = att * gate
    gated = opened.astype(BF)
    gated_ref[...] = gated
    for q in range(4):
        send_ref[8 + q] = gated[q * 192 : (q + 1) * 192]
    for kind in range(3):
        gproj_ref[kind * 4 : kind * 4 + 4] = back_ref[:, (kind + 1) * DH : (kind + 2) * DH, :].reshape(
            4, 4 * DH, flat
        )
    gproj_ref[12:16] = (gg_ref[...].astype(F32) * opened * (1.0 - gate)).astype(BF).reshape(4, 4 * DH, flat)
    for n in range(8):
        send_ref[n] = gproj_ref[2 * n + other]


def gate_step(core, back, gate, ggated):
    def whole(shape):
        return pl.BlockSpec(shape, lambda t, core: (0,) * len(shape))

    flat = gate.shape[1]
    shapes = [(16, 4 * DH, flat), (C, flat), (12, 4 * DH, flat)]
    return pl.pallas_call(
        gate_kernel,
        grid_spec=pltpu.PrefetchScalarGridSpec(
            num_scalar_prefetch=1,
            grid=(1,),
            in_specs=[whole(back.shape), whole(gate.shape), whole(ggated.shape)],
            out_specs=[whole(s) for s in shapes],
        ),
        out_shape=[jax.ShapeDtypeStruct(s, BF) for s in shapes],
        compiler_params=params(),
        cost_estimate=pl.CostEstimate(flops=6 * C * flat, bytes_accessed=6 * 2**20, transcendentals=0),
        name="gate",
    )(core, back, gate, ggated)


def input_grad_kernel(g_ref, w_ref, normed_ref, inv_ref, gain_ref, grad_ref, ggain_ref, total_s):
    step = pl.program_id(0)
    flat = normed_ref.shape[0]
    part = dot(w_ref[...], g_ref[...].reshape(C, flat))

    @pl.when(step == 0)
    def _():
        total_s[...] = part

    @pl.when(step > 0)
    def _():
        total_s[...] += part

    @pl.when(step == 3)
    def _():
        grad_scaled = total_s[...].T
        normed = normed_ref[...]
        ggain_ref[...] = jnp.sum(grad_scaled * normed, axis=0, keepdims=True)
        grad_normed = grad_scaled * gain_ref[...]
        grad_ref[...] = (
            inv_ref[...]
            * (
                grad_normed
                - jnp.mean(grad_normed, -1, keepdims=True)
                - normed * jnp.mean(grad_normed * normed, -1, keepdims=True)
            )
        ).astype(BF)


def input_grad(gproj, w_in, normed, inv_std, ln_gain):
    flat = normed.shape[0]

    def whole(shape):
        return pl.BlockSpec(shape, lambda t: (0,) * len(shape))

    return pl.pallas_call(
        input_grad_kernel,
        grid=(4,),
        in_specs=[
            pl.BlockSpec((4, 4 * DH, flat), lambda t: (t, 0, 0)),
            pl.BlockSpec((C, C), lambda t: (0, t)),
            whole((flat, C)),
            whole((flat, 1)),
            whole((1, C)),
        ],
        out_specs=[whole((flat, C)), whole((1, C))],
        out_shape=[jax.ShapeDtypeStruct((flat, C), BF), jax.ShapeDtypeStruct((1, C), F32)],
        scratch_shapes=[pltpu.VMEM((C, flat), F32)],
        compiler_params=params(),
        cost_estimate=pl.CostEstimate(
            flops=2 * flat * C * 4 * C, bytes_accessed=8 * 2**20, transcendentals=0
        ),
        name="input_grad",
    )(gproj, w_in, normed, inv_std, ln_gain)


def weight_kernel(
    core_ref, g_ref, o_ref, gated_ref, sc_ref, sco_ref, do_ref, doo_ref, gain_ref, out_ref, scaled_s, gated_s
):
    core = core_ref[0]
    n = pl.program_id(0)
    flat = sc_ref.shape[0]

    @pl.when(n == 0)
    def _():
        scaled_s[:flat] = sc_ref[...]
        scaled_s[flat:] = sco_ref[...]
        gated_s[:flat] = gated_ref[...].T
        gated_s[flat:] = o_ref[8:12].reshape(C, flat).T

    left = jnp.concatenate([g_ref[2 * n + core], o_ref[n]], axis=1)
    win = dot(left, scaled_s[...])
    wout = dot(jnp.concatenate([do_ref[n], doo_ref[n]], axis=1), gated_s[...])
    gain = gain_ref[...]
    gain_hi = gain.astype(BF).astype(F32)
    gain_lo = gain - gain_hi
    row = lax.broadcasted_iota(jnp.int32, (8, C), 0)
    for k in range(8):
        tail = jnp.where(row == 6, gain_hi, jnp.where(row == 7, gain_lo, wout[k * 8 : k * 8 + 8]))
        out_ref[k] = jnp.concatenate([win[k * 24 : k * 24 + 24], tail], axis=0).astype(BF)


def weight_grads(core, operands):
    def whole(shape):
        return pl.BlockSpec(shape, lambda t, core: (0,) * len(shape))

    flat = operands[3].shape[0]
    return pl.pallas_call(
        weight_kernel,
        grid_spec=pltpu.PrefetchScalarGridSpec(
            num_scalar_prefetch=1,
            grid=(8,),
            in_specs=[whole(o.shape) for o in operands],
            out_specs=pl.BlockSpec((8, 32, C), lambda t, core: (t, 0, 0)),
            scratch_shapes=[pltpu.VMEM((2 * flat, C), BF), pltpu.VMEM((2 * flat, C), BF)],
        ),
        out_shape=jax.ShapeDtypeStruct((64, 32, C), BF),
        compiler_params=params(),
        cost_estimate=pl.CostEstimate(
            flops=2 * 2 * flat * C * 2048, bytes_accessed=8 * 2**20, transcendentals=0
        ),
        name="weight_grads",
    )(core, *operands)


def per_device(act, pair_bias, ln_gain, w_in, w_out, d_out):
    sample_count, row_count, channels = act.shape
    flat = sample_count * row_count
    core = lax.axis_index("core")
    core_arg = jnp.full((1,), core, jnp.int32)
    place = lax.axis_index("x") * 2 + core
    zh = lax.axis_index("zh")

    bias = lax.dynamic_slice(pair_bias, (zh * 8, place * 16, 0), (8, 16, KEYS))
    bias = lax.all_to_all(bias, ("zl", "y"), 0, 0, tiled=True)

    rows_out = d_out.reshape(flat, channels)
    scaled, normed, inv_std, send, gate, ggated = front(
        act.reshape(flat, channels), ln_gain.reshape(1, C), w_in, w_out, rows_out
    )
    bias, send = lax.optimization_barrier((bias, send))
    bias = lax.all_gather(bias, ("x", "core"))
    received = lax.all_to_all(send, PLANE, 0, 0, tiled=True)

    dout_t = jnp.pad(rows_out.T.reshape(128, 6, flat), ((0, 0), (0, 2), (0, 0)))
    dout_t = dout_t.reshape(8, 2, 64, flat)
    dout_mine = lax.dynamic_index_in_dim(dout_t, core, 1, keepdims=False)
    dout_send = lax.dynamic_index_in_dim(dout_t, 1 - core, 1, keepdims=False)
    dout_other = lax.ppermute(dout_send, "core", SWAP)
    scaled_other = lax.ppermute(scaled, "core", SWAP)

    received, dout_mine, dout_other, scaled_other = lax.optimization_barrier(
        (received, dout_mine, dout_other, scaled_other)
    )
    result, keep, give = attention(core_arg, received, bias)
    back = lax.all_to_all(result, PLANE, 0, 0, tiled=True)

    got = lax.ppermute(give, "core", SWAP)
    gb = (keep.astype(F32) + got.astype(F32)).astype(BF)
    gb = lax.psum_scatter(gb, "x", scatter_dimension=0, tiled=False)
    gb = gb.reshape(8, TOK, 2, 64).transpose(2, 0, 1, 3).reshape(HEADS, TOK, 64)
    grad_bias = lax.all_to_all(gb, PLANE, 0, 0, tiled=True).astype(F32)

    gproj, gated, half = gate_step(core_arg, back, gate, ggated)
    other = lax.ppermute(half, "core", SWAP)
    grad_act, gain = input_grad(gproj, w_in, normed, inv_std, ln_gain.reshape(1, C))
    chunks = weight_grads(
        core_arg, (gproj, other, gated, scaled, scaled_other, dout_mine, dout_other, gain)
    )
    chunks, gated = lax.optimization_barrier((chunks, gated))
    output = jnp.einsum("cr,cd->rd", gated, w_out, preferred_element_type=F32).astype(BF)
    chunks = lax.all_to_all(chunks, ("x", "zh", "zl", "y"), 0, 0, tiled=True)
    total = jnp.sum(chunks.astype(F32), axis=0)
    gain = total[30] + total[31]
    return (
        output.reshape(sample_count, row_count, channels),
        grad_act.reshape(sample_count, row_count, channels),
        grad_bias,
        gain + lax.ppermute(gain, "core", SWAP),
        total[:24].T,
        total[24:30].T,
    )


def solution(mesh):
    fine = Mesh(mesh.devices.reshape(4, 2, 2, 2, 4), ("x", "zh", "core", "zl", "y"))
    sample = ("x", "zh", "core")
    tok = ("zl", "y")
    return jax.shard_map(
        per_device,
        mesh=fine,
        in_specs=(
            P(sample, tok, None),
            P(None, tok, None),
            P(),
            P(),
            P(),
            P(sample, tok, None),
        ),
        out_specs=(
            P(sample, tok, None),
            P(sample, tok, None),
            P(None, tok, sample),
            P(),
            P(None, sample + tok),
            P(None, sample + tok),
        ),
        check_vma=False,
    )
```

```python
import functools
import math

import jax
import jax.numpy as jnp
from jax import lax
from jax.experimental import pallas as pl
from jax.experimental.pallas import tpu as pltpu
from jax.sharding import Mesh
from jax.sharding import PartitionSpec as P

EPS = 1e-05
LOG2E = math.log2(math.e)
BF = jnp.bfloat16
F32 = jnp.float32
C = 768
HEADS = 16
DH = 48
TOK = 128
KEYS = 1024
PLANE = ("zh", "zl", "y")
SWAP = [(0, 1), (1, 0)]
SCALE = 1.0 / math.sqrt(DH)
VMEM_LIMIT = 60 * 1024 * 1024


def dot(a, b):
    return jnp.dot(a, b, preferred_element_type=F32)


def dot_nt(a, b):
    return lax.dot_general(a, b, (((1,), (1,)), ((), ())), preferred_element_type=F32)


def params():
    return pltpu.CompilerParams(vmem_limit_bytes=VMEM_LIMIT)


def front_kernel(
    act_ref, gain_ref, w_ref, wout_ref, dout_ref, scaled_ref, normed_ref, inv_ref, send_ref, gate_ref, gg_ref
):
    step = pl.program_id(0)
    flat = act_ref.shape[0]

    @pl.when(step == 0)
    def _():
        values = act_ref[...].astype(F32)
        center = jnp.mean(values, -1, keepdims=True)
        shifted = values - center
        spread = jnp.mean(shifted * shifted, -1, keepdims=True)
        inv_std = lax.rsqrt(spread + EPS)
        normed = shifted * inv_std
        normed_ref[...] = normed
        inv_ref[...] = inv_std
        scaled_ref[...] = (normed * gain_ref[...].reshape(1, C)).astype(BF)

    block = dot(scaled_ref[...], w_ref[...])

    for kind in range(3):

        @pl.when(step == kind)
        def _(kind=kind):
            send_ref[:, kind * DH : (kind + 1) * DH, :] = block.astype(BF).T.reshape(HEADS, DH, flat)

    @pl.when(step == 3)
    def _():
        gate = jax.nn.sigmoid(block.T)
        ggated = dot_nt(wout_ref[...], dout_ref[...]).astype(BF)
        gate_ref[...] = gate
        gg_ref[...] = ggated
        send_ref[:, 3 * DH : 4 * DH, :] = (ggated.astype(F32) * gate).astype(BF).reshape(HEADS, DH, flat)


def front(act, ln_gain, w_in, w_out, d_out):
    flat = act.shape[0]
    shapes = [
        ((flat, C), BF),
        ((flat, C), F32),
        ((flat, 1), F32),
        ((HEADS, 4 * DH, flat), BF),
        ((C, flat), F32),
        ((C, flat), BF),
    ]

    def whole(shape):
        return pl.BlockSpec(shape, lambda t: (0,) * len(shape))

    return pl.pallas_call(
        front_kernel,
        grid=(4,),
        in_specs=[
            whole((flat, C)),
            whole((C,)),
            pl.BlockSpec((C, C), lambda t: (0, t)),
            whole((C, C)),
            whole((flat, C)),
        ],
        out_specs=[whole(s) for s, _ in shapes],
        out_shape=[jax.ShapeDtypeStruct(s, d) for s, d in shapes],
        compiler_params=params(),
        cost_estimate=pl.CostEstimate(
            flops=2 * flat * C * 5 * C, bytes_accessed=11 * 2**20, transcendentals=flat * C
        ),
        name="front",
    )(act, ln_gain, w_in, w_out, d_out)


def attention_kernel(
    core_ref, x_ref, bias_ref, out_ref, keep_ref, give_ref,
    qa_s, ka_s, va_s, vt_s, kn_s, gn_s, gb_s, bias_s, *, blocks,
):
    core = core_ref[0]
    sample = pl.program_id(0)
    half = sample // 2
    lane0 = pl.multiple_of((sample % 2) * TOK, TOK)

    @pl.when(sample == 0)
    def _():
        for t in range(8):
            tile = jnp.concatenate([bias_ref[p, t] for p in range(8)], axis=0)
            bias_s[t * TOK : (t + 1) * TOK] = tile.astype(F32) * LOG2E

    whole = jnp.concatenate([x_ref[half * 8 + t, :, pl.ds(lane0, TOK)] for t in range(8)], axis=1)
    qt, kt, vt, gt = (whole[i * DH : (i + 1) * DH] for i in range(4))
    qs = qt.astype(F32) * (SCALE * LOG2E)
    q_hi = qs.astype(BF)
    q_lo = (qs - q_hi.astype(F32)).astype(BF)
    zeros32 = jnp.zeros((32, KEYS), BF)
    zeros64 = jnp.zeros((64, KEYS), BF)
    zeros80 = jnp.zeros((80, KEYS), BF)
    ones16 = jnp.ones((16, KEYS), BF)
    qa_s[...] = jnp.concatenate([q_hi, q_lo, zeros32], axis=0).T
    ka_s[...] = jnp.concatenate([kt, kt, zeros32], axis=0)
    v_one = jnp.concatenate([vt, ones16, zeros64], axis=0)
    va_s[...] = v_one
    vt_s[...] = v_one.T
    kn_s[...] = jnp.concatenate([kt, zeros80], axis=0).T
    gn_s[...] = jnp.concatenate([gt, zeros80], axis=0).T

    rows = KEYS // blocks
    every = [slice(i * rows, (i + 1) * rows) for i in range(blocks)]
    lane = lax.broadcasted_iota(jnp.int32, (rows, 128), 1)
    scores = [dot(qa_s[p], ka_s[...]) + bias_s[p] for p in every]
    expd = [jnp.exp2(s - jnp.max(s, axis=1, keepdims=True)) for s in scores]
    expd_low = [e.astype(BF) for e in expd]
    summed = [dot(e, vt_s[...]) for e in expd_low]
    inv = [1.0 / s[:, DH : DH + 1] for s in summed]
    out = [s * i for s, i in zip(summed, inv)]
    gscaled = [(gn_s[p].astype(F32) * i).astype(BF).astype(F32) for p, i in zip(every, inv)]
    left = []
    for o, g in zip(out, gscaled):
        delta = jnp.sum(o * g, axis=1, keepdims=True)
        delta_hi = delta.astype(BF).astype(F32)
        left.append(
            jnp.where(lane == DH, -delta_hi, jnp.where(lane == DH + 1, delta_hi - delta, g)).astype(BF)
        )
    dscores = [e * dot(l, va_s[...]) for e, l in zip(expd, left)]
    dscores_low = [d.astype(BF) for d in dscores]

    @pl.when(sample == 0)
    def _():
        for p, d in zip(every, dscores):
            gb_s[p] = d

    @pl.when((sample > 0) & (sample < 3))
    def _():
        for p, d in zip(every, dscores):
            gb_s[p] = gb_s[p] + d

    @pl.when(sample == 3)
    def _():
        for p, d in zip(every, dscores):
            total = (gb_s[p] + d).astype(BF)
            for t in range(rows // TOK):
                for n in range(8):
                    tile = total[t * TOK : (t + 1) * TOK, n * TOK : (n + 1) * TOK]
                    low = jnp.concatenate([tile[:64, :64], tile[64:, :64]], axis=1)
                    high = jnp.concatenate([tile[:64, 64:], tile[64:, 64:]], axis=1)
                    where = (n % 2) * 8 + p.start // TOK + t
                    keep_ref[n // 2, where] = jnp.where(core == 0, low, high)
                    give_ref[n // 2, where] = jnp.where(core == 0, high, low)

    all_low = jnp.concatenate(dscores_low, axis=0)
    gscaled_t = jnp.concatenate(gscaled, axis=0).T.astype(BF)
    out_t = jnp.concatenate(out, axis=0).T[:DH].astype(BF)
    dquery_t = (dot(all_low, kn_s[...]) * SCALE).T[:DH].astype(BF)
    dkey_t = (dot(qt, all_low) * SCALE).astype(BF)
    dvalue_t = dot(gscaled_t[:DH], jnp.concatenate(expd_low, axis=0)).astype(BF)
    for t in range(8):
        cols = slice(t * TOK, (t + 1) * TOK)
        for i, part in enumerate((out_t, dquery_t, dkey_t, dvalue_t)):
            out_ref[half * 8 + t, i * DH : (i + 1) * DH, pl.ds(lane0, TOK)] = part[:, cols]


def attention(core, x, bias, blocks=4):
    def whole(shape):
        return pl.BlockSpec(shape, lambda s, core: (0,) * len(shape))

    half_sum = (4, HEADS, 64, 128)
    return pl.pallas_call(
        functools.partial(attention_kernel, blocks=blocks),
        grid_spec=pltpu.PrefetchScalarGridSpec(
            num_scalar_prefetch=1,
            grid=(4,),
            in_specs=[whole(x.shape), whole(bias.shape)],
            out_specs=[whole(x.shape), whole(half_sum), whole(half_sum)],
            scratch_shapes=[
                pltpu.VMEM((KEYS, 128), BF),
                pltpu.VMEM((128, KEYS), BF),
                pltpu.VMEM((128, KEYS), BF),
                pltpu.VMEM((KEYS, 128), BF),
                pltpu.VMEM((KEYS, 128), BF),
                pltpu.VMEM((KEYS, 128), BF),
                pltpu.VMEM((KEYS, KEYS), F32),
                pltpu.VMEM((KEYS, KEYS), F32),
            ],
        ),
        out_shape=[
            jax.ShapeDtypeStruct(x.shape, BF),
            jax.ShapeDtypeStruct(half_sum, BF),
            jax.ShapeDtypeStruct(half_sum, BF),
        ],
        compiler_params=params(),
        cost_estimate=pl.CostEstimate(
            flops=4 * 6 * 2 * KEYS * KEYS * 256, bytes_accessed=8 * 2**20, transcendentals=4 * KEYS * KEYS
        ),
        name="attention",
    )(core, x, bias)


def gate_kernel(core_ref, back_ref, gate_ref, gg_ref, ggate_ref, gated_ref, send_ref):
    other = 1 - core_ref[0]
    flat = gate_ref.shape[1]
    att = back_ref[:, :DH, :].astype(F32).reshape(C, flat)
    gate = gate_ref[...]
    opened = att * gate
    gated = opened.astype(BF)
    gated_ref[...] = gated
    for q in range(4):
        send_ref[8 + q] = gated[q * 192 : (q + 1) * 192]
    ggate_ref[...] = (gg_ref[...].astype(F32) * opened * (1.0 - gate)).astype(BF).reshape(4, 4 * DH, flat)
    for n in range(8):
        send_ref[n] = head_rows(back_ref, ggate_ref, n, other)


def head_rows(back_ref, ggate_ref, n, core):
    kind = n // 2
    group = (n % 2) * 2 + core
    if kind == 3:
        return ggate_ref[group]
    flat = back_ref.shape[2]
    return back_ref[pl.ds(group * 4, 4), (kind + 1) * DH : (kind + 2) * DH, :].reshape(4 * DH, flat)


def gate_step(core, back, gate, ggated):
    def whole(shape):
        return pl.BlockSpec(shape, lambda t, core: (0,) * len(shape))

    flat = gate.shape[1]
    shapes = [(4, 4 * DH, flat), (C, flat), (12, 4 * DH, flat)]
    return pl.pallas_call(
        gate_kernel,
        grid_spec=pltpu.PrefetchScalarGridSpec(
            num_scalar_prefetch=1,
            grid=(1,),
            in_specs=[whole(back.shape), whole(gate.shape), whole(ggated.shape)],
            out_specs=[whole(s) for s in shapes],
        ),
        out_shape=[jax.ShapeDtypeStruct(s, BF) for s in shapes],
        compiler_params=params(),
        cost_estimate=pl.CostEstimate(flops=6 * C * flat, bytes_accessed=6 * 2**20, transcendentals=0),
        name="gate",
    )(core, back, gate, ggated)


def input_grad_kernel(back_ref, ggate_ref, w_ref, normed_ref, inv_ref, gain_ref, grad_ref, total_s):
    step = pl.program_id(0)
    flat = normed_ref.shape[0]

    for kind in range(4):

        @pl.when(step == kind)
        def _(kind=kind):
            if kind == 3:
                total_s[...] += dot(w_ref[...], ggate_ref[...].reshape(C, flat))
            else:
                rows = back_ref[:, (kind + 1) * DH : (kind + 2) * DH, :].reshape(C, flat)
                part = dot(w_ref[...], rows)
                if kind == 0:
                    total_s[...] = part
                else:
                    total_s[...] += part

    @pl.when(step == 3)
    def _():
        normed = normed_ref[...]
        grad_normed = total_s[...].T * gain_ref[...].reshape(1, C)
        grad_ref[...] = (
            inv_ref[...]
            * (
                grad_normed
                - jnp.mean(grad_normed, -1, keepdims=True)
                - normed * jnp.mean(grad_normed * normed, -1, keepdims=True)
            )
        ).astype(BF)


def input_grad(back, ggate, w_in, normed, inv_std, ln_gain):
    flat = normed.shape[0]

    def whole(shape):
        return pl.BlockSpec(shape, lambda t: (0,) * len(shape))

    return pl.pallas_call(
        input_grad_kernel,
        grid=(4,),
        in_specs=[
            whole(back.shape),
            whole(ggate.shape),
            pl.BlockSpec((C, C), lambda t: (0, t)),
            whole((flat, C)),
            whole((flat, 1)),
            whole((C,)),
        ],
        out_specs=whole((flat, C)),
        out_shape=jax.ShapeDtypeStruct((flat, C), BF),
        scratch_shapes=[pltpu.VMEM((C, flat), F32)],
        compiler_params=params(),
        cost_estimate=pl.CostEstimate(
            flops=2 * flat * C * 4 * C, bytes_accessed=8 * 2**20, transcendentals=0
        ),
        name="input_grad",
    )(back, ggate, w_in, normed, inv_std, ln_gain)


def weight_kernel(
    core_ref, back_ref, ggate_ref, o_ref, gated_ref, sc_ref, sco_ref, do_ref, doo_ref, wt_ref, gain_ref,
    out_ref, scaled_s, gated_s, sum_s,
):
    core = core_ref[0]
    step = pl.program_id(0)
    flat = sc_ref.shape[0]
    last = pl.num_programs(0) - 1

    @pl.when(step == 0)
    def _():
        scaled_s[:flat] = sc_ref[...]
        scaled_s[flat:] = sco_ref[...]
        gated_s[:flat] = gated_ref[...].T
        gated_s[flat:] = o_ref[8:12].reshape(C, flat).T
        sum_s[...] = jnp.zeros_like(sum_s)

    for kind in range(4):

        @pl.when(step == kind)
        def _(kind=kind):
            blocks = [
                jnp.concatenate([head_rows(back_ref, ggate_ref, n, core), o_ref[n]], axis=1)
                for n in (2 * kind, 2 * kind + 1)
            ]
            win = dot(jnp.concatenate(blocks, axis=0), scaled_s[...])
            tails = jnp.concatenate(
                [
                    jnp.concatenate([do_ref[n], doo_ref[n]], axis=1)
                    for n in (2 * kind, 2 * kind + 1)
                ],
                axis=0,
            )
            wout = dot(tails, gated_s[...])
            weights = wt_ref[2 * kind : 2 * kind + 2].reshape(8 * DH, C).astype(F32)
            sum_s[...] += jnp.sum((win * weights).reshape(DH, 8, C), axis=0)
            for k in range(16):
                out_ref[kind * 16 + k] = jnp.concatenate(
                    [win[k * 24 : k * 24 + 24], wout[k * 8 : k * 8 + 8]], axis=0
                ).astype(BF)

    @pl.when(step == last)
    def _():
        gain = jnp.sum(sum_s[...], axis=0, keepdims=True) / gain_ref[...].reshape(1, C)
        gain_hi = gain.astype(BF).astype(F32)
        row = lax.broadcasted_iota(jnp.int32, (16, C), 0)
        extra = jnp.where(row == 14, gain_hi, gain - gain_hi).astype(BF)
        for k in range(64):
            out_ref[k, 16:] = jnp.where(row >= 14, extra, out_ref[k, 16:])


def weight_grads(core, operands):
    def whole(shape):
        return pl.BlockSpec(shape, lambda t, core: (0,) * len(shape))

    flat = operands[4].shape[0]
    return pl.pallas_call(
        weight_kernel,
        grid_spec=pltpu.PrefetchScalarGridSpec(
            num_scalar_prefetch=1,
            grid=(4,),
            in_specs=[whole(o.shape) for o in operands],
            out_specs=whole((64, 32, C)),
            scratch_shapes=[
                pltpu.VMEM((2 * flat, C), BF),
                pltpu.VMEM((2 * flat, C), BF),
                pltpu.VMEM((8, C), F32),
            ],
        ),
        out_shape=jax.ShapeDtypeStruct((64, 32, C), BF),
        compiler_params=params(),
        cost_estimate=pl.CostEstimate(
            flops=2 * 2 * flat * C * 2048, bytes_accessed=8 * 2**20, transcendentals=0
        ),
        name="weight_grads",
    )(core, *operands)


def per_device(act, pair_bias, ln_gain, w_in, w_out, d_out):
    sample_count, row_count, channels = act.shape
    flat = sample_count * row_count
    core = lax.axis_index("core")
    core_arg = jnp.full((1,), core, jnp.int32)
    place = lax.axis_index("x") * 2 + core
    zh = lax.axis_index("zh")

    bias = lax.dynamic_slice(pair_bias, (zh * 8, place * 16, 0), (8, 16, KEYS))
    bias = lax.all_to_all(bias, ("zl", "y"), 0, 0, tiled=True)

    rows_out = d_out.reshape(flat, channels)
    scaled, normed, inv_std, send, gate, ggated = front(
        act.reshape(flat, channels), ln_gain, w_in, w_out, rows_out
    )
    bias, send = lax.optimization_barrier((bias, send))
    bias = lax.all_gather(bias, ("x", "core"))
    received = lax.all_to_all(send, PLANE, 0, 0, tiled=True)

    dout_t = jnp.pad(rows_out.T.reshape(128, 6, flat), ((0, 0), (0, 2), (0, 0)))
    dout_t = dout_t.reshape(8, 2, 64, flat)
    dout_mine = lax.dynamic_index_in_dim(dout_t, core, 1, keepdims=False)
    dout_send = lax.dynamic_index_in_dim(dout_t, 1 - core, 1, keepdims=False)
    dout_other = lax.ppermute(dout_send, "core", SWAP)
    scaled_other = lax.ppermute(scaled, "core", SWAP)

    w_rows = lax.dynamic_index_in_dim(w_in.T.reshape(8, 2, 4 * DH, C), core, 1, keepdims=False)
    received, dout_mine, dout_other, scaled_other, w_rows = lax.optimization_barrier(
        (received, dout_mine, dout_other, scaled_other, w_rows)
    )
    result, keep, give = attention(core_arg, received, bias)
    back = lax.all_to_all(result, PLANE, 0, 0, tiled=True)

    got = lax.ppermute(give, "core", SWAP)
    gb = (keep.astype(F32) + got.astype(F32)).astype(BF)
    gb = lax.psum_scatter(gb, "x", scatter_dimension=0, tiled=False)
    gb = lax.all_to_all(gb, PLANE, 0, 0, tiled=True)

    ggate, gated, half = gate_step(core_arg, back, gate, ggated)
    other = lax.ppermute(half, "core", SWAP)
    chunks = weight_grads(
        core_arg,
        (back, ggate, other, gated, scaled, scaled_other, dout_mine, dout_other, w_rows, ln_gain),
    )
    chunks, gated, ggate, gb = lax.optimization_barrier((chunks, gated, ggate, gb))
    grad_act = input_grad(back, ggate, w_in, normed, inv_std, ln_gain)
    gb = gb.astype(F32)
    grad_bias = jnp.concatenate([gb[:, :, :64], gb[:, :, 64:]], axis=1)
    output = jnp.einsum("cr,cd->rd", gated, w_out, preferred_element_type=F32).astype(BF)
    chunks = lax.all_to_all(chunks, ("x", "zh", "zl", "y"), 0, 0, tiled=True)
    total = jnp.sum(chunks.astype(F32), axis=0)
    gain = total[30] + total[31]
    return (
        output.reshape(sample_count, row_count, channels),
        grad_act.reshape(sample_count, row_count, channels),
        grad_bias,
        gain + lax.ppermute(gain, "core", SWAP),
        total[:24].T,
        total[24:30].T,
    )


def solution(mesh):
    fine = Mesh(mesh.devices.reshape(4, 2, 2, 2, 4), ("x", "zh", "core", "zl", "y"))
    sample = ("x", "zh", "core")
    tok = ("zl", "y")
    return jax.shard_map(
        per_device,
        mesh=fine,
        in_specs=(
            P(sample, tok, None),
            P(None, tok, None),
            P(),
            P(),
            P(),
            P(sample, tok, None),
        ),
        out_specs=(
            P(sample, tok, None),
            P(sample, tok, None),
            P(None, tok, sample),
            P(),
            P(None, sample + tok),
            P(None, sample + tok),
        ),
        check_vma=False,
    )
```

```python
import functools
import math

import jax
import jax.numpy as jnp
from jax import lax
from jax.experimental import pallas as pl
from jax.experimental.pallas import tpu as pltpu
from jax.sharding import Mesh
from jax.sharding import PartitionSpec as P

EPS = 1e-05
LOG2E = math.log2(math.e)
BF = jnp.bfloat16
F32 = jnp.float32
C = 768
HEADS = 16
DH = 48
TOK = 128
KEYS = 1024
PLANE = ("zh", "zl", "y")
SWAP = [(0, 1), (1, 0)]
SCALE = 1.0 / math.sqrt(DH)
VMEM_LIMIT = 60 * 1024 * 1024


def dot(a, b):
    return jnp.dot(a, b, preferred_element_type=F32)


def dot_nt(a, b):
    return lax.dot_general(a, b, (((1,), (1,)), ((), ())), preferred_element_type=F32)


def turn(shift):
    return [(i, (i + shift) % 4) for i in range(4)]


def params():
    return pltpu.CompilerParams(vmem_limit_bytes=VMEM_LIMIT)


def front_kernel(
    act_ref, gain_ref, w_ref, wout_ref, dout_ref, scaled_ref, normed_ref, inv_ref, send_ref, gate_ref, gg_ref
):
    step = pl.program_id(0)
    flat = act_ref.shape[0]

    @pl.when(step == 0)
    def _():
        values = act_ref[...].astype(F32)
        center = jnp.mean(values, -1, keepdims=True)
        shifted = values - center
        spread = jnp.mean(shifted * shifted, -1, keepdims=True)
        inv_std = lax.rsqrt(spread + EPS)
        normed = shifted * inv_std
        normed_ref[...] = normed
        inv_ref[...] = inv_std
        scaled_ref[...] = (normed * gain_ref[...].reshape(1, C)).astype(BF)

    block = dot(scaled_ref[...], w_ref[...])

    for kind in range(3):

        @pl.when(step == kind)
        def _(kind=kind):
            send_ref[:, kind * DH : (kind + 1) * DH, :] = block.astype(BF).T.reshape(HEADS, DH, flat)

    @pl.when(step == 3)
    def _():
        gate = jax.nn.sigmoid(block.T)
        ggated = dot_nt(wout_ref[...], dout_ref[...]).astype(BF)
        gate_ref[...] = gate
        gg_ref[...] = ggated
        send_ref[:, 3 * DH : 4 * DH, :] = (ggated.astype(F32) * gate).astype(BF).reshape(HEADS, DH, flat)


def front(act, ln_gain, w_in, w_out, d_out):
    flat = act.shape[0]
    shapes = [
        ((flat, C), BF),
        ((flat, C), F32),
        ((flat, 1), F32),
        ((HEADS, 4 * DH, flat), BF),
        ((C, flat), F32),
        ((C, flat), BF),
    ]

    def whole(shape):
        return pl.BlockSpec(shape, lambda t: (0,) * len(shape))

    return pl.pallas_call(
        front_kernel,
        grid=(4,),
        in_specs=[
            whole((flat, C)),
            whole((C,)),
            pl.BlockSpec((C, C), lambda t: (0, t)),
            whole((C, C)),
            whole((flat, C)),
        ],
        out_specs=[whole(s) for s, _ in shapes],
        out_shape=[jax.ShapeDtypeStruct(s, d) for s, d in shapes],
        compiler_params=params(),
        cost_estimate=pl.CostEstimate(
            flops=2 * flat * C * 5 * C, bytes_accessed=11 * 2**20, transcendentals=flat * C
        ),
        name="front",
    )(act, ln_gain, w_in, w_out, d_out)


def attention_kernel(
    place_ref, x_ref, mine_ref, other_ref, out_ref, keep_ref, give_ref,
    qa_s, ka_s, va_s, vt_s, kn_s, gn_s, gb_s, bias_s, *, blocks,
):
    core = place_ref[0]
    own_x = place_ref[1]
    sample = pl.program_id(0)
    half = sample // 2
    lane0 = pl.multiple_of((sample % 2) * TOK, TOK)

    @pl.when(sample == 0)
    def _():
        for t in range(8):
            pieces = []
            for x in range(4):
                mine = mine_ref[(own_x - x + 4) % 4, t]
                other = other_ref[(own_x - x + 4) % 4, t]
                pieces += [jnp.where(core == 0, mine, other), jnp.where(core == 0, other, mine)]
            bias_s[t * TOK : (t + 1) * TOK] = jnp.concatenate(pieces, axis=0).astype(F32) * LOG2E

    whole = jnp.concatenate([x_ref[half * 8 + t, :, pl.ds(lane0, TOK)] for t in range(8)], axis=1)
    qt, kt, vt, gt = (whole[i * DH : (i + 1) * DH] for i in range(4))
    qs = qt.astype(F32) * (SCALE * LOG2E)
    q_hi = qs.astype(BF)
    q_lo = (qs - q_hi.astype(F32)).astype(BF)
    zeros32 = jnp.zeros((32, KEYS), BF)
    zeros64 = jnp.zeros((64, KEYS), BF)
    zeros80 = jnp.zeros((80, KEYS), BF)
    ones16 = jnp.ones((16, KEYS), BF)
    qa_s[...] = jnp.concatenate([q_hi, q_lo, zeros32], axis=0).T
    ka_s[...] = jnp.concatenate([kt, kt, zeros32], axis=0)
    v_one = jnp.concatenate([vt, ones16, zeros64], axis=0)
    va_s[...] = v_one
    vt_s[...] = v_one.T
    kn_s[...] = jnp.concatenate([kt, zeros80], axis=0).T
    gn_s[...] = jnp.concatenate([gt, zeros80], axis=0).T

    rows = KEYS // blocks
    every = [slice(i * rows, (i + 1) * rows) for i in range(blocks)]
    lane = lax.broadcasted_iota(jnp.int32, (rows, 128), 1)
    scores = [dot(qa_s[p], ka_s[...]) + bias_s[p] for p in every]
    expd = [jnp.exp2(s - jnp.max(s, axis=1, keepdims=True)) for s in scores]
    expd_low = [e.astype(BF) for e in expd]
    summed = [dot(e, vt_s[...]) for e in expd_low]
    inv = [1.0 / s[:, DH : DH + 1] for s in summed]
    out = [s * i for s, i in zip(summed, inv)]
    gscaled = [(gn_s[p].astype(F32) * i).astype(BF).astype(F32) for p, i in zip(every, inv)]
    left = []
    for o, g in zip(out, gscaled):
        delta = jnp.sum(o * g, axis=1, keepdims=True)
        delta_hi = delta.astype(BF).astype(F32)
        left.append(
            jnp.where(lane == DH, -delta_hi, jnp.where(lane == DH + 1, delta_hi - delta, g)).astype(BF)
        )
    dscores = [e * dot(l, va_s[...]) for e, l in zip(expd, left)]
    dscores_low = [d.astype(BF) for d in dscores]

    @pl.when(sample == 0)
    def _():
        for p, d in zip(every, dscores):
            gb_s[p] = d

    @pl.when((sample > 0) & (sample < 3))
    def _():
        for p, d in zip(every, dscores):
            gb_s[p] = gb_s[p] + d

    @pl.when(sample == 3)
    def _():
        for p, d in zip(every, dscores):
            total = (gb_s[p] + d).astype(BF)
            for t in range(rows // TOK):
                for n in range(8):
                    tile = total[t * TOK : (t + 1) * TOK, n * TOK : (n + 1) * TOK]
                    low = jnp.concatenate([tile[:64, :64], tile[64:, :64]], axis=1)
                    high = jnp.concatenate([tile[:64, 64:], tile[64:, 64:]], axis=1)
                    where = (n % 2) * 8 + p.start // TOK + t
                    ahead = (n // 2 - own_x + 4) % 4
                    keep_ref[ahead, where] = jnp.where(core == 0, low, high)
                    give_ref[ahead, where] = jnp.where(core == 0, high, low)

    all_low = jnp.concatenate(dscores_low, axis=0)
    gscaled_t = jnp.concatenate(gscaled, axis=0).T.astype(BF)
    out_t = jnp.concatenate(out, axis=0).T[:DH].astype(BF)
    dquery_t = (dot(all_low, kn_s[...]) * SCALE).T[:DH].astype(BF)
    dkey_t = (dot(qt, all_low) * SCALE).astype(BF)
    dvalue_t = dot(gscaled_t[:DH], jnp.concatenate(expd_low, axis=0)).astype(BF)
    for t in range(8):
        cols = slice(t * TOK, (t + 1) * TOK)
        for i, part in enumerate((out_t, dquery_t, dkey_t, dvalue_t)):
            out_ref[half * 8 + t, i * DH : (i + 1) * DH, pl.ds(lane0, TOK)] = part[:, cols]


def attention(place, x, mine, other, blocks=4):
    def whole(shape):
        return pl.BlockSpec(shape, lambda s, place: (0,) * len(shape))

    half_sum = (4, HEADS, 64, 128)
    return pl.pallas_call(
        functools.partial(attention_kernel, blocks=blocks),
        grid_spec=pltpu.PrefetchScalarGridSpec(
            num_scalar_prefetch=1,
            grid=(4,),
            in_specs=[whole(x.shape), whole(mine.shape), whole(other.shape)],
            out_specs=[whole(x.shape), whole(half_sum), whole(half_sum)],
            scratch_shapes=[
                pltpu.VMEM((KEYS, 128), BF),
                pltpu.VMEM((128, KEYS), BF),
                pltpu.VMEM((128, KEYS), BF),
                pltpu.VMEM((KEYS, 128), BF),
                pltpu.VMEM((KEYS, 128), BF),
                pltpu.VMEM((KEYS, 128), BF),
                pltpu.VMEM((KEYS, KEYS), F32),
                pltpu.VMEM((KEYS, KEYS), F32),
            ],
        ),
        out_shape=[
            jax.ShapeDtypeStruct(x.shape, BF),
            jax.ShapeDtypeStruct(half_sum, BF),
            jax.ShapeDtypeStruct(half_sum, BF),
        ],
        compiler_params=params(),
        cost_estimate=pl.CostEstimate(
            flops=4 * 6 * 2 * KEYS * KEYS * 256, bytes_accessed=8 * 2**20, transcendentals=4 * KEYS * KEYS
        ),
        name="attention",
    )(place, x, mine, other)


def gate_kernel(core_ref, back_ref, gate_ref, gg_ref, ggate_ref, gated_ref, send_ref):
    other = 1 - core_ref[0]
    flat = gate_ref.shape[1]
    att = back_ref[:, :DH, :].astype(F32).reshape(C, flat)
    gate = gate_ref[...]
    opened = att * gate
    gated = opened.astype(BF)
    gated_ref[...] = gated
    for q in range(4):
        send_ref[8 + q] = gated[q * 192 : (q + 1) * 192]
    ggate_ref[...] = (gg_ref[...].astype(F32) * opened * (1.0 - gate)).astype(BF).reshape(4, 4 * DH, flat)
    for n in range(8):
        send_ref[n] = head_rows(back_ref, ggate_ref, n, other)


def head_rows(back_ref, ggate_ref, n, core):
    kind = n // 2
    group = (n % 2) * 2 + core
    if kind == 3:
        return ggate_ref[group]
    flat = back_ref.shape[2]
    return back_ref[pl.ds(group * 4, 4), (kind + 1) * DH : (kind + 2) * DH, :].reshape(4 * DH, flat)


def gate_step(core, back, gate, ggated):
    def whole(shape):
        return pl.BlockSpec(shape, lambda t, core: (0,) * len(shape))

    flat = gate.shape[1]
    shapes = [(4, 4 * DH, flat), (C, flat), (12, 4 * DH, flat)]
    return pl.pallas_call(
        gate_kernel,
        grid_spec=pltpu.PrefetchScalarGridSpec(
            num_scalar_prefetch=1,
            grid=(1,),
            in_specs=[whole(back.shape), whole(gate.shape), whole(ggated.shape)],
            out_specs=[whole(s) for s in shapes],
        ),
        out_shape=[jax.ShapeDtypeStruct(s, BF) for s in shapes],
        compiler_params=params(),
        cost_estimate=pl.CostEstimate(flops=6 * C * flat, bytes_accessed=6 * 2**20, transcendentals=0),
        name="gate",
    )(core, back, gate, ggated)


def input_grad_kernel(back_ref, ggate_ref, w_ref, normed_ref, inv_ref, gain_ref, grad_ref, total_s):
    step = pl.program_id(0)
    flat = normed_ref.shape[0]

    for kind in range(4):

        @pl.when(step == kind)
        def _(kind=kind):
            if kind == 3:
                total_s[...] += dot(w_ref[...], ggate_ref[...].reshape(C, flat))
            else:
                rows = back_ref[:, (kind + 1) * DH : (kind + 2) * DH, :].reshape(C, flat)
                part = dot(w_ref[...], rows)
                if kind == 0:
                    total_s[...] = part
                else:
                    total_s[...] += part

    @pl.when(step == 3)
    def _():
        normed = normed_ref[...]
        grad_normed = total_s[...].T * gain_ref[...].reshape(1, C)
        grad_ref[...] = (
            inv_ref[...]
            * (
                grad_normed
                - jnp.mean(grad_normed, -1, keepdims=True)
                - normed * jnp.mean(grad_normed * normed, -1, keepdims=True)
            )
        ).astype(BF)


def input_grad(back, ggate, w_in, normed, inv_std, ln_gain):
    flat = normed.shape[0]

    def whole(shape):
        return pl.BlockSpec(shape, lambda t: (0,) * len(shape))

    return pl.pallas_call(
        input_grad_kernel,
        grid=(4,),
        in_specs=[
            whole(back.shape),
            whole(ggate.shape),
            pl.BlockSpec((C, C), lambda t: (0, t)),
            whole((flat, C)),
            whole((flat, 1)),
            whole((C,)),
        ],
        out_specs=whole((flat, C)),
        out_shape=jax.ShapeDtypeStruct((flat, C), BF),
        scratch_shapes=[pltpu.VMEM((C, flat), F32)],
        compiler_params=params(),
        cost_estimate=pl.CostEstimate(
            flops=2 * flat * C * 4 * C, bytes_accessed=8 * 2**20, transcendentals=0
        ),
        name="input_grad",
    )(back, ggate, w_in, normed, inv_std, ln_gain)


def weight_kernel(
    core_ref, back_ref, ggate_ref, o_ref, gated_ref, sc_ref, sco_ref, do_ref, doo_ref, wt_ref, gain_ref,
    out_ref, scaled_s, gated_s, sum_s,
):
    core = core_ref[0]
    step = pl.program_id(0)
    flat = sc_ref.shape[0]
    last = pl.num_programs(0) - 1

    @pl.when(step == 0)
    def _():
        scaled_s[:flat] = sc_ref[...]
        scaled_s[flat:] = sco_ref[...]
        gated_s[:flat] = gated_ref[...].T
        gated_s[flat:] = o_ref[8:12].reshape(C, flat).T
        sum_s[...] = jnp.zeros_like(sum_s)

    for kind in range(4):

        @pl.when(step == kind)
        def _(kind=kind):
            blocks = [
                jnp.concatenate([head_rows(back_ref, ggate_ref, n, core), o_ref[n]], axis=1)
                for n in (2 * kind, 2 * kind + 1)
            ]
            win = dot(jnp.concatenate(blocks, axis=0), scaled_s[...])
            tails = jnp.concatenate(
                [
                    jnp.concatenate([do_ref[n], doo_ref[n]], axis=1)
                    for n in (2 * kind, 2 * kind + 1)
                ],
                axis=0,
            )
            wout = dot(tails, gated_s[...])
            weights = wt_ref[2 * kind : 2 * kind + 2].reshape(8 * DH, C).astype(F32)
            sum_s[...] += jnp.sum((win * weights).reshape(DH, 8, C), axis=0)
            for k in range(16):
                out_ref[kind * 16 + k] = jnp.concatenate(
                    [win[k * 24 : k * 24 + 24], wout[k * 8 : k * 8 + 8]], axis=0
                ).astype(BF)

    @pl.when(step == last)
    def _():
        gain = jnp.sum(sum_s[...], axis=0, keepdims=True) / gain_ref[...].reshape(1, C)
        gain_hi = gain.astype(BF).astype(F32)
        row = lax.broadcasted_iota(jnp.int32, (16, C), 0)
        extra = jnp.where(row == 14, gain_hi, gain - gain_hi).astype(BF)
        for k in range(64):
            out_ref[k, 16:] = jnp.where(row >= 14, extra, out_ref[k, 16:])


def weight_grads(core, operands):
    def whole(shape):
        return pl.BlockSpec(shape, lambda t, core: (0,) * len(shape))

    flat = operands[4].shape[0]
    return pl.pallas_call(
        weight_kernel,
        grid_spec=pltpu.PrefetchScalarGridSpec(
            num_scalar_prefetch=1,
            grid=(4,),
            in_specs=[whole(o.shape) for o in operands],
            out_specs=whole((64, 32, C)),
            scratch_shapes=[
                pltpu.VMEM((2 * flat, C), BF),
                pltpu.VMEM((2 * flat, C), BF),
                pltpu.VMEM((8, C), F32),
            ],
        ),
        out_shape=jax.ShapeDtypeStruct((64, 32, C), BF),
        compiler_params=params(),
        cost_estimate=pl.CostEstimate(
            flops=2 * 2 * flat * C * 2048, bytes_accessed=8 * 2**20, transcendentals=0
        ),
        name="weight_grads",
    )(core, *operands)


def per_device(act, pair_bias, ln_gain, w_in, w_out, d_out):
    sample_count, row_count, channels = act.shape
    flat = sample_count * row_count
    core = lax.axis_index("core")
    core_arg = jnp.full((1,), core, jnp.int32)
    own_x = lax.axis_index("x")
    place = jnp.stack([core, own_x]).astype(jnp.int32)
    zh = lax.axis_index("zh")

    bias = lax.dynamic_slice(pair_bias, (zh * 8, (own_x * 2 + core) * 16, 0), (8, 16, KEYS))
    bias = lax.all_to_all(bias, ("zl", "y"), 0, 0, tiled=True)

    rows_out = d_out.reshape(flat, channels)
    scaled, normed, inv_std, send, gate, ggated = front(
        act.reshape(flat, channels), ln_gain, w_in, w_out, rows_out
    )
    bias, send = lax.optimization_barrier((bias, send))
    bias = jnp.stack([bias] + [lax.ppermute(bias, "x", turn(s)) for s in (1, 2, 3)])
    bias_other = lax.ppermute(bias, "core", SWAP)
    received = lax.all_to_all(send, PLANE, 0, 0, tiled=True)

    dout_t = jnp.pad(rows_out.T.reshape(128, 6, flat), ((0, 0), (0, 2), (0, 0)))
    dout_t = dout_t.reshape(8, 2, 64, flat)
    dout_mine = lax.dynamic_index_in_dim(dout_t, core, 1, keepdims=False)
    dout_send = lax.dynamic_index_in_dim(dout_t, 1 - core, 1, keepdims=False)
    dout_other = lax.ppermute(dout_send, "core", SWAP)
    scaled_other = lax.ppermute(scaled, "core", SWAP)

    w_rows = lax.dynamic_index_in_dim(w_in.T.reshape(8, 2, 4 * DH, C), core, 1, keepdims=False)
    received, dout_mine, dout_other, scaled_other, w_rows = lax.optimization_barrier(
        (received, dout_mine, dout_other, scaled_other, w_rows)
    )
    result, keep, give = attention(place, received, bias, bias_other)
    back = lax.all_to_all(result, PLANE, 0, 0, tiled=True)

    got = lax.ppermute(give, "core", SWAP)
    sums = [(keep[s].astype(F32) + got[s].astype(F32)).astype(BF) for s in range(4)]
    gb = sums[0].astype(F32)
    for s in (1, 2, 3):
        gb = gb + lax.ppermute(sums[s], "x", turn(s)).astype(F32)
    back, gb = lax.optimization_barrier((back, gb.astype(BF)))
    gb = lax.all_to_all(gb, PLANE, 0, 0, tiled=True)

    ggate, gated, half = gate_step(core_arg, back, gate, ggated)
    other = lax.ppermute(half, "core", SWAP)
    chunks = weight_grads(
        core_arg,
        (back, ggate, other, gated, scaled, scaled_other, dout_mine, dout_other, w_rows, ln_gain),
    )
    chunks, gated, ggate, gb = lax.optimization_barrier((chunks, gated, ggate, gb))
    grad_act = input_grad(back, ggate, w_in, normed, inv_std, ln_gain)
    gb = gb.astype(F32)
    grad_bias = jnp.concatenate([gb[:, :, :64], gb[:, :, 64:]], axis=1)
    output = jnp.einsum("cr,cd->rd", gated, w_out, preferred_element_type=F32).astype(BF)
    chunks = lax.all_to_all(chunks, ("x", "zh", "zl", "y"), 0, 0, tiled=True)
    total = jnp.sum(chunks.astype(F32), axis=0)
    gain = total[30] + total[31]
    return (
        output.reshape(sample_count, row_count, channels),
        grad_act.reshape(sample_count, row_count, channels),
        grad_bias,
        gain + lax.ppermute(gain, "core", SWAP),
        total[:24].T,
        total[24:30].T,
    )


def solution(mesh):
    fine = Mesh(mesh.devices.reshape(4, 2, 2, 2, 4), ("x", "zh", "core", "zl", "y"))
    sample = ("x", "zh", "core")
    tok = ("zl", "y")
    return jax.shard_map(
        per_device,
        mesh=fine,
        in_specs=(
            P(sample, tok, None),
            P(None, tok, None),
            P(),
            P(),
            P(),
            P(sample, tok, None),
        ),
        out_specs=(
            P(sample, tok, None),
            P(sample, tok, None),
            P(None, tok, sample),
            P(),
            P(None, sample + tok),
            P(None, sample + tok),
        ),
        check_vma=False,
    )
```

```python
import functools
import math

import jax
import jax.numpy as jnp
from jax import lax
from jax.experimental import pallas as pl
from jax.experimental.pallas import tpu as pltpu
from jax.sharding import Mesh
from jax.sharding import PartitionSpec as P

EPS = 1e-05
LOG2E = math.log2(math.e)
BF = jnp.bfloat16
F32 = jnp.float32
C = 768
HEADS = 16
DH = 48
TOK = 128
KEYS = 1024
PLANE = ("zh", "zl", "y")
SWAP = [(0, 1), (1, 0)]
SCALE = 1.0 / math.sqrt(DH)
VMEM_LIMIT = 60 * 1024 * 1024


def dot(a, b):
    return jnp.dot(a, b, preferred_element_type=F32)


def dot_nt(a, b):
    return lax.dot_general(a, b, (((1,), (1,)), ((), ())), preferred_element_type=F32)


def turn(shift):
    return [(i, (i + shift) % 4) for i in range(4)]


def params():
    return pltpu.CompilerParams(vmem_limit_bytes=VMEM_LIMIT)


def front_kernel(
    act_ref, gain_ref, w_ref, wout_ref, dout_ref, scaled_ref, normed_ref, inv_ref, send_ref, gate_ref, gg_ref
):
    step = pl.program_id(0)
    flat = act_ref.shape[0]

    @pl.when(step == 0)
    def _():
        values = act_ref[...].astype(F32)
        center = jnp.mean(values, -1, keepdims=True)
        shifted = values - center
        spread = jnp.mean(shifted * shifted, -1, keepdims=True)
        inv_std = lax.rsqrt(spread + EPS)
        normed = shifted * inv_std
        normed_ref[...] = normed
        inv_ref[...] = inv_std
        scaled_ref[...] = (normed * gain_ref[...].reshape(1, C)).astype(BF)

    block = dot(scaled_ref[...], w_ref[...])

    for kind in range(3):

        @pl.when(step == kind)
        def _(kind=kind):
            send_ref[:, kind * DH : (kind + 1) * DH, :] = block.astype(BF).T.reshape(HEADS, DH, flat)

    @pl.when(step == 3)
    def _():
        gate = jax.nn.sigmoid(block.T)
        ggated = dot_nt(wout_ref[...], dout_ref[...]).astype(BF)
        gate_ref[...] = gate
        gg_ref[...] = ggated
        send_ref[:, 3 * DH : 4 * DH, :] = (ggated.astype(F32) * gate).astype(BF).reshape(HEADS, DH, flat)


def front(act, ln_gain, w_in, w_out, d_out):
    flat = act.shape[0]
    shapes = [
        ((flat, C), BF),
        ((flat, C), F32),
        ((flat, 1), F32),
        ((HEADS, 4 * DH, flat), BF),
        ((C, flat), F32),
        ((C, flat), BF),
    ]

    def whole(shape):
        return pl.BlockSpec(shape, lambda t: (0,) * len(shape))

    return pl.pallas_call(
        front_kernel,
        grid=(4,),
        in_specs=[
            whole((flat, C)),
            whole((C,)),
            pl.BlockSpec((C, C), lambda t: (0, t)),
            whole((C, C)),
            whole((flat, C)),
        ],
        out_specs=[whole(s) for s, _ in shapes],
        out_shape=[jax.ShapeDtypeStruct(s, d) for s, d in shapes],
        compiler_params=params(),
        cost_estimate=pl.CostEstimate(
            flops=2 * flat * C * 5 * C, bytes_accessed=11 * 2**20, transcendentals=flat * C
        ),
        name="front",
    )(act, ln_gain, w_in, w_out, d_out)


def attention_kernel(
    place_ref, x_ref, mine_ref, other_ref, out_ref, keep_ref, give_ref,
    qa_s, ka_s, va_s, vt_s, kn_s, gn_s, gb_s, bias_s, *, blocks,
):
    core = place_ref[0]
    own_x = place_ref[1]
    sample = pl.program_id(0)
    half = sample // 2
    lane0 = pl.multiple_of((sample % 2) * TOK, TOK)

    @pl.when(sample == 0)
    def _():
        for t in range(8):
            pieces = []
            for x in range(4):
                mine = mine_ref[(own_x - x + 4) % 4, t]
                other = other_ref[(own_x - x + 4) % 4, t]
                pieces += [jnp.where(core == 0, mine, other), jnp.where(core == 0, other, mine)]
            bias_s[t * TOK : (t + 1) * TOK] = jnp.concatenate(pieces, axis=0).astype(F32) * LOG2E

    whole = jnp.concatenate([x_ref[half * 8 + t, :, pl.ds(lane0, TOK)] for t in range(8)], axis=1)
    qt, kt, vt, gt = (whole[i * DH : (i + 1) * DH] for i in range(4))
    qs = qt.astype(F32) * (SCALE * LOG2E)
    q_hi = qs.astype(BF)
    q_lo = (qs - q_hi.astype(F32)).astype(BF)
    zeros32 = jnp.zeros((32, KEYS), BF)
    zeros64 = jnp.zeros((64, KEYS), BF)
    zeros80 = jnp.zeros((80, KEYS), BF)
    ones16 = jnp.ones((16, KEYS), BF)
    qa_s[...] = jnp.concatenate([q_hi, q_lo, zeros32], axis=0).T
    ka_s[...] = jnp.concatenate([kt, kt, zeros32], axis=0)
    v_one = jnp.concatenate([vt, ones16, zeros64], axis=0)
    va_s[...] = v_one
    vt_s[...] = v_one.T
    kn_s[...] = jnp.concatenate([kt, zeros80], axis=0).T
    gn_s[...] = jnp.concatenate([gt, zeros80], axis=0).T

    rows = KEYS // blocks
    every = [slice(i * rows, (i + 1) * rows) for i in range(blocks)]
    lane = lax.broadcasted_iota(jnp.int32, (rows, 128), 1)
    scores = [dot(qa_s[p], ka_s[...]) + bias_s[p] for p in every]
    expd = [jnp.exp2(s - jnp.max(s, axis=1, keepdims=True)) for s in scores]
    expd_low = [e.astype(BF) for e in expd]
    summed = [dot(e, vt_s[...]) for e in expd_low]
    inv = [1.0 / s[:, DH : DH + 1] for s in summed]
    out = [s * i for s, i in zip(summed, inv)]
    gscaled = [(gn_s[p].astype(F32) * i).astype(BF).astype(F32) for p, i in zip(every, inv)]
    left = []
    for o, g in zip(out, gscaled):
        delta = jnp.sum(o * g, axis=1, keepdims=True)
        delta_hi = delta.astype(BF).astype(F32)
        left.append(
            jnp.where(lane == DH, -delta_hi, jnp.where(lane == DH + 1, delta_hi - delta, g)).astype(BF)
        )
    dscores = [e * dot(l, va_s[...]) for e, l in zip(expd, left)]
    dscores_low = [d.astype(BF) for d in dscores]

    @pl.when(sample == 0)
    def _():
        for p, d in zip(every, dscores):
            gb_s[p] = d

    @pl.when((sample > 0) & (sample < 3))
    def _():
        for p, d in zip(every, dscores):
            gb_s[p] = gb_s[p] + d

    @pl.when(sample == 3)
    def _():
        for p, d in zip(every, dscores):
            total = (gb_s[p] + d).astype(BF)
            for t in range(rows // TOK):
                for n in range(8):
                    tile = total[t * TOK : (t + 1) * TOK, n * TOK : (n + 1) * TOK]
                    low = jnp.concatenate([tile[:64, :64], tile[64:, :64]], axis=1)
                    high = jnp.concatenate([tile[:64, 64:], tile[64:, 64:]], axis=1)
                    where = (n % 2) * 8 + p.start // TOK + t
                    ahead = (n // 2 - own_x + 4) % 4
                    keep_ref[ahead, where] = jnp.where(core == 0, low, high)
                    give_ref[ahead, where] = jnp.where(core == 0, high, low)

    all_low = jnp.concatenate(dscores_low, axis=0)
    gscaled_t = jnp.concatenate(gscaled, axis=0).T.astype(BF)
    out_t = jnp.concatenate(out, axis=0).T[:DH].astype(BF)
    dquery_t = (dot(all_low, kn_s[...]) * SCALE).T[:DH].astype(BF)
    dkey_t = (dot(qt, all_low) * SCALE).astype(BF)
    dvalue_t = dot(gscaled_t[:DH], jnp.concatenate(expd_low, axis=0)).astype(BF)
    for t in range(8):
        cols = slice(t * TOK, (t + 1) * TOK)
        for i, part in enumerate((out_t, dquery_t, dkey_t, dvalue_t)):
            out_ref[half * 8 + t, i * DH : (i + 1) * DH, pl.ds(lane0, TOK)] = part[:, cols]


def attention(place, x, mine, other, blocks=4):
    def whole(shape):
        return pl.BlockSpec(shape, lambda s, place: (0,) * len(shape))

    half_sum = (4, HEADS, 64, 128)
    return pl.pallas_call(
        functools.partial(attention_kernel, blocks=blocks),
        grid_spec=pltpu.PrefetchScalarGridSpec(
            num_scalar_prefetch=1,
            grid=(4,),
            in_specs=[whole(x.shape), whole(mine.shape), whole(other.shape)],
            out_specs=[whole(x.shape), whole(half_sum), whole(half_sum)],
            scratch_shapes=[
                pltpu.VMEM((KEYS, 128), BF),
                pltpu.VMEM((128, KEYS), BF),
                pltpu.VMEM((128, KEYS), BF),
                pltpu.VMEM((KEYS, 128), BF),
                pltpu.VMEM((KEYS, 128), BF),
                pltpu.VMEM((KEYS, 128), BF),
                pltpu.VMEM((KEYS, KEYS), F32),
                pltpu.VMEM((KEYS, KEYS), F32),
            ],
        ),
        out_shape=[
            jax.ShapeDtypeStruct(x.shape, BF),
            jax.ShapeDtypeStruct(half_sum, BF),
            jax.ShapeDtypeStruct(half_sum, BF),
        ],
        compiler_params=params(),
        cost_estimate=pl.CostEstimate(
            flops=4 * 6 * 2 * KEYS * KEYS * 256, bytes_accessed=8 * 2**20, transcendentals=4 * KEYS * KEYS
        ),
        name="attention",
    )(place, x, mine, other)


def turn_kernel(core_ref, w_ref, out_ref, turned_s):
    turned_s[...] = w_ref[...].T
    out_ref[0] = turned_s[pl.ds(pl.multiple_of(core_ref[0] * 4 * DH, 4 * DH), 4 * DH), :]


def turn_half(core, w_in):
    return pl.pallas_call(
        turn_kernel,
        grid_spec=pltpu.PrefetchScalarGridSpec(
            num_scalar_prefetch=1,
            grid=(8,),
            in_specs=[pl.BlockSpec((C, 8 * DH), lambda n, core: (0, n))],
            out_specs=pl.BlockSpec((1, 4 * DH, C), lambda n, core: (n, 0, 0)),
            scratch_shapes=[pltpu.VMEM((8 * DH, C), BF)],
        ),
        out_shape=jax.ShapeDtypeStruct((8, 4 * DH, C), BF),
        compiler_params=params(),
        cost_estimate=pl.CostEstimate(flops=8 * C * C, bytes_accessed=7 * 2**20, transcendentals=0),
        name="turn_half",
    )(core, w_in)


def gate_kernel(core_ref, back_ref, gate_ref, gg_ref, ggate_ref, gated_ref, send_ref):
    other = 1 - core_ref[0]
    group = pl.program_id(0)
    flat = gate_ref.shape[1]
    att = back_ref[:, :DH, :].astype(F32).reshape(4 * DH, flat)
    gate = gate_ref[...]
    opened = att * gate
    gated = opened.astype(BF)
    ggate = (gg_ref[...].astype(F32) * opened * (1.0 - gate)).astype(BF)
    gated_ref[...] = gated
    ggate_ref[0] = ggate
    send_ref[8 + group] = gated

    @pl.when(group % 2 == other)
    def _():
        for kind in range(3):
            send_ref[2 * kind + group // 2] = back_ref[:, (kind + 1) * DH : (kind + 2) * DH, :].reshape(
                4 * DH, flat
            )
        send_ref[6 + group // 2] = ggate


def head_rows(back_ref, ggate_ref, n, core):
    kind = n // 2
    group = (n % 2) * 2 + core
    if kind == 3:
        return ggate_ref[group]
    flat = back_ref.shape[2]
    return back_ref[pl.ds(group * 4, 4), (kind + 1) * DH : (kind + 2) * DH, :].reshape(4 * DH, flat)


def gate_step(core, back, gate, ggated):
    flat = gate.shape[1]
    rows = pl.BlockSpec((4 * DH, flat), lambda t, core: (t, 0))
    shapes = [(4, 4 * DH, flat), (C, flat), (12, 4 * DH, flat)]
    return pl.pallas_call(
        gate_kernel,
        grid_spec=pltpu.PrefetchScalarGridSpec(
            num_scalar_prefetch=1,
            grid=(4,),
            in_specs=[pl.BlockSpec((4, 4 * DH, flat), lambda t, core: (t, 0, 0)), rows, rows],
            out_specs=[
                pl.BlockSpec((1, 4 * DH, flat), lambda t, core: (t, 0, 0)),
                rows,
                pl.BlockSpec(shapes[2], lambda t, core: (0, 0, 0)),
            ],
        ),
        out_shape=[jax.ShapeDtypeStruct(s, BF) for s in shapes],
        compiler_params=params(),
        cost_estimate=pl.CostEstimate(flops=6 * C * flat, bytes_accessed=6 * 2**20, transcendentals=0),
        name="gate",
    )(core, back, gate, ggated)


def input_grad_kernel(back_ref, ggate_ref, w_ref, normed_ref, inv_ref, gain_ref, grad_ref, total_s):
    step = pl.program_id(0)
    flat = normed_ref.shape[0]

    for kind in range(4):

        @pl.when(step == kind)
        def _(kind=kind):
            if kind == 3:
                total_s[...] += dot(w_ref[...], ggate_ref[...].reshape(C, flat))
            else:
                rows = back_ref[:, (kind + 1) * DH : (kind + 2) * DH, :].reshape(C, flat)
                part = dot(w_ref[...], rows)
                if kind == 0:
                    total_s[...] = part
                else:
                    total_s[...] += part

    @pl.when(step == 3)
    def _():
        normed = normed_ref[...]
        grad_normed = total_s[...].T * gain_ref[...].reshape(1, C)
        grad_ref[...] = (
            inv_ref[...]
            * (
                grad_normed
                - jnp.mean(grad_normed, -1, keepdims=True)
                - normed * jnp.mean(grad_normed * normed, -1, keepdims=True)
            )
        ).astype(BF)


def input_grad(back, ggate, w_in, normed, inv_std, ln_gain):
    flat = normed.shape[0]

    def whole(shape):
        return pl.BlockSpec(shape, lambda t: (0,) * len(shape))

    return pl.pallas_call(
        input_grad_kernel,
        grid=(4,),
        in_specs=[
            whole(back.shape),
            whole(ggate.shape),
            pl.BlockSpec((C, C), lambda t: (0, t)),
            whole((flat, C)),
            whole((flat, 1)),
            whole((C,)),
        ],
        out_specs=whole((flat, C)),
        out_shape=jax.ShapeDtypeStruct((flat, C), BF),
        scratch_shapes=[pltpu.VMEM((C, flat), F32)],
        compiler_params=params(),
        cost_estimate=pl.CostEstimate(
            flops=2 * flat * C * 4 * C, bytes_accessed=8 * 2**20, transcendentals=0
        ),
        name="input_grad",
    )(back, ggate, w_in, normed, inv_std, ln_gain)


def weight_kernel(
    core_ref, back_ref, ggate_ref, o_ref, gated_ref, sc_ref, sco_ref, do_ref, doo_ref, wt_ref, gain_ref,
    out_ref, scaled_s, gated_s, sum_s,
):
    core = core_ref[0]
    step = pl.program_id(0)
    flat = sc_ref.shape[0]
    last = pl.num_programs(0) - 1

    @pl.when(step == 0)
    def _():
        scaled_s[:flat] = sc_ref[...]
        scaled_s[flat:] = sco_ref[...]
        gated_s[:flat] = gated_ref[...].T
        gated_s[flat:] = o_ref[8:12].reshape(C, flat).T
        sum_s[...] = jnp.zeros_like(sum_s)

    for kind in range(4):

        @pl.when(step == kind)
        def _(kind=kind):
            blocks = [
                jnp.concatenate([head_rows(back_ref, ggate_ref, n, core), o_ref[n]], axis=1)
                for n in (2 * kind, 2 * kind + 1)
            ]
            win = dot(jnp.concatenate(blocks, axis=0), scaled_s[...])
            tails = jnp.concatenate(
                [
                    jnp.concatenate([do_ref[n], doo_ref[n]], axis=1)
                    for n in (2 * kind, 2 * kind + 1)
                ],
                axis=0,
            )
            wout = dot(tails, gated_s[...])
            weights = wt_ref[...].reshape(8 * DH, C).astype(F32)
            sum_s[...] += jnp.sum((win * weights).reshape(DH, 8, C), axis=0)
            for k in range(16):
                out_ref[kind * 16 + k] = jnp.concatenate(
                    [win[k * 24 : k * 24 + 24], wout[k * 8 : k * 8 + 8]], axis=0
                ).astype(BF)

    @pl.when(step == last)
    def _():
        gain = jnp.sum(sum_s[...], axis=0, keepdims=True) / gain_ref[...].reshape(1, C)
        gain_hi = gain.astype(BF).astype(F32)
        row = lax.broadcasted_iota(jnp.int32, (16, C), 0)
        extra = jnp.where(row == 14, gain_hi, gain - gain_hi).astype(BF)
        for k in range(64):
            out_ref[k, 16:] = jnp.where(row >= 14, extra, out_ref[k, 16:])


def weight_grads(core, operands):
    def whole(shape):
        return pl.BlockSpec(shape, lambda t, core: (0,) * len(shape))

    flat = operands[4].shape[0]
    return pl.pallas_call(
        weight_kernel,
        grid_spec=pltpu.PrefetchScalarGridSpec(
            num_scalar_prefetch=1,
            grid=(4,),
            in_specs=[whole(o.shape) for o in operands[:8]]
            + [pl.BlockSpec((2, 4 * DH, C), lambda t, core: (t, 0, 0)), whole(operands[9].shape)],
            out_specs=whole((64, 32, C)),
            scratch_shapes=[
                pltpu.VMEM((2 * flat, C), BF),
                pltpu.VMEM((2 * flat, C), BF),
                pltpu.VMEM((8, C), F32),
            ],
        ),
        out_shape=jax.ShapeDtypeStruct((64, 32, C), BF),
        compiler_params=params(),
        cost_estimate=pl.CostEstimate(
            flops=2 * 2 * flat * C * 2048, bytes_accessed=8 * 2**20, transcendentals=0
        ),
        name="weight_grads",
    )(core, *operands)


def per_device(act, pair_bias, ln_gain, w_in, w_out, d_out):
    sample_count, row_count, channels = act.shape
    flat = sample_count * row_count
    core = lax.axis_index("core")
    core_arg = jnp.full((1,), core, jnp.int32)
    own_x = lax.axis_index("x")
    place = jnp.stack([core, own_x]).astype(jnp.int32)
    zh = lax.axis_index("zh")

    bias = lax.dynamic_slice(pair_bias, (zh * 8, (own_x * 2 + core) * 16, 0), (8, 16, KEYS))
    bias = lax.all_to_all(bias, ("zl", "y"), 0, 0, tiled=True)

    rows_out = d_out.reshape(flat, channels)
    scaled, normed, inv_std, send, gate, ggated = front(
        act.reshape(flat, channels), ln_gain, w_in, w_out, rows_out
    )
    bias, send = lax.optimization_barrier((bias, send))
    pieces = [bias] + [lax.ppermute(bias, "x", turn(s)) for s in (1, 2, 3)]
    received = lax.all_to_all(send, PLANE, 0, 0, tiled=True)

    dout_t = jnp.pad(rows_out.T.reshape(128, 6, flat), ((0, 0), (0, 2), (0, 0)))
    dout_t = dout_t.reshape(8, 2, 64, flat)
    dout_mine = lax.dynamic_index_in_dim(dout_t, core, 1, keepdims=False)
    dout_send = lax.dynamic_index_in_dim(dout_t, 1 - core, 1, keepdims=False)
    scaled_other = lax.ppermute(scaled, "core", SWAP)

    w_rows = turn_half(core_arg, w_in)
    pieces, dout_mine, dout_send, w_rows = lax.optimization_barrier((pieces, dout_mine, dout_send, w_rows))
    bias = jnp.stack(pieces)
    bias_other = lax.ppermute(bias, "core", SWAP)
    dout_other = lax.ppermute(dout_send, "core", SWAP)
    received, dout_other, scaled_other, bias_other = lax.optimization_barrier(
        (received, dout_other, scaled_other, bias_other)
    )
    result, keep, give = attention(place, received, bias, bias_other)
    back = lax.all_to_all(result, PLANE, 0, 0, tiled=True)

    got = lax.ppermute(give, "core", SWAP)
    sums = [(keep[s].astype(F32) + got[s].astype(F32)).astype(BF) for s in range(4)]
    gb = sums[0].astype(F32)
    for s in (1, 2, 3):
        gb = gb + lax.ppermute(sums[s], "x", turn(s)).astype(F32)
    back, gb = lax.optimization_barrier((back, gb.astype(BF)))
    gb = lax.all_to_all(gb, PLANE, 0, 0, tiled=True)

    ggate, gated, half = gate_step(core_arg, back, gate, ggated)
    other = lax.ppermute(half, "core", SWAP)
    chunks = weight_grads(
        core_arg,
        (back, ggate, other, gated, scaled, scaled_other, dout_mine, dout_other, w_rows, ln_gain),
    )
    chunks, gated, ggate, gb = lax.optimization_barrier((chunks, gated, ggate, gb))
    grad_act = input_grad(back, ggate, w_in, normed, inv_std, ln_gain)
    gb = gb.astype(F32)
    grad_bias = jnp.concatenate([gb[:, :, :64], gb[:, :, 64:]], axis=1)
    output = jnp.einsum("cr,cd->rd", gated, w_out, preferred_element_type=F32).astype(BF)
    chunks = lax.all_to_all(chunks, ("x", "zh", "zl", "y"), 0, 0, tiled=True)
    total = jnp.sum(chunks.astype(F32), axis=0)
    gain = total[30] + total[31]
    return (
        output.reshape(sample_count, row_count, channels),
        grad_act.reshape(sample_count, row_count, channels),
        grad_bias,
        gain + lax.ppermute(gain, "core", SWAP),
        total[:24].T,
        total[24:30].T,
    )


def solution(mesh):
    fine = Mesh(mesh.devices.reshape(4, 2, 2, 2, 4), ("x", "zh", "core", "zl", "y"))
    sample = ("x", "zh", "core")
    tok = ("zl", "y")
    return jax.shard_map(
        per_device,
        mesh=fine,
        in_specs=(
            P(sample, tok, None),
            P(None, tok, None),
            P(),
            P(),
            P(),
            P(sample, tok, None),
        ),
        out_specs=(
            P(sample, tok, None),
            P(sample, tok, None),
            P(None, tok, sample),
            P(),
            P(None, sample + tok),
            P(None, sample + tok),
        ),
        check_vma=False,
    )
```

```python
import functools
import math

import jax
import jax.numpy as jnp
from jax import lax
from jax.experimental import pallas as pl
from jax.experimental.pallas import tpu as pltpu
from jax.sharding import Mesh
from jax.sharding import PartitionSpec as P

EPS = 1e-05
LOG2E = math.log2(math.e)
BF = jnp.bfloat16
F32 = jnp.float32
C = 768
HEADS = 16
DH = 48
TOK = 128
KEYS = 1024
PLANE = ("zh", "zl", "y")
SWAP = [(0, 1), (1, 0)]
SCALE = 1.0 / math.sqrt(DH)
MIB = 1024 * 1024


def in_vmem(x):
    return pltpu.with_memory_space_constraint(x, pltpu.VMEM)


def dot(a, b):
    return jnp.dot(a, b, preferred_element_type=F32)


def dot_nt(a, b):
    return lax.dot_general(a, b, (((1,), (1,)), ((), ())), preferred_element_type=F32)


def turn(shift):
    return [(i, (i + shift) % 4) for i in range(4)]


def params(mib=20):
    return pltpu.CompilerParams(vmem_limit_bytes=mib * MIB)


def front_kernel(
    act_ref, gain_ref, w_ref, wout_ref, dout_ref, scaled_ref, mean_ref, inv_ref, send_ref, gate_ref, gg_ref
):
    step = pl.program_id(0)
    flat = act_ref.shape[0]

    @pl.when(step == 0)
    def _():
        values = act_ref[...].astype(F32)
        center = jnp.mean(values, -1, keepdims=True)
        shifted = values - center
        spread = jnp.mean(shifted * shifted, -1, keepdims=True)
        inv_std = lax.rsqrt(spread + EPS)
        mean_ref[...] = center
        inv_ref[...] = inv_std
        scaled_ref[...] = (shifted * inv_std * gain_ref[...].reshape(1, C)).astype(BF)

    block = dot(scaled_ref[...], w_ref[...])
    rows = pl.ds(pl.multiple_of(step * 4 * DH, 4 * DH), 4 * DH)
    gg_ref[rows, :] = dot_nt(wout_ref[...], dout_ref[...]).astype(BF)

    @pl.when(step < 3)
    def _():
        send_ref[...] = block.astype(BF).T.reshape(HEADS, DH, flat)

    @pl.when(step == 3)
    def _():
        gate = jax.nn.sigmoid(block.T)
        gate_ref[...] = gate
        send_ref[...] = (gg_ref[...].astype(F32) * gate).astype(BF).reshape(HEADS, DH, flat)


def front(act, ln_gain, w_in, w_out, d_out):
    flat = act.shape[0]

    def whole(shape):
        return pl.BlockSpec(shape, lambda t: (0,) * len(shape))

    outs = [
        ((flat, C), BF, whole((flat, C))),
        ((flat, 1), F32, whole((flat, 1))),
        ((flat, 1), F32, whole((flat, 1))),
        ((HEADS, 4 * DH, flat), BF, pl.BlockSpec((HEADS, DH, flat), lambda t: (0, t, 0))),
        ((C, flat), F32, whole((C, flat))),
        ((C, flat), BF, whole((C, flat))),
    ]
    return pl.pallas_call(
        front_kernel,
        grid=(4,),
        in_specs=[
            whole((flat, C)),
            whole((C,)),
            pl.BlockSpec((C, C), lambda t: (0, t)),
            pl.BlockSpec((4 * DH, C), lambda t: (t, 0)),
            whole((flat, C)),
        ],
        out_specs=[spec for _, _, spec in outs],
        out_shape=[jax.ShapeDtypeStruct(shape, kind) for shape, kind, _ in outs],
        compiler_params=params(60),
        cost_estimate=pl.CostEstimate(
            flops=2 * flat * C * 5 * C, bytes_accessed=11 * 2**20, transcendentals=flat * C
        ),
        name="front",
    )(act, ln_gain, w_in, w_out, d_out)


def attention_kernel(
    place_ref, x_ref, mine_ref, other_ref, out_ref, keep_ref, give_ref,
    qa_s, ka_s, va_s, vt_s, kn_s, gn_s, gb_s, bias_s, *, blocks,
):
    core = place_ref[0]
    own_x = place_ref[1]
    sample = pl.program_id(0)

    @pl.when(sample == 0)
    def _():
        for t in range(8):
            pieces = []
            for x in range(4):
                mine = mine_ref[(own_x - x + 4) % 4, t]
                other = other_ref[(own_x - x + 4) % 4, t]
                pieces += [jnp.where(core == 0, mine, other), jnp.where(core == 0, other, mine)]
            bias_s[t * TOK : (t + 1) * TOK] = jnp.concatenate(pieces, axis=0).astype(F32) * LOG2E

    whole = jnp.concatenate([x_ref[t] for t in range(8)], axis=1)
    qt, kt, vt, gt = (whole[i * DH : (i + 1) * DH] for i in range(4))
    qs = qt.astype(F32) * (SCALE * LOG2E)
    q_hi = qs.astype(BF)
    q_lo = (qs - q_hi.astype(F32)).astype(BF)
    zeros32 = jnp.zeros((32, KEYS), BF)
    zeros64 = jnp.zeros((64, KEYS), BF)
    zeros80 = jnp.zeros((80, KEYS), BF)
    ones16 = jnp.ones((16, KEYS), BF)
    qa_s[...] = jnp.concatenate([q_hi, q_lo, zeros32], axis=0).T
    ka_s[...] = jnp.concatenate([kt, kt, zeros32], axis=0)
    v_one = jnp.concatenate([vt, ones16, zeros64], axis=0)
    va_s[...] = v_one
    vt_s[...] = v_one.T
    kn_s[...] = jnp.concatenate([kt, zeros80], axis=0).T
    gn_s[...] = jnp.concatenate([gt, zeros80], axis=0).T

    rows = KEYS // blocks
    every = [slice(i * rows, (i + 1) * rows) for i in range(blocks)]
    lane = lax.broadcasted_iota(jnp.int32, (rows, 128), 1)
    scores = [dot(qa_s[p], ka_s[...]) + bias_s[p] for p in every]
    expd = [jnp.exp2(s - jnp.max(s, axis=1, keepdims=True)) for s in scores]
    expd_low = [e.astype(BF) for e in expd]
    summed = [dot(e, vt_s[...]) for e in expd_low]
    inv = [1.0 / s[:, DH : DH + 1] for s in summed]
    out = [s * i for s, i in zip(summed, inv)]
    gscaled = [(gn_s[p].astype(F32) * i).astype(BF).astype(F32) for p, i in zip(every, inv)]
    left = []
    for o, g in zip(out, gscaled):
        delta = jnp.sum(o * g, axis=1, keepdims=True)
        delta_hi = delta.astype(BF).astype(F32)
        left.append(
            jnp.where(lane == DH, -delta_hi, jnp.where(lane == DH + 1, delta_hi - delta, g)).astype(BF)
        )
    dscores = [e * dot(l, va_s[...]) for e, l in zip(expd, left)]
    dscores_low = [d.astype(BF) for d in dscores]

    @pl.when(sample == 0)
    def _():
        for p, d in zip(every, dscores):
            gb_s[p] = d

    @pl.when((sample > 0) & (sample < 3))
    def _():
        for p, d in zip(every, dscores):
            gb_s[p] = gb_s[p] + d

    @pl.when(sample == 3)
    def _():
        for p, d in zip(every, dscores):
            total = (gb_s[p] + d).astype(BF)
            for t in range(rows // TOK):
                for n in range(8):
                    tile = total[t * TOK : (t + 1) * TOK, n * TOK : (n + 1) * TOK]
                    low = jnp.concatenate([tile[:64, :64], tile[64:, :64]], axis=1)
                    high = jnp.concatenate([tile[:64, 64:], tile[64:, 64:]], axis=1)
                    where = (n % 2) * 8 + p.start // TOK + t
                    ahead = (n // 2 - own_x + 4) % 4
                    keep_ref[ahead, where] = jnp.where(core == 0, low, high)
                    give_ref[ahead, where] = jnp.where(core == 0, high, low)

    all_low = jnp.concatenate(dscores_low, axis=0)
    gscaled_t = jnp.concatenate(gscaled, axis=0).T.astype(BF)
    out_t = jnp.concatenate(out, axis=0).T[:DH].astype(BF)
    dquery_t = (dot(all_low, kn_s[...]) * SCALE).T[:DH].astype(BF)
    dkey_t = (dot(qt, all_low) * SCALE).astype(BF)
    dvalue_t = dot(gscaled_t[:DH], jnp.concatenate(expd_low, axis=0)).astype(BF)
    for t in range(8):
        cols = slice(t * TOK, (t + 1) * TOK)
        for i, part in enumerate((out_t, dquery_t, dkey_t, dvalue_t)):
            out_ref[t, i * DH : (i + 1) * DH, :] = part[:, cols]


def attention(place, x, mine, other, blocks=4):
    def whole(shape):
        return pl.BlockSpec(shape, lambda s, place: (0,) * len(shape))

    one = pl.BlockSpec((8, 4 * DH, TOK), lambda s, place: (s // 2, 0, s % 2))
    half_sum = (4, HEADS, 64, 128)
    return pl.pallas_call(
        functools.partial(attention_kernel, blocks=blocks),
        grid_spec=pltpu.PrefetchScalarGridSpec(
            num_scalar_prefetch=1,
            grid=(4,),
            in_specs=[one, whole(mine.shape), whole(other.shape)],
            out_specs=[one, whole(half_sum), whole(half_sum)],
            scratch_shapes=[
                pltpu.VMEM((KEYS, 128), BF),
                pltpu.VMEM((128, KEYS), BF),
                pltpu.VMEM((128, KEYS), BF),
                pltpu.VMEM((KEYS, 128), BF),
                pltpu.VMEM((KEYS, 128), BF),
                pltpu.VMEM((KEYS, 128), BF),
                pltpu.VMEM((KEYS, KEYS), F32),
                pltpu.VMEM((KEYS, KEYS), F32),
            ],
        ),
        out_shape=[
            jax.ShapeDtypeStruct(x.shape, BF),
            jax.ShapeDtypeStruct(half_sum, BF),
            jax.ShapeDtypeStruct(half_sum, BF),
        ],
        compiler_params=params(60),
        cost_estimate=pl.CostEstimate(
            flops=4 * 6 * 2 * KEYS * KEYS * 256, bytes_accessed=8 * 2**20, transcendentals=4 * KEYS * KEYS
        ),
        name="attention",
    )(place, x, mine, other)


def stage_kernel(core_ref, w_ref, sc_ref, sco_ref, do_ref, doo_ref, wt_ref, scaled_ref, dout_ref, turned_s):
    n = pl.program_id(0)
    flat = sc_ref.shape[0]

    @pl.when(n == 0)
    def _():
        scaled_ref[:flat] = sc_ref[...]
        scaled_ref[flat:] = sco_ref[...]
        dout_ref[:, :, :flat] = do_ref[...]
        dout_ref[:, :, flat:] = doo_ref[...]

    turned_s[...] = w_ref[...].T
    wt_ref[n] = turned_s[pl.ds(pl.multiple_of(core_ref[0] * 4 * DH, 4 * DH), 4 * DH), :]


def stage(core, w_in, *early):
    def whole(shape):
        return pl.BlockSpec(shape, lambda t, core: (0,) * len(shape))

    flat = early[0].shape[0]
    shapes = [(8, 4 * DH, C), (2 * flat, C), (8, 64, 2 * flat)]
    return pl.pallas_call(
        stage_kernel,
        grid_spec=pltpu.PrefetchScalarGridSpec(
            num_scalar_prefetch=1,
            grid=(8,),
            in_specs=[pl.BlockSpec((C, 8 * DH), lambda n, core: (0, n))] + [whole(e.shape) for e in early],
            out_specs=[whole(s) for s in shapes],
            scratch_shapes=[pltpu.VMEM((8 * DH, C), BF)],
        ),
        out_shape=[pltpu.VMEM(s, BF) for s in shapes],
        compiler_params=params(24),
        cost_estimate=pl.CostEstimate(flops=8 * C * C, bytes_accessed=7 * 2**20, transcendentals=0),
        name="stage",
    )(core, w_in, *early)


def gate_kernel(core_ref, back_ref, gate_ref, gg_ref, ggate_ref, gated_ref, send_ref):
    other = 1 - core_ref[0]
    flat = gate_ref.shape[1]
    att = back_ref[:, :DH, :].astype(F32).reshape(C, flat)
    gate = gate_ref[...]
    opened = att * gate
    gated = opened.astype(BF)
    gated_ref[...] = gated
    for q in range(4):
        send_ref[8 + q] = gated[q * 192 : (q + 1) * 192]
    ggate_ref[...] = (gg_ref[...].astype(F32) * opened * (1.0 - gate)).astype(BF).reshape(4, 4 * DH, flat)
    for n in range(8):
        send_ref[n] = head_rows(back_ref, ggate_ref, n, other)


def head_rows(back_ref, ggate_ref, n, core):
    kind = n // 2
    group = (n % 2) * 2 + core
    if kind == 3:
        return ggate_ref[group]
    flat = back_ref.shape[2]
    return back_ref[pl.ds(group * 4, 4), (kind + 1) * DH : (kind + 2) * DH, :].reshape(4 * DH, flat)


def gate_step(core, back, gate, ggated):
    def whole(shape):
        return pl.BlockSpec(shape, lambda t, core: (0,) * len(shape))

    flat = gate.shape[1]
    shapes = [(4, 4 * DH, flat), (C, flat), (12, 4 * DH, flat)]
    return pl.pallas_call(
        gate_kernel,
        grid_spec=pltpu.PrefetchScalarGridSpec(
            num_scalar_prefetch=1,
            grid=(1,),
            in_specs=[whole(back.shape), whole(gate.shape), whole(ggated.shape)],
            out_specs=[whole(s) for s in shapes],
        ),
        out_shape=[jax.ShapeDtypeStruct(s, BF) for s in shapes],
        compiler_params=params(20),
        cost_estimate=pl.CostEstimate(flops=6 * C * flat, bytes_accessed=6 * 2**20, transcendentals=0),
        name="gate",
    )(core, back, gate, ggated)


def input_grad_kernel(back_ref, ggate_ref, w_ref, act_ref, mean_ref, inv_ref, gain_ref, grad_ref, total_s):
    step = pl.program_id(0)
    flat = act_ref.shape[0]

    for kind in range(4):

        @pl.when(step == kind)
        def _(kind=kind):
            if kind == 3:
                total_s[...] += dot(w_ref[...], ggate_ref[...].reshape(C, flat))
            else:
                rows = back_ref[:, (kind + 1) * DH : (kind + 2) * DH, :].reshape(C, flat)
                part = dot(w_ref[...], rows)
                if kind == 0:
                    total_s[...] = part
                else:
                    total_s[...] += part

    @pl.when(step == 3)
    def _():
        normed = (act_ref[...].astype(F32) - mean_ref[...]) * inv_ref[...]
        grad_normed = total_s[...].T * gain_ref[...].reshape(1, C)
        grad_ref[...] = (
            inv_ref[...]
            * (
                grad_normed
                - jnp.mean(grad_normed, -1, keepdims=True)
                - normed * jnp.mean(grad_normed * normed, -1, keepdims=True)
            )
        ).astype(BF)


def input_grad(back, ggate, w_in, act, mean, inv_std, ln_gain):
    flat = act.shape[0]

    def whole(shape):
        return pl.BlockSpec(shape, lambda t: (0,) * len(shape))

    return pl.pallas_call(
        input_grad_kernel,
        grid=(4,),
        in_specs=[
            whole(back.shape),
            whole(ggate.shape),
            pl.BlockSpec((C, C), lambda t: (0, t)),
            whole((flat, C)),
            whole((flat, 1)),
            whole((flat, 1)),
            whole((C,)),
        ],
        out_specs=whole((flat, C)),
        out_shape=jax.ShapeDtypeStruct((flat, C), BF),
        scratch_shapes=[pltpu.VMEM((C, flat), F32)],
        compiler_params=params(60),
        cost_estimate=pl.CostEstimate(
            flops=2 * flat * C * 4 * C, bytes_accessed=8 * 2**20, transcendentals=0
        ),
        name="input_grad",
    )(back, ggate, w_in, act, mean, inv_std, ln_gain)


def weight_kernel(
    core_ref, back_ref, ggate_ref, o_ref, gated_ref, scaled_ref, dout_ref, wt_ref, gain_ref, out_ref, gated_s, sum_s
):
    core = core_ref[0]
    step = pl.program_id(0)
    flat = gated_ref.shape[1]
    last = pl.num_programs(0) - 1

    @pl.when(step == 0)
    def _():
        gated_s[:flat] = gated_ref[...].T
        gated_s[flat:] = o_ref[8:12].reshape(C, flat).T
        sum_s[...] = jnp.zeros_like(sum_s)

    for kind in range(4):

        @pl.when(step == kind)
        def _(kind=kind):
            blocks = [
                jnp.concatenate([head_rows(back_ref, ggate_ref, n, core), o_ref[n]], axis=1)
                for n in (2 * kind, 2 * kind + 1)
            ]
            win = dot(jnp.concatenate(blocks, axis=0), scaled_ref[...])
            wout = dot(dout_ref[2 * kind : 2 * kind + 2].reshape(128, 2 * flat), gated_s[...])
            weights = wt_ref[2 * kind : 2 * kind + 2].reshape(8 * DH, C).astype(F32)
            sum_s[...] += jnp.sum((win * weights).reshape(DH, 8, C), axis=0)
            for k in range(16):
                out_ref[kind * 16 + k] = jnp.concatenate(
                    [win[k * 24 : k * 24 + 24], wout[k * 8 : k * 8 + 8]], axis=0
                ).astype(BF)

    @pl.when(step == last)
    def _():
        gain = jnp.sum(sum_s[...], axis=0, keepdims=True) / gain_ref[...].reshape(1, C)
        gain_hi = gain.astype(BF).astype(F32)
        row = lax.broadcasted_iota(jnp.int32, (16, C), 0)
        extra = jnp.where(row == 14, gain_hi, gain - gain_hi).astype(BF)
        for k in range(64):
            out_ref[k, 16:] = jnp.where(row >= 14, extra, out_ref[k, 16:])


def weight_grads(core, operands):
    def whole(shape):
        return pl.BlockSpec(shape, lambda t, core: (0,) * len(shape))

    flat = operands[3].shape[1]
    return pl.pallas_call(
        weight_kernel,
        grid_spec=pltpu.PrefetchScalarGridSpec(
            num_scalar_prefetch=1,
            grid=(4,),
            in_specs=[whole(o.shape) for o in operands],
            out_specs=whole((64, 32, C)),
            scratch_shapes=[
                pltpu.VMEM((2 * flat, C), BF),
                pltpu.VMEM((8, C), F32),
            ],
        ),
        out_shape=jax.ShapeDtypeStruct((64, 32, C), BF),
        compiler_params=params(24),
        cost_estimate=pl.CostEstimate(
            flops=2 * 2 * flat * C * 2048, bytes_accessed=8 * 2**20, transcendentals=0
        ),
        name="weight_grads",
    )(core, *operands)


def per_device(act, pair_bias, ln_gain, w_in, w_out, d_out):
    sample_count, row_count, channels = act.shape
    flat = sample_count * row_count
    core = lax.axis_index("core")
    core_arg = jnp.full((1,), core, jnp.int32)
    own_x = lax.axis_index("x")
    place = jnp.stack([core, own_x]).astype(jnp.int32)
    zh = lax.axis_index("zh")

    bias = lax.dynamic_slice(pair_bias, (zh * 8, (own_x * 2 + core) * 16, 0), (8, 16, KEYS))
    bias = lax.all_to_all(bias, ("zl", "y"), 0, 0, tiled=True)

    rows_out = d_out.reshape(flat, channels)
    act = act.reshape(flat, channels)
    scaled, mean, inv_std, send, gate, ggated = front(
        act, ln_gain, w_in, w_out, rows_out
    )
    bias, send = lax.optimization_barrier((bias, send))
    pieces = [bias] + [lax.ppermute(bias, "x", turn(s)) for s in (1, 2, 3)]
    received = lax.all_to_all(send, PLANE, 0, 0, tiled=True)

    dout_t = jnp.pad(rows_out.T.reshape(128, 6, flat), ((0, 0), (0, 2), (0, 0)))
    dout_t = dout_t.reshape(8, 2, 64, flat)
    dout_mine = lax.dynamic_index_in_dim(dout_t, core, 1, keepdims=False)
    dout_send = lax.dynamic_index_in_dim(dout_t, 1 - core, 1, keepdims=False)
    scaled_other = lax.ppermute(scaled, "core", SWAP)

    pieces, dout_mine, dout_send = lax.optimization_barrier((pieces, dout_mine, dout_send))
    bias = jnp.stack(pieces)
    bias_other = lax.ppermute(bias, "core", SWAP)
    dout_other = lax.ppermute(dout_send, "core", SWAP)
    received, dout_other, scaled_other, bias_other = lax.optimization_barrier(
        (received, dout_other, scaled_other, bias_other)
    )
    result, keep, give = attention(place, received, bias, bias_other)
    back = lax.all_to_all(result, PLANE, 0, 0, tiled=True)

    keep, scaled, scaled_other, dout_mine, dout_other = lax.optimization_barrier(
        (keep, scaled, scaled_other, dout_mine, dout_other)
    )
    got = lax.ppermute(give, "core", SWAP)
    sums = [(keep[s].astype(F32) + got[s].astype(F32)).astype(BF) for s in range(4)]
    gb = sums[0].astype(F32)
    for s in (1, 2, 3):
        gb = gb + lax.ppermute(sums[s], "x", turn(s)).astype(F32)
    staged = stage(core_arg, w_in, scaled, scaled_other, dout_mine, dout_other)
    back, gb, staged = lax.optimization_barrier((back, gb.astype(BF), staged))
    gb = lax.all_to_all(gb, PLANE, 0, 0, tiled=True)

    ggate, gated, half = gate_step(core_arg, back, gate, ggated)
    other = lax.ppermute(half, "core", SWAP)
    chunks = weight_grads(
        core_arg,
        (back, ggate, other, gated, in_vmem(staged[1]), in_vmem(staged[2]), in_vmem(staged[0]), ln_gain),
    )
    chunks, gated, ggate, gb = lax.optimization_barrier((chunks, gated, ggate, gb))
    grad_act = input_grad(back, ggate, w_in, act, mean, inv_std, ln_gain)
    gb = gb.astype(F32)
    grad_bias = jnp.concatenate([gb[:, :, :64], gb[:, :, 64:]], axis=1)
    output = jnp.einsum("cr,cd->rd", gated, w_out, preferred_element_type=F32).astype(BF)
    chunks = lax.all_to_all(chunks, ("x", "zh", "zl", "y"), 0, 0, tiled=True)
    total = jnp.sum(chunks.astype(F32), axis=0)
    gain = total[30] + total[31]
    return (
        output.reshape(sample_count, row_count, channels),
        grad_act.reshape(sample_count, row_count, channels),
        grad_bias,
        gain + lax.ppermute(gain, "core", SWAP),
        total[:24].T,
        total[24:30].T,
    )


def solution(mesh):
    fine = Mesh(mesh.devices.reshape(4, 2, 2, 2, 4), ("x", "zh", "core", "zl", "y"))
    sample = ("x", "zh", "core")
    tok = ("zl", "y")
    return jax.shard_map(
        per_device,
        mesh=fine,
        in_specs=(
            P(sample, tok, None),
            P(None, tok, None),
            P(),
            P(),
            P(),
            P(sample, tok, None),
        ),
        out_specs=(
            P(sample, tok, None),
            P(sample, tok, None),
            P(None, tok, sample),
            P(),
            P(None, sample + tok),
            P(None, sample + tok),
        ),
        check_vma=False,
    )
```

```python
import functools
import math

import jax
import jax.numpy as jnp
from jax import lax
from jax.experimental import pallas as pl
from jax.experimental.pallas import tpu as pltpu
from jax.sharding import Mesh
from jax.sharding import PartitionSpec as P

EPS = 1e-05
LOG2E = math.log2(math.e)
BF = jnp.bfloat16
F32 = jnp.float32
C = 768
HEADS = 16
DH = 48
TOK = 128
KEYS = 1024
PLANE = ("zh", "zl", "y")
SWAP = [(0, 1), (1, 0)]
SCALE = 1.0 / math.sqrt(DH)
MIB = 1024 * 1024


def in_vmem(x):
    return pltpu.with_memory_space_constraint(x, pltpu.VMEM)


def dot(a, b):
    return jnp.dot(a, b, preferred_element_type=F32)


def dot_nt(a, b):
    return lax.dot_general(a, b, (((1,), (1,)), ((), ())), preferred_element_type=F32)


def turn(shift):
    return [(i, (i + shift) % 4) for i in range(4)]


def params(mib=20):
    return pltpu.CompilerParams(vmem_limit_bytes=mib * MIB)


def front_kernel(
    act_ref, gain_ref, w_ref, wout_ref, dout_ref, scaled_ref, mean_ref, inv_ref, send_ref, gate_ref, gg_ref
):
    step = pl.program_id(0)
    flat = act_ref.shape[0]

    @pl.when(step == 0)
    def _():
        values = act_ref[...].astype(F32)
        center = jnp.mean(values, -1, keepdims=True)
        shifted = values - center
        spread = jnp.mean(shifted * shifted, -1, keepdims=True)
        inv_std = lax.rsqrt(spread + EPS)
        mean_ref[...] = center
        inv_ref[...] = inv_std
        scaled_ref[...] = (shifted * inv_std * gain_ref[...].reshape(1, C)).astype(BF)

    block = dot(scaled_ref[...], w_ref[...])
    rows = pl.ds(pl.multiple_of(step * 4 * DH, 4 * DH), 4 * DH)
    gg_ref[rows, :] = dot_nt(wout_ref[...], dout_ref[...]).astype(BF)

    @pl.when(step < 3)
    def _():
        send_ref[...] = block.astype(BF).T.reshape(HEADS, DH, flat)

    @pl.when(step == 3)
    def _():
        gate = jax.nn.sigmoid(block.T)
        gate_ref[...] = gate
        send_ref[...] = (gg_ref[...].astype(F32) * gate).astype(BF).reshape(HEADS, DH, flat)


def front(act, ln_gain, w_in, w_out, d_out):
    flat = act.shape[0]

    def whole(shape):
        return pl.BlockSpec(shape, lambda t: (0,) * len(shape))

    outs = [
        ((flat, C), BF, whole((flat, C))),
        ((flat, 1), F32, whole((flat, 1))),
        ((flat, 1), F32, whole((flat, 1))),
        ((HEADS, 4 * DH, flat), BF, pl.BlockSpec((HEADS, DH, flat), lambda t: (0, t, 0))),
        ((C, flat), F32, whole((C, flat))),
        ((C, flat), BF, whole((C, flat))),
    ]
    return pl.pallas_call(
        front_kernel,
        grid=(4,),
        in_specs=[
            whole((flat, C)),
            whole((C,)),
            pl.BlockSpec((C, C), lambda t: (0, t)),
            pl.BlockSpec((4 * DH, C), lambda t: (t, 0)),
            whole((flat, C)),
        ],
        out_specs=[spec for _, _, spec in outs],
        out_shape=[jax.ShapeDtypeStruct(shape, kind) for shape, kind, _ in outs],
        compiler_params=params(60),
        cost_estimate=pl.CostEstimate(
            flops=2 * flat * C * 5 * C, bytes_accessed=11 * 2**20, transcendentals=flat * C
        ),
        name="front",
    )(act, ln_gain, w_in, w_out, d_out)


def attention_kernel(
    place_ref, x_ref, mine_ref, other_ref, out_ref, keep_ref, give_ref,
    qa_s, ka_s, va_s, vt_s, kn_s, gn_s, gb_s, bias_s, *, blocks,
):
    core = place_ref[0]
    own_x = place_ref[1]
    sample = pl.program_id(0)

    @pl.when(sample == 0)
    def _():
        for t in range(8):
            pieces = []
            for x in range(4):
                mine = mine_ref[(own_x - x + 4) % 4, t]
                other = other_ref[(own_x - x + 4) % 4, t]
                pieces += [jnp.where(core == 0, mine, other), jnp.where(core == 0, other, mine)]
            gb_s[t * TOK : (t + 1) * TOK] = jnp.zeros((TOK, KEYS), F32)
            bias_s[t * TOK : (t + 1) * TOK] = jnp.concatenate(pieces, axis=0).astype(F32) * LOG2E

    whole = jnp.concatenate([x_ref[t] for t in range(8)], axis=1)
    qt, kt, vt, gt = (whole[i * DH : (i + 1) * DH] for i in range(4))
    qs = qt.astype(F32) * (SCALE * LOG2E)
    q_hi = qs.astype(BF)
    q_lo = (qs - q_hi.astype(F32)).astype(BF)
    zeros32 = jnp.zeros((32, KEYS), BF)
    zeros64 = jnp.zeros((64, KEYS), BF)
    zeros80 = jnp.zeros((80, KEYS), BF)
    ones16 = jnp.ones((16, KEYS), BF)
    qa_s[...] = jnp.concatenate([q_hi, q_lo, zeros32], axis=0).T
    ka_s[...] = jnp.concatenate([kt, kt, zeros32], axis=0)
    v_one = jnp.concatenate([vt, ones16, zeros64], axis=0)
    va_s[...] = v_one
    vt_s[...] = v_one.T
    kn_s[...] = jnp.concatenate([kt, zeros80], axis=0).T
    gn_s[...] = jnp.concatenate([gt, zeros80], axis=0).T

    rows = KEYS // blocks
    every = [slice(i * rows, (i + 1) * rows) for i in range(blocks)]
    lane = lax.broadcasted_iota(jnp.int32, (rows, 128), 1)
    scores = [dot(qa_s[p], ka_s[...]) + bias_s[p] for p in every]
    expd = [jnp.exp2(s - jnp.max(s, axis=1, keepdims=True)) for s in scores]
    expd_low = [e.astype(BF) for e in expd]
    summed = [dot(e, vt_s[...]) for e in expd_low]
    inv = [1.0 / s[:, DH : DH + 1] for s in summed]
    out = [s * i for s, i in zip(summed, inv)]
    gscaled = [(gn_s[p].astype(F32) * i).astype(BF).astype(F32) for p, i in zip(every, inv)]
    left = []
    for o, g in zip(out, gscaled):
        delta = jnp.sum(o * g, axis=1, keepdims=True)
        delta_hi = delta.astype(BF).astype(F32)
        left.append(
            jnp.where(lane == DH, -delta_hi, jnp.where(lane == DH + 1, delta_hi - delta, g)).astype(BF)
        )
    dscores = [e * dot(l, va_s[...]) for e, l in zip(expd, left)]
    dscores_low = [d.astype(BF) for d in dscores]

    for p, d in zip(every, dscores):
        gb_s[p] = gb_s[p] + d

    @pl.when(sample == 3)
    def _():
        for p, d in zip(every, dscores):
            total = gb_s[p].astype(BF)
            for t in range(rows // TOK):
                for n in range(8):
                    tile = total[t * TOK : (t + 1) * TOK, n * TOK : (n + 1) * TOK]
                    low = jnp.concatenate([tile[:64, :64], tile[64:, :64]], axis=1)
                    high = jnp.concatenate([tile[:64, 64:], tile[64:, 64:]], axis=1)
                    where = (n % 2) * 8 + p.start // TOK + t
                    ahead = (n // 2 - own_x + 4) % 4
                    keep_ref[ahead, where] = jnp.where(core == 0, low, high)
                    give_ref[ahead, where] = jnp.where(core == 0, high, low)

    all_low = jnp.concatenate(dscores_low, axis=0)
    gscaled_t = jnp.concatenate(gscaled, axis=0).T.astype(BF)
    out_t = jnp.concatenate(out, axis=0).T[:DH].astype(BF)
    dquery_t = (dot(all_low, kn_s[...]) * SCALE).T[:DH].astype(BF)
    dkey_t = (dot(qt, all_low) * SCALE).astype(BF)
    dvalue_t = dot(gscaled_t[:DH], jnp.concatenate(expd_low, axis=0)).astype(BF)
    for t in range(8):
        cols = slice(t * TOK, (t + 1) * TOK)
        for i, part in enumerate((out_t, dquery_t, dkey_t, dvalue_t)):
            out_ref[t, i * DH : (i + 1) * DH, :] = part[:, cols]


def attention(place, x, mine, other, blocks=4):
    def whole(shape):
        return pl.BlockSpec(shape, lambda s, place: (0,) * len(shape))

    one = pl.BlockSpec((8, 4 * DH, TOK), lambda s, place: (s // 2, 0, s % 2))
    half_sum = (4, HEADS, 64, 128)
    return pl.pallas_call(
        functools.partial(attention_kernel, blocks=blocks),
        grid_spec=pltpu.PrefetchScalarGridSpec(
            num_scalar_prefetch=1,
            grid=(4,),
            in_specs=[one, whole(mine.shape), whole(other.shape)],
            out_specs=[one, whole(half_sum), whole(half_sum)],
            scratch_shapes=[
                pltpu.VMEM((KEYS, 128), BF),
                pltpu.VMEM((128, KEYS), BF),
                pltpu.VMEM((128, KEYS), BF),
                pltpu.VMEM((KEYS, 128), BF),
                pltpu.VMEM((KEYS, 128), BF),
                pltpu.VMEM((KEYS, 128), BF),
                pltpu.VMEM((KEYS, KEYS), F32),
                pltpu.VMEM((KEYS, KEYS), F32),
            ],
        ),
        out_shape=[
            jax.ShapeDtypeStruct(x.shape, BF),
            jax.ShapeDtypeStruct(half_sum, BF),
            jax.ShapeDtypeStruct(half_sum, BF),
        ],
        compiler_params=params(60),
        cost_estimate=pl.CostEstimate(
            flops=4 * 6 * 2 * KEYS * KEYS * 256, bytes_accessed=8 * 2**20, transcendentals=4 * KEYS * KEYS
        ),
        name="attention",
    )(place, x, mine, other)


def stage_kernel(core_ref, w_ref, sc_ref, sco_ref, do_ref, doo_ref, wt_ref, scaled_ref, dout_ref, turned_s):
    n = pl.program_id(0)
    flat = sc_ref.shape[0]

    @pl.when(n == 0)
    def _():
        scaled_ref[:flat] = sc_ref[...]
        scaled_ref[flat:] = sco_ref[...]
        dout_ref[:, :, :flat] = do_ref[...]
        dout_ref[:, :, flat:] = doo_ref[...]

    turned_s[...] = w_ref[...].T
    wt_ref[n] = turned_s[pl.ds(pl.multiple_of(core_ref[0] * 4 * DH, 4 * DH), 4 * DH), :]


def stage(core, w_in, *early):
    def whole(shape):
        return pl.BlockSpec(shape, lambda t, core: (0,) * len(shape))

    flat = early[0].shape[0]
    shapes = [(8, 4 * DH, C), (2 * flat, C), (8, 64, 2 * flat)]
    return pl.pallas_call(
        stage_kernel,
        grid_spec=pltpu.PrefetchScalarGridSpec(
            num_scalar_prefetch=1,
            grid=(8,),
            in_specs=[pl.BlockSpec((C, 8 * DH), lambda n, core: (0, n))] + [whole(e.shape) for e in early],
            out_specs=[whole(s) for s in shapes],
            scratch_shapes=[pltpu.VMEM((8 * DH, C), BF)],
        ),
        out_shape=[pltpu.VMEM(s, BF) for s in shapes],
        compiler_params=params(24),
        cost_estimate=pl.CostEstimate(flops=8 * C * C, bytes_accessed=7 * 2**20, transcendentals=0),
        name="stage",
    )(core, w_in, *early)


def gate_kernel(core_ref, back_ref, gate_ref, gg_ref, ggate_ref, gated_ref, send_ref):
    other = 1 - core_ref[0]
    flat = gate_ref.shape[1]
    att = back_ref[:, :DH, :].astype(F32).reshape(C, flat)
    gate = gate_ref[...]
    opened = att * gate
    gated = opened.astype(BF)
    gated_ref[...] = gated
    for q in range(4):
        send_ref[8 + q] = gated[q * 192 : (q + 1) * 192]
    ggate_ref[...] = (gg_ref[...].astype(F32) * opened * (1.0 - gate)).astype(BF).reshape(4, 4 * DH, flat)
    for n in range(8):
        send_ref[n] = head_rows(back_ref, ggate_ref, n, other)


def head_rows(back_ref, ggate_ref, n, core):
    kind = n // 2
    group = (n % 2) * 2 + core
    if kind == 3:
        return ggate_ref[group]
    flat = back_ref.shape[2]
    return back_ref[pl.ds(group * 4, 4), (kind + 1) * DH : (kind + 2) * DH, :].reshape(4 * DH, flat)


def gate_step(core, back, gate, ggated):
    def whole(shape):
        return pl.BlockSpec(shape, lambda t, core: (0,) * len(shape))

    flat = gate.shape[1]
    shapes = [(4, 4 * DH, flat), (C, flat), (12, 4 * DH, flat)]
    return pl.pallas_call(
        gate_kernel,
        grid_spec=pltpu.PrefetchScalarGridSpec(
            num_scalar_prefetch=1,
            grid=(1,),
            in_specs=[whole(back.shape), whole(gate.shape), whole(ggated.shape)],
            out_specs=[whole(s) for s in shapes],
        ),
        out_shape=[jax.ShapeDtypeStruct(s, BF) for s in shapes],
        compiler_params=params(20),
        cost_estimate=pl.CostEstimate(flops=6 * C * flat, bytes_accessed=6 * 2**20, transcendentals=0),
        name="gate",
    )(core, back, gate, ggated)


def input_grad_kernel(back_ref, ggate_ref, w_ref, act_ref, mean_ref, inv_ref, gain_ref, grad_ref, total_s):
    step = pl.program_id(0)
    flat = act_ref.shape[0]

    for kind in range(4):

        @pl.when(step == kind)
        def _(kind=kind):
            if kind == 3:
                total_s[...] += dot(w_ref[...], ggate_ref[...].reshape(C, flat))
            else:
                rows = back_ref[:, (kind + 1) * DH : (kind + 2) * DH, :].reshape(C, flat)
                part = dot(w_ref[...], rows)
                if kind == 0:
                    total_s[...] = part
                else:
                    total_s[...] += part

    @pl.when(step == 3)
    def _():
        normed = (act_ref[...].astype(F32) - mean_ref[...]) * inv_ref[...]
        grad_normed = total_s[...].T * gain_ref[...].reshape(1, C)
        grad_ref[...] = (
            inv_ref[...]
            * (
                grad_normed
                - jnp.mean(grad_normed, -1, keepdims=True)
                - normed * jnp.mean(grad_normed * normed, -1, keepdims=True)
            )
        ).astype(BF)


def input_grad(back, ggate, w_in, act, mean, inv_std, ln_gain):
    flat = act.shape[0]

    def whole(shape):
        return pl.BlockSpec(shape, lambda t: (0,) * len(shape))

    return pl.pallas_call(
        input_grad_kernel,
        grid=(4,),
        in_specs=[
            whole(back.shape),
            whole(ggate.shape),
            pl.BlockSpec((C, C), lambda t: (0, t)),
            whole((flat, C)),
            whole((flat, 1)),
            whole((flat, 1)),
            whole((C,)),
        ],
        out_specs=whole((flat, C)),
        out_shape=jax.ShapeDtypeStruct((flat, C), BF),
        scratch_shapes=[pltpu.VMEM((C, flat), F32)],
        compiler_params=params(60),
        cost_estimate=pl.CostEstimate(
            flops=2 * flat * C * 4 * C, bytes_accessed=8 * 2**20, transcendentals=0
        ),
        name="input_grad",
    )(back, ggate, w_in, act, mean, inv_std, ln_gain)


def weight_kernel(
    core_ref, back_ref, ggate_ref, o_ref, gated_ref, scaled_ref, dout_ref, wt_ref, gain_ref, out_ref, gated_s, sum_s
):
    core = core_ref[0]
    step = pl.program_id(0)
    flat = gated_ref.shape[1]
    last = pl.num_programs(0) - 1

    @pl.when(step == 0)
    def _():
        gated_s[:flat] = gated_ref[...].T
        gated_s[flat:] = o_ref[8:12].reshape(C, flat).T
        sum_s[...] = jnp.zeros_like(sum_s)

    for kind in range(4):

        @pl.when(step == kind)
        def _(kind=kind):
            blocks = [
                jnp.concatenate([head_rows(back_ref, ggate_ref, n, core), o_ref[n]], axis=1)
                for n in (2 * kind, 2 * kind + 1)
            ]
            win = dot(jnp.concatenate(blocks, axis=0), scaled_ref[...])
            wout = dot(dout_ref[2 * kind : 2 * kind + 2].reshape(128, 2 * flat), gated_s[...])
            weights = wt_ref[2 * kind : 2 * kind + 2].reshape(8 * DH, C).astype(F32)
            sum_s[...] += jnp.sum((win * weights).reshape(DH, 8, C), axis=0)
            for k in range(16):
                out_ref[kind * 16 + k] = jnp.concatenate(
                    [win[k * 24 : k * 24 + 24], wout[k * 8 : k * 8 + 8]], axis=0
                ).astype(BF)

    @pl.when(step == last)
    def _():
        gain = jnp.sum(sum_s[...], axis=0, keepdims=True) / gain_ref[...].reshape(1, C)
        gain_hi = gain.astype(BF).astype(F32)
        row = lax.broadcasted_iota(jnp.int32, (16, C), 0)
        extra = jnp.where(row == 14, gain_hi, gain - gain_hi).astype(BF)
        for k in range(64):
            out_ref[k, 16:] = jnp.where(row >= 14, extra, out_ref[k, 16:])


def weight_grads(core, operands):
    def whole(shape):
        return pl.BlockSpec(shape, lambda t, core: (0,) * len(shape))

    flat = operands[3].shape[1]
    return pl.pallas_call(
        weight_kernel,
        grid_spec=pltpu.PrefetchScalarGridSpec(
            num_scalar_prefetch=1,
            grid=(4,),
            in_specs=[whole(o.shape) for o in operands],
            out_specs=whole((64, 32, C)),
            scratch_shapes=[
                pltpu.VMEM((2 * flat, C), BF),
                pltpu.VMEM((8, C), F32),
            ],
        ),
        out_shape=jax.ShapeDtypeStruct((64, 32, C), BF),
        compiler_params=params(24),
        cost_estimate=pl.CostEstimate(
            flops=2 * 2 * flat * C * 2048, bytes_accessed=8 * 2**20, transcendentals=0
        ),
        name="weight_grads",
    )(core, *operands)


def per_device(act, pair_bias, ln_gain, w_in, w_out, d_out):
    sample_count, row_count, channels = act.shape
    flat = sample_count * row_count
    core = lax.axis_index("core")
    core_arg = jnp.full((1,), core, jnp.int32)
    own_x = lax.axis_index("x")
    place = jnp.stack([core, own_x]).astype(jnp.int32)
    zh = lax.axis_index("zh")

    bias = lax.dynamic_slice(pair_bias, (zh * 8, (own_x * 2 + core) * 16, 0), (8, 16, KEYS))
    bias = lax.all_to_all(bias, ("zl", "y"), 0, 0, tiled=True)

    rows_out = d_out.reshape(flat, channels)
    act = act.reshape(flat, channels)
    scaled, mean, inv_std, send, gate, ggated = front(
        act, ln_gain, w_in, w_out, rows_out
    )
    bias, send = lax.optimization_barrier((bias, send))
    pieces = [bias] + [lax.ppermute(bias, "x", turn(s)) for s in (1, 2, 3)]
    received = lax.all_to_all(send, PLANE, 0, 0, tiled=True)

    dout_t = jnp.pad(rows_out.T.reshape(128, 6, flat), ((0, 0), (0, 2), (0, 0)))
    dout_t = dout_t.reshape(8, 2, 64, flat)
    dout_mine = lax.dynamic_index_in_dim(dout_t, core, 1, keepdims=False)
    dout_send = lax.dynamic_index_in_dim(dout_t, 1 - core, 1, keepdims=False)
    scaled_other = lax.ppermute(scaled, "core", SWAP)

    pieces, dout_mine, dout_send = lax.optimization_barrier((pieces, dout_mine, dout_send))
    bias = jnp.stack(pieces)
    bias_other = lax.ppermute(bias, "core", SWAP)
    dout_other = lax.ppermute(dout_send, "core", SWAP)
    received, dout_other, scaled_other, bias_other = lax.optimization_barrier(
        (received, dout_other, scaled_other, bias_other)
    )
    result, keep, give = attention(place, received, bias, bias_other)
    back = lax.all_to_all(result, PLANE, 0, 0, tiled=True)

    keep, scaled, scaled_other, dout_mine, dout_other = lax.optimization_barrier(
        (keep, scaled, scaled_other, dout_mine, dout_other)
    )
    got = lax.ppermute(give, "core", SWAP)
    sums = [(keep[s].astype(F32) + got[s].astype(F32)).astype(BF) for s in range(4)]
    gb = sums[0].astype(F32)
    for s in (1, 2, 3):
        gb = gb + lax.ppermute(sums[s], "x", turn(s)).astype(F32)
    staged = stage(core_arg, w_in, scaled, scaled_other, dout_mine, dout_other)
    back, gb, staged = lax.optimization_barrier((back, gb.astype(BF), staged))
    gb = lax.all_to_all(gb, PLANE, 0, 0, tiled=True)

    ggate, gated, half = gate_step(core_arg, back, gate, ggated)
    other = lax.ppermute(half, "core", SWAP)
    chunks = weight_grads(
        core_arg,
        (back, ggate, other, gated, in_vmem(staged[1]), in_vmem(staged[2]), in_vmem(staged[0]), ln_gain),
    )
    chunks, gated, ggate, gb = lax.optimization_barrier((chunks, gated, ggate, gb))
    grad_act = input_grad(back, ggate, w_in, act, mean, inv_std, ln_gain)
    gb = gb.astype(F32)
    grad_bias = jnp.concatenate([gb[:, :, :64], gb[:, :, 64:]], axis=1)
    output = jnp.einsum("cr,cd->rd", gated, w_out, preferred_element_type=F32).astype(BF)
    chunks = lax.all_to_all(chunks, ("x", "zh", "zl", "y"), 0, 0, tiled=True)
    total = jnp.sum(chunks.astype(F32), axis=0)
    gain = total[30] + total[31]
    return (
        output.reshape(sample_count, row_count, channels),
        grad_act.reshape(sample_count, row_count, channels),
        grad_bias,
        gain + lax.ppermute(gain, "core", SWAP),
        total[:24].T,
        total[24:30].T,
    )


def solution(mesh):
    fine = Mesh(mesh.devices.reshape(4, 2, 2, 2, 4), ("x", "zh", "core", "zl", "y"))
    sample = ("x", "zh", "core")
    tok = ("zl", "y")
    return jax.shard_map(
        per_device,
        mesh=fine,
        in_specs=(
            P(sample, tok, None),
            P(None, tok, None),
            P(),
            P(),
            P(),
            P(sample, tok, None),
        ),
        out_specs=(
            P(sample, tok, None),
            P(sample, tok, None),
            P(None, tok, sample),
            P(),
            P(None, sample + tok),
            P(None, sample + tok),
        ),
        check_vma=False,
    )
```

```python
import functools
import math

import jax
import jax.numpy as jnp
from jax import lax
from jax.experimental import pallas as pl
from jax.experimental.pallas import tpu as pltpu
from jax.sharding import Mesh
from jax.sharding import PartitionSpec as P

EPS = 1e-05
LOG2E = math.log2(math.e)
BF = jnp.bfloat16
F32 = jnp.float32
C = 768
HEADS = 16
DH = 48
TOK = 128
KEYS = 1024
PLANE = ("zh", "zl", "y")
SWAP = [(0, 1), (1, 0)]
SCALE = 1.0 / math.sqrt(DH)
MIB = 1024 * 1024


def in_vmem(x):
    return pltpu.with_memory_space_constraint(x, pltpu.VMEM)


def dot(a, b):
    return jnp.dot(a, b, preferred_element_type=F32)


def dot_nt(a, b):
    return lax.dot_general(a, b, (((1,), (1,)), ((), ())), preferred_element_type=F32)


def turn(shift):
    return [(i, (i + shift) % 4) for i in range(4)]


def params(mib=20):
    return pltpu.CompilerParams(vmem_limit_bytes=mib * MIB)


def front_kernel(
    act_ref, gain_ref, w_ref, wout_ref, dout_ref, scaled_ref, mean_ref, inv_ref, send_ref, gate_ref, gg_ref
):
    step = pl.program_id(0)
    flat = act_ref.shape[0]

    @pl.when(step == 0)
    def _():
        values = act_ref[...].astype(F32)
        center = jnp.mean(values, -1, keepdims=True)
        shifted = values - center
        spread = jnp.mean(shifted * shifted, -1, keepdims=True)
        inv_std = lax.rsqrt(spread + EPS)
        mean_ref[...] = center
        inv_ref[...] = inv_std
        scaled_ref[...] = (shifted * inv_std * gain_ref[...].reshape(1, C)).astype(BF)

    block = dot(scaled_ref[...], w_ref[...])
    rows = pl.ds(pl.multiple_of(step * 4 * DH, 4 * DH), 4 * DH)
    gg_ref[rows, :] = dot_nt(wout_ref[...], dout_ref[...]).astype(BF)

    @pl.when(step < 3)
    def _():
        send_ref[...] = block.astype(BF).T.reshape(HEADS, DH, flat)

    @pl.when(step == 3)
    def _():
        gate = jax.nn.sigmoid(block.T)
        gate_ref[...] = gate
        send_ref[...] = (gg_ref[...].astype(F32) * gate).astype(BF).reshape(HEADS, DH, flat)


def front(act, ln_gain, w_in, w_out, d_out):
    flat = act.shape[0]

    def whole(shape):
        return pl.BlockSpec(shape, lambda t: (0,) * len(shape))

    outs = [
        ((flat, C), BF, whole((flat, C))),
        ((flat, 1), F32, whole((flat, 1))),
        ((flat, 1), F32, whole((flat, 1))),
        ((HEADS, 4 * DH, flat), BF, pl.BlockSpec((HEADS, DH, flat), lambda t: (0, t, 0))),
        ((C, flat), F32, whole((C, flat))),
        ((C, flat), BF, whole((C, flat))),
    ]
    return pl.pallas_call(
        front_kernel,
        grid=(4,),
        in_specs=[
            whole((flat, C)),
            whole((C,)),
            pl.BlockSpec((C, C), lambda t: (0, t)),
            pl.BlockSpec((4 * DH, C), lambda t: (t, 0)),
            whole((flat, C)),
        ],
        out_specs=[spec for _, _, spec in outs],
        out_shape=[jax.ShapeDtypeStruct(shape, kind) for shape, kind, _ in outs],
        compiler_params=params(60),
        cost_estimate=pl.CostEstimate(
            flops=2 * flat * C * 5 * C, bytes_accessed=11 * 2**20, transcendentals=flat * C
        ),
        name="front",
    )(act, ln_gain, w_in, w_out, d_out)


def attention_kernel(
    place_ref, x_ref, mine_ref, other_ref, out_ref, keep_ref, give_ref,
    qa_s, ka_s, va_s, vt_s, kn_s, gn_s, gb_s, bias_s, *, blocks,
):
    core = place_ref[0]
    own_x = place_ref[1]
    sample = pl.program_id(0)

    @pl.when(sample == 0)
    def _():
        for t in range(8):
            pieces = []
            for x in range(4):
                mine = mine_ref[(own_x - x + 4) % 4, t]
                other = other_ref[(own_x - x + 4) % 4, t]
                pieces += [jnp.where(core == 0, mine, other), jnp.where(core == 0, other, mine)]
            gb_s[t * TOK : (t + 1) * TOK] = jnp.zeros((TOK, KEYS), F32)
            bias_s[t * TOK : (t + 1) * TOK] = jnp.concatenate(pieces, axis=0).astype(F32) * LOG2E

    whole = jnp.concatenate([x_ref[t] for t in range(8)], axis=1)
    qt, kt, vt, gt = (whole[i * DH : (i + 1) * DH] for i in range(4))
    qs = qt.astype(F32) * (SCALE * LOG2E)
    q_hi = qs.astype(BF)
    q_lo = (qs - q_hi.astype(F32)).astype(BF)
    zeros32 = jnp.zeros((32, KEYS), BF)
    zeros64 = jnp.zeros((64, KEYS), BF)
    zeros80 = jnp.zeros((80, KEYS), BF)
    ones16 = jnp.ones((16, KEYS), BF)
    qa_s[...] = jnp.concatenate([q_hi, q_lo, zeros32], axis=0).T
    ka_s[...] = jnp.concatenate([kt, kt, zeros32], axis=0)
    v_one = jnp.concatenate([vt, ones16, zeros64], axis=0)
    va_s[...] = v_one
    vt_s[...] = v_one.T
    kn_s[...] = jnp.concatenate([kt, zeros80], axis=0).T
    gn_s[...] = jnp.concatenate([gt, zeros80], axis=0).T

    rows = KEYS // blocks
    every = [slice(i * rows, (i + 1) * rows) for i in range(blocks)]
    lane = lax.broadcasted_iota(jnp.int32, (rows, 128), 1)
    scores = [dot(qa_s[p], ka_s[...]) + bias_s[p] for p in every]
    expd = [jnp.exp2(s - jnp.max(s, axis=1, keepdims=True)) for s in scores]
    expd_low = [e.astype(BF) for e in expd]
    summed = [dot(e, vt_s[...]) for e in expd_low]
    inv = [1.0 / s[:, DH : DH + 1] for s in summed]
    out = [s * i for s, i in zip(summed, inv)]
    gscaled = [(gn_s[p].astype(F32) * i).astype(BF).astype(F32) for p, i in zip(every, inv)]
    left = []
    for o, g in zip(out, gscaled):
        delta = jnp.sum(o * g, axis=1, keepdims=True)
        high = delta.astype(BF).astype(F32)
        middle = (delta - high).astype(BF).astype(F32)
        low = delta - high - middle
        tail = jnp.where(lane == DH, high, jnp.where(lane == DH + 1, middle, low))
        left.append(jnp.where((lane >= DH) & (lane <= DH + 2), -tail, g).astype(BF))
    dscores = [e * dot(l, va_s[...]) for e, l in zip(expd, left)]
    dscores_low = [d.astype(BF) for d in dscores]

    for p, d in zip(every, dscores):
        gb_s[p] = gb_s[p] + d

    @pl.when(sample == 3)
    def _():
        for p, d in zip(every, dscores):
            total = gb_s[p].astype(BF)
            for t in range(rows // TOK):
                for n in range(8):
                    tile = total[t * TOK : (t + 1) * TOK, n * TOK : (n + 1) * TOK]
                    low = jnp.concatenate([tile[:64, :64], tile[64:, :64]], axis=1)
                    high = jnp.concatenate([tile[:64, 64:], tile[64:, 64:]], axis=1)
                    where = (n % 2) * 8 + p.start // TOK + t
                    ahead = (n // 2 - own_x + 4) % 4
                    keep_ref[ahead, where] = jnp.where(core == 0, low, high)
                    give_ref[ahead, where] = jnp.where(core == 0, high, low)

    all_low = jnp.concatenate(dscores_low, axis=0)
    gscaled_t = jnp.concatenate(gscaled, axis=0).T.astype(BF)
    out_t = jnp.concatenate(out, axis=0).T[:DH].astype(BF)
    dquery_t = (dot(all_low, kn_s[...]) * SCALE).T[:DH].astype(BF)
    dkey_t = (dot(qt, all_low) * SCALE).astype(BF)
    dvalue_t = dot(gscaled_t[:DH], jnp.concatenate(expd_low, axis=0)).astype(BF)
    for t in range(8):
        cols = slice(t * TOK, (t + 1) * TOK)
        for i, part in enumerate((out_t, dquery_t, dkey_t, dvalue_t)):
            out_ref[t, i * DH : (i + 1) * DH, :] = part[:, cols]


def attention(place, x, mine, other, blocks=4):
    def whole(shape):
        return pl.BlockSpec(shape, lambda s, place: (0,) * len(shape))

    one = pl.BlockSpec((8, 4 * DH, TOK), lambda s, place: (s // 2, 0, s % 2))
    half_sum = (4, HEADS, 64, 128)
    return pl.pallas_call(
        functools.partial(attention_kernel, blocks=blocks),
        grid_spec=pltpu.PrefetchScalarGridSpec(
            num_scalar_prefetch=1,
            grid=(4,),
            in_specs=[one, whole(mine.shape), whole(other.shape)],
            out_specs=[one, whole(half_sum), whole(half_sum)],
            scratch_shapes=[
                pltpu.VMEM((KEYS, 128), BF),
                pltpu.VMEM((128, KEYS), BF),
                pltpu.VMEM((128, KEYS), BF),
                pltpu.VMEM((KEYS, 128), BF),
                pltpu.VMEM((KEYS, 128), BF),
                pltpu.VMEM((KEYS, 128), BF),
                pltpu.VMEM((KEYS, KEYS), F32),
                pltpu.VMEM((KEYS, KEYS), F32),
            ],
        ),
        out_shape=[
            jax.ShapeDtypeStruct(x.shape, BF),
            jax.ShapeDtypeStruct(half_sum, BF),
            jax.ShapeDtypeStruct(half_sum, BF),
        ],
        compiler_params=params(60),
        cost_estimate=pl.CostEstimate(
            flops=4 * 6 * 2 * KEYS * KEYS * 256, bytes_accessed=8 * 2**20, transcendentals=4 * KEYS * KEYS
        ),
        name="attention",
    )(place, x, mine, other)


def stage_kernel(core_ref, w_ref, sc_ref, sco_ref, do_ref, doo_ref, wt_ref, scaled_ref, dout_ref, turned_s):
    n = pl.program_id(0)
    flat = sc_ref.shape[0]

    @pl.when(n == 0)
    def _():
        scaled_ref[:flat] = sc_ref[...]
        scaled_ref[flat:] = sco_ref[...]
        dout_ref[:, :, :flat] = do_ref[...]
        dout_ref[:, :, flat:] = doo_ref[...]

    turned_s[...] = w_ref[...].T
    wt_ref[n] = turned_s[pl.ds(pl.multiple_of(core_ref[0] * 4 * DH, 4 * DH), 4 * DH), :]


def stage(core, w_in, *early):
    def whole(shape):
        return pl.BlockSpec(shape, lambda t, core: (0,) * len(shape))

    flat = early[0].shape[0]
    shapes = [(8, 4 * DH, C), (2 * flat, C), (8, 64, 2 * flat)]
    return pl.pallas_call(
        stage_kernel,
        grid_spec=pltpu.PrefetchScalarGridSpec(
            num_scalar_prefetch=1,
            grid=(8,),
            in_specs=[pl.BlockSpec((C, 8 * DH), lambda n, core: (0, n))] + [whole(e.shape) for e in early],
            out_specs=[whole(s) for s in shapes],
            scratch_shapes=[pltpu.VMEM((8 * DH, C), BF)],
        ),
        out_shape=[pltpu.VMEM(s, BF) for s in shapes],
        compiler_params=params(24),
        cost_estimate=pl.CostEstimate(flops=8 * C * C, bytes_accessed=7 * 2**20, transcendentals=0),
        name="stage",
    )(core, w_in, *early)


def gate_kernel(core_ref, back_ref, gate_ref, gg_ref, ggate_ref, gated_ref, send_ref):
    other = 1 - core_ref[0]
    flat = gate_ref.shape[1]
    att = back_ref[:, :DH, :].astype(F32).reshape(C, flat)
    gate = gate_ref[...]
    opened = att * gate
    gated = opened.astype(BF)
    gated_ref[...] = gated
    for q in range(4):
        send_ref[8 + q] = gated[q * 192 : (q + 1) * 192]
    ggate_ref[...] = (gg_ref[...].astype(F32) * opened * (1.0 - gate)).astype(BF).reshape(4, 4 * DH, flat)
    for n in range(8):
        send_ref[n] = head_rows(back_ref, ggate_ref, n, other)


def head_rows(back_ref, ggate_ref, n, core):
    kind = n // 2
    group = (n % 2) * 2 + core
    if kind == 3:
        return ggate_ref[group]
    flat = back_ref.shape[2]
    return back_ref[pl.ds(group * 4, 4), (kind + 1) * DH : (kind + 2) * DH, :].reshape(4 * DH, flat)


def gate_step(core, back, gate, ggated):
    def whole(shape):
        return pl.BlockSpec(shape, lambda t, core: (0,) * len(shape))

    flat = gate.shape[1]
    shapes = [(4, 4 * DH, flat), (C, flat), (12, 4 * DH, flat)]
    return pl.pallas_call(
        gate_kernel,
        grid_spec=pltpu.PrefetchScalarGridSpec(
            num_scalar_prefetch=1,
            grid=(1,),
            in_specs=[whole(back.shape), whole(gate.shape), whole(ggated.shape)],
            out_specs=[whole(s) for s in shapes],
        ),
        out_shape=[jax.ShapeDtypeStruct(s, BF) for s in shapes],
        compiler_params=params(20),
        cost_estimate=pl.CostEstimate(flops=6 * C * flat, bytes_accessed=6 * 2**20, transcendentals=0),
        name="gate",
    )(core, back, gate, ggated)


def input_grad_kernel(back_ref, ggate_ref, w_ref, act_ref, mean_ref, inv_ref, gain_ref, grad_ref, total_s):
    step = pl.program_id(0)
    flat = act_ref.shape[0]

    for kind in range(4):

        @pl.when(step == kind)
        def _(kind=kind):
            if kind == 3:
                total_s[...] += dot(w_ref[...], ggate_ref[...].reshape(C, flat))
            else:
                rows = back_ref[:, (kind + 1) * DH : (kind + 2) * DH, :].reshape(C, flat)
                part = dot(w_ref[...], rows)
                if kind == 0:
                    total_s[...] = part
                else:
                    total_s[...] += part

    @pl.when(step == 3)
    def _():
        normed = (act_ref[...].astype(F32) - mean_ref[...]) * inv_ref[...]
        grad_normed = total_s[...].T * gain_ref[...].reshape(1, C)
        grad_ref[...] = (
            inv_ref[...]
            * (
                grad_normed
                - jnp.mean(grad_normed, -1, keepdims=True)
                - normed * jnp.mean(grad_normed * normed, -1, keepdims=True)
            )
        ).astype(BF)


def input_grad(back, ggate, w_in, act, mean, inv_std, ln_gain):
    flat = act.shape[0]

    def whole(shape):
        return pl.BlockSpec(shape, lambda t: (0,) * len(shape))

    return pl.pallas_call(
        input_grad_kernel,
        grid=(4,),
        in_specs=[
            whole(back.shape),
            whole(ggate.shape),
            pl.BlockSpec((C, C), lambda t: (0, t)),
            whole((flat, C)),
            whole((flat, 1)),
            whole((flat, 1)),
            whole((C,)),
        ],
        out_specs=whole((flat, C)),
        out_shape=jax.ShapeDtypeStruct((flat, C), BF),
        scratch_shapes=[pltpu.VMEM((C, flat), F32)],
        compiler_params=params(60),
        cost_estimate=pl.CostEstimate(
            flops=2 * flat * C * 4 * C, bytes_accessed=8 * 2**20, transcendentals=0
        ),
        name="input_grad",
    )(back, ggate, w_in, act, mean, inv_std, ln_gain)


def weight_kernel(
    core_ref, back_ref, ggate_ref, o_ref, gated_ref, scaled_ref, dout_ref, wt_ref, gain_ref, out_ref, gated_s, sum_s
):
    core = core_ref[0]
    step = pl.program_id(0)
    flat = gated_ref.shape[1]
    last = pl.num_programs(0) - 1

    @pl.when(step == 0)
    def _():
        gated_s[:flat] = gated_ref[...].T
        gated_s[flat:] = o_ref[8:12].reshape(C, flat).T
        sum_s[...] = jnp.zeros_like(sum_s)

    for kind in range(4):

        @pl.when(step == kind)
        def _(kind=kind):
            blocks = [
                jnp.concatenate([head_rows(back_ref, ggate_ref, n, core), o_ref[n]], axis=1)
                for n in (2 * kind, 2 * kind + 1)
            ]
            win = dot(jnp.concatenate(blocks, axis=0), scaled_ref[...])
            wout = dot(dout_ref[2 * kind : 2 * kind + 2].reshape(128, 2 * flat), gated_s[...])
            weights = wt_ref[2 * kind : 2 * kind + 2].reshape(8 * DH, C).astype(F32)
            sum_s[...] += jnp.sum((win * weights).reshape(DH, 8, C), axis=0)
            for k in range(16):
                out_ref[kind * 16 + k] = jnp.concatenate(
                    [win[k * 24 : k * 24 + 24], wout[k * 8 : k * 8 + 8]], axis=0
                ).astype(BF)

    @pl.when(step == last)
    def _():
        gain = jnp.sum(sum_s[...], axis=0, keepdims=True) / gain_ref[...].reshape(1, C)
        gain_hi = gain.astype(BF).astype(F32)
        row = lax.broadcasted_iota(jnp.int32, (16, C), 0)
        extra = jnp.where(row == 14, gain_hi, gain - gain_hi).astype(BF)
        for k in range(64):
            out_ref[k, 16:] = jnp.where(row >= 14, extra, out_ref[k, 16:])


def weight_grads(core, operands):
    def whole(shape):
        return pl.BlockSpec(shape, lambda t, core: (0,) * len(shape))

    flat = operands[3].shape[1]
    return pl.pallas_call(
        weight_kernel,
        grid_spec=pltpu.PrefetchScalarGridSpec(
            num_scalar_prefetch=1,
            grid=(4,),
            in_specs=[whole(o.shape) for o in operands],
            out_specs=whole((64, 32, C)),
            scratch_shapes=[
                pltpu.VMEM((2 * flat, C), BF),
                pltpu.VMEM((8, C), F32),
            ],
        ),
        out_shape=jax.ShapeDtypeStruct((64, 32, C), BF),
        compiler_params=params(24),
        cost_estimate=pl.CostEstimate(
            flops=2 * 2 * flat * C * 2048, bytes_accessed=8 * 2**20, transcendentals=0
        ),
        name="weight_grads",
    )(core, *operands)


def per_device(act, pair_bias, ln_gain, w_in, w_out, d_out):
    sample_count, row_count, channels = act.shape
    flat = sample_count * row_count
    core = lax.axis_index("core")
    core_arg = jnp.full((1,), core, jnp.int32)
    own_x = lax.axis_index("x")
    place = jnp.stack([core, own_x]).astype(jnp.int32)
    zh = lax.axis_index("zh")

    bias = lax.dynamic_slice(pair_bias, (zh * 8, (own_x * 2 + core) * 16, 0), (8, 16, KEYS))
    bias = lax.all_to_all(bias, ("zl", "y"), 0, 0, tiled=True)

    rows_out = d_out.reshape(flat, channels)
    act = act.reshape(flat, channels)
    scaled, mean, inv_std, send, gate, ggated = front(
        act, ln_gain, w_in, w_out, rows_out
    )
    bias, send = lax.optimization_barrier((bias, send))
    pieces = [bias] + [lax.ppermute(bias, "x", turn(s)) for s in (1, 2, 3)]
    received = lax.all_to_all(send, PLANE, 0, 0, tiled=True)

    dout_t = jnp.pad(rows_out.T.reshape(128, 6, flat), ((0, 0), (0, 2), (0, 0)))
    dout_t = dout_t.reshape(8, 2, 64, flat)
    dout_mine = lax.dynamic_index_in_dim(dout_t, core, 1, keepdims=False)
    dout_send = lax.dynamic_index_in_dim(dout_t, 1 - core, 1, keepdims=False)
    scaled_other = lax.ppermute(scaled, "core", SWAP)

    pieces, dout_mine, dout_send = lax.optimization_barrier((pieces, dout_mine, dout_send))
    bias = jnp.stack(pieces)
    bias_other = lax.ppermute(bias, "core", SWAP)
    dout_other = lax.ppermute(dout_send, "core", SWAP)
    received, dout_other, scaled_other, bias_other = lax.optimization_barrier(
        (received, dout_other, scaled_other, bias_other)
    )
    result, keep, give = attention(place, received, bias, bias_other)
    back = lax.all_to_all(result, PLANE, 0, 0, tiled=True)

    keep, scaled, scaled_other, dout_mine, dout_other = lax.optimization_barrier(
        (keep, scaled, scaled_other, dout_mine, dout_other)
    )
    got = lax.ppermute(give, "core", SWAP)
    sums = [(keep[s].astype(F32) + got[s].astype(F32)).astype(BF) for s in range(4)]
    gb = sums[0].astype(F32)
    for s in (1, 2, 3):
        gb = gb + lax.ppermute(sums[s], "x", turn(s)).astype(F32)
    staged = stage(core_arg, w_in, scaled, scaled_other, dout_mine, dout_other)
    back, gb, staged = lax.optimization_barrier((back, gb.astype(BF), staged))
    gb = lax.all_to_all(gb, PLANE, 0, 0, tiled=True)

    ggate, gated, half = gate_step(core_arg, back, gate, ggated)
    other = lax.ppermute(half, "core", SWAP)
    chunks = weight_grads(
        core_arg,
        (back, ggate, other, gated, in_vmem(staged[1]), in_vmem(staged[2]), in_vmem(staged[0]), ln_gain),
    )
    chunks, gated, ggate, gb = lax.optimization_barrier((chunks, gated, ggate, gb))
    grad_act = input_grad(back, ggate, w_in, act, mean, inv_std, ln_gain)
    gb = gb.astype(F32)
    grad_bias = jnp.concatenate([gb[:, :, :64], gb[:, :, 64:]], axis=1)
    output = jnp.einsum("cr,cd->rd", gated, w_out, preferred_element_type=F32).astype(BF)
    chunks = lax.all_to_all(chunks, ("x", "zh", "zl", "y"), 0, 0, tiled=True)
    total = jnp.sum(chunks.astype(F32), axis=0)
    gain = total[30] + total[31]
    return (
        output.reshape(sample_count, row_count, channels),
        grad_act.reshape(sample_count, row_count, channels),
        grad_bias,
        gain + lax.ppermute(gain, "core", SWAP),
        total[:24].T,
        total[24:30].T,
    )


def solution(mesh):
    fine = Mesh(mesh.devices.reshape(4, 2, 2, 2, 4), ("x", "zh", "core", "zl", "y"))
    sample = ("x", "zh", "core")
    tok = ("zl", "y")
    return jax.shard_map(
        per_device,
        mesh=fine,
        in_specs=(
            P(sample, tok, None),
            P(None, tok, None),
            P(),
            P(),
            P(),
            P(sample, tok, None),
        ),
        out_specs=(
            P(sample, tok, None),
            P(sample, tok, None),
            P(None, tok, sample),
            P(),
            P(None, sample + tok),
            P(None, sample + tok),
        ),
        check_vma=False,
    )
```

```python
import functools
import math

import jax
import jax.numpy as jnp
from jax import lax
from jax.experimental import pallas as pl
from jax.experimental.pallas import tpu as pltpu
from jax.sharding import Mesh
from jax.sharding import PartitionSpec as P

EPS = 1e-05
LOG2E = math.log2(math.e)
BF = jnp.bfloat16
F32 = jnp.float32
C = 768
HEADS = 16
DH = 48
TOK = 128
KEYS = 1024
PLANE = ("zh", "zl", "y")
SWAP = [(0, 1), (1, 0)]
SCALE = 1.0 / math.sqrt(DH)
MIB = 1024 * 1024


def in_vmem(x):
    return pltpu.with_memory_space_constraint(x, pltpu.VMEM)


def dot(a, b):
    return jnp.dot(a, b, preferred_element_type=F32)


def dot_nt(a, b):
    return lax.dot_general(a, b, (((1,), (1,)), ((), ())), preferred_element_type=F32)


def turn(shift):
    return [(i, (i + shift) % 4) for i in range(4)]


def params(mib=20):
    return pltpu.CompilerParams(vmem_limit_bytes=mib * MIB)


def front_kernel(
    act_ref, gain_ref, w_ref, wout_ref, dout_ref, scaled_ref, mean_ref, inv_ref, send_ref, gate_ref, gg_ref
):
    step = pl.program_id(0)
    flat = act_ref.shape[0]

    @pl.when(step == 0)
    def _():
        values = act_ref[...].astype(F32)
        center = jnp.mean(values, -1, keepdims=True)
        shifted = values - center
        spread = jnp.mean(shifted * shifted, -1, keepdims=True)
        inv_std = lax.rsqrt(spread + EPS)
        mean_ref[...] = center
        inv_ref[...] = inv_std
        scaled_ref[...] = (shifted * inv_std * gain_ref[...].reshape(1, C)).astype(BF)

    block = dot(scaled_ref[...], w_ref[...])
    rows = pl.ds(pl.multiple_of(step * 4 * DH, 4 * DH), 4 * DH)
    gg_ref[rows, :] = dot_nt(wout_ref[...], dout_ref[...]).astype(BF)

    @pl.when(step < 3)
    def _():
        send_ref[...] = block.astype(BF).T.reshape(HEADS, DH, flat)

    @pl.when(step == 3)
    def _():
        gate = jax.nn.sigmoid(block.T)
        gate_ref[...] = gate
        send_ref[...] = (gg_ref[...].astype(F32) * gate).astype(BF).reshape(HEADS, DH, flat)


def front(act, ln_gain, w_in, w_out, d_out):
    flat = act.shape[0]

    def whole(shape):
        return pl.BlockSpec(shape, lambda t: (0,) * len(shape))

    outs = [
        ((flat, C), BF, whole((flat, C))),
        ((flat, 1), F32, whole((flat, 1))),
        ((flat, 1), F32, whole((flat, 1))),
        ((HEADS, 4 * DH, flat), BF, pl.BlockSpec((HEADS, DH, flat), lambda t: (0, t, 0))),
        ((C, flat), F32, whole((C, flat))),
        ((C, flat), BF, whole((C, flat))),
    ]
    return pl.pallas_call(
        front_kernel,
        grid=(4,),
        in_specs=[
            whole((flat, C)),
            whole((C,)),
            pl.BlockSpec((C, C), lambda t: (0, t)),
            pl.BlockSpec((4 * DH, C), lambda t: (t, 0)),
            whole((flat, C)),
        ],
        out_specs=[spec for _, _, spec in outs],
        out_shape=[jax.ShapeDtypeStruct(shape, kind) for shape, kind, _ in outs],
        compiler_params=params(60),
        cost_estimate=pl.CostEstimate(
            flops=2 * flat * C * 5 * C, bytes_accessed=11 * 2**20, transcendentals=flat * C
        ),
        name="front",
    )(act, ln_gain, w_in, w_out, d_out)


def attention_kernel(
    place_ref, x_ref, mine_ref, other_ref, out_ref, keep_ref, give_ref,
    qa_s, ka_s, va_s, vt_s, kn_s, gn_s, gb_s, bias_s, *, blocks,
):
    core = place_ref[0]
    own_x = place_ref[1]
    sample = pl.program_id(0)

    @pl.when(sample == 0)
    def _():
        for t in range(8):
            pieces = []
            for x in range(4):
                mine = mine_ref[(own_x - x + 4) % 4, t]
                other = other_ref[(own_x - x + 4) % 4, t]
                pieces += [jnp.where(core == 0, mine, other), jnp.where(core == 0, other, mine)]
            gb_s[t * TOK : (t + 1) * TOK] = jnp.zeros((TOK, KEYS), F32)
            bias_s[t * TOK : (t + 1) * TOK] = jnp.concatenate(pieces, axis=0).astype(F32) * LOG2E

    whole = jnp.concatenate([x_ref[t] for t in range(8)], axis=1)
    qt, kt, vt, gt = (whole[i * DH : (i + 1) * DH] for i in range(4))
    qs = qt.astype(F32) * (SCALE * LOG2E)
    q_hi = qs.astype(BF)
    q_lo = (qs - q_hi.astype(F32)).astype(BF)
    zeros32 = jnp.zeros((32, KEYS), BF)
    zeros64 = jnp.zeros((64, KEYS), BF)
    zeros80 = jnp.zeros((80, KEYS), BF)
    ones16 = jnp.ones((16, KEYS), BF)
    qa_s[...] = jnp.concatenate([q_hi, q_lo, zeros32], axis=0).T
    ka_s[...] = jnp.concatenate([kt, kt, zeros32], axis=0)
    v_one = jnp.concatenate([vt, ones16, zeros64], axis=0)
    va_s[...] = v_one
    vt_s[...] = v_one.T
    kn_s[...] = jnp.concatenate([kt, zeros80], axis=0).T
    gn_s[...] = jnp.concatenate([gt, zeros80], axis=0).T

    rows = KEYS // blocks
    every = [slice(i * rows, (i + 1) * rows) for i in range(blocks)]
    lane = lax.broadcasted_iota(jnp.int32, (rows, 128), 1)
    scores = [dot(qa_s[p], ka_s[...]) + bias_s[p] for p in every]
    expd = [jnp.exp2(s - jnp.max(s, axis=1, keepdims=True)) for s in scores]
    expd_low = [e.astype(BF) for e in expd]
    summed = [dot(e, vt_s[...]) for e in expd_low]
    inv = [1.0 / s[:, DH : DH + 1] for s in summed]
    out = [s * i for s, i in zip(summed, inv)]
    gscaled = [(gn_s[p].astype(F32) * i).astype(BF).astype(F32) for p, i in zip(every, inv)]
    left = []
    for o, g in zip(out, gscaled):
        delta = jnp.sum(o * g, axis=1, keepdims=True)
        high = delta.astype(BF).astype(F32)
        middle = (delta - high).astype(BF).astype(F32)
        low = delta - high - middle
        tail = jnp.where(lane == DH, high, jnp.where(lane == DH + 1, middle, low))
        left.append(jnp.where((lane >= DH) & (lane <= DH + 2), -tail, g).astype(BF))
    dscores = [e * dot(l, va_s[...]) for e, l in zip(expd, left)]
    dscores_low = [d.astype(BF) for d in dscores]

    for p, d in zip(every, dscores):
        gb_s[p] = gb_s[p] + d

    @pl.when(sample == 3)
    def _():
        for p, d in zip(every, dscores):
            total = gb_s[p].astype(BF)
            for t in range(rows // TOK):
                for n in range(8):
                    tile = total[t * TOK : (t + 1) * TOK, n * TOK : (n + 1) * TOK]
                    low = jnp.concatenate([tile[:64, :64], tile[64:, :64]], axis=1)
                    high = jnp.concatenate([tile[:64, 64:], tile[64:, 64:]], axis=1)
                    where = (n % 2) * 8 + p.start // TOK + t
                    ahead = (n // 2 - own_x + 4) % 4
                    keep_ref[ahead, where] = jnp.where(core == 0, low, high)
                    give_ref[ahead, where] = jnp.where(core == 0, high, low)

    all_low = jnp.concatenate(dscores_low, axis=0)
    gscaled_t = jnp.concatenate(gscaled, axis=0).T.astype(BF)
    out_t = jnp.concatenate(out, axis=0).T[:DH].astype(BF)
    dquery_t = (dot(all_low, kn_s[...]) * SCALE).T[:DH].astype(BF)
    dkey_t = (dot(qt, all_low) * SCALE).astype(BF)
    dvalue_t = dot(gscaled_t[:DH], jnp.concatenate(expd_low, axis=0)).astype(BF)
    for t in range(8):
        cols = slice(t * TOK, (t + 1) * TOK)
        for i, part in enumerate((out_t, dquery_t, dkey_t, dvalue_t)):
            out_ref[t, i * DH : (i + 1) * DH, :] = part[:, cols]


def attention(place, x, mine, other, blocks=4):
    def whole(shape):
        return pl.BlockSpec(shape, lambda s, place: (0,) * len(shape))

    one = pl.BlockSpec((8, 4 * DH, TOK), lambda s, place: (s // 2, 0, s % 2))
    half_sum = (4, HEADS, 64, 128)
    return pl.pallas_call(
        functools.partial(attention_kernel, blocks=blocks),
        grid_spec=pltpu.PrefetchScalarGridSpec(
            num_scalar_prefetch=1,
            grid=(4,),
            in_specs=[one, whole(mine.shape), whole(other.shape)],
            out_specs=[one, whole(half_sum), whole(half_sum)],
            scratch_shapes=[
                pltpu.VMEM((KEYS, 128), BF),
                pltpu.VMEM((128, KEYS), BF),
                pltpu.VMEM((128, KEYS), BF),
                pltpu.VMEM((KEYS, 128), BF),
                pltpu.VMEM((KEYS, 128), BF),
                pltpu.VMEM((KEYS, 128), BF),
                pltpu.VMEM((KEYS, KEYS), F32),
                pltpu.VMEM((KEYS, KEYS), F32),
            ],
        ),
        out_shape=[
            jax.ShapeDtypeStruct(x.shape, BF),
            jax.ShapeDtypeStruct(half_sum, BF),
            jax.ShapeDtypeStruct(half_sum, BF),
        ],
        compiler_params=params(60),
        cost_estimate=pl.CostEstimate(
            flops=4 * 6 * 2 * KEYS * KEYS * 256, bytes_accessed=8 * 2**20, transcendentals=4 * KEYS * KEYS
        ),
        name="attention",
    )(place, x, mine, other)


def stage_kernel(core_ref, w_ref, sc_ref, sco_ref, do_ref, doo_ref, wt_ref, scaled_ref, dout_ref, turned_s):
    n = pl.program_id(0)
    flat = sc_ref.shape[0]

    @pl.when(n == 0)
    def _():
        scaled_ref[:flat] = sc_ref[...]
        scaled_ref[flat:] = sco_ref[...]
        dout_ref[:, :, :flat] = do_ref[...]
        dout_ref[:, :, flat:] = doo_ref[...]

    turned_s[...] = w_ref[...].T
    wt_ref[n] = turned_s[pl.ds(pl.multiple_of(core_ref[0] * 4 * DH, 4 * DH), 4 * DH), :]


def stage(core, w_in, *early):
    def whole(shape):
        return pl.BlockSpec(shape, lambda t, core: (0,) * len(shape))

    flat = early[0].shape[0]
    shapes = [(8, 4 * DH, C), (2 * flat, C), (8, 64, 2 * flat)]
    return pl.pallas_call(
        stage_kernel,
        grid_spec=pltpu.PrefetchScalarGridSpec(
            num_scalar_prefetch=1,
            grid=(8,),
            in_specs=[pl.BlockSpec((C, 8 * DH), lambda n, core: (0, n))] + [whole(e.shape) for e in early],
            out_specs=[whole(s) for s in shapes],
            scratch_shapes=[pltpu.VMEM((8 * DH, C), BF)],
        ),
        out_shape=[pltpu.VMEM(s, BF) for s in shapes],
        compiler_params=params(24),
        cost_estimate=pl.CostEstimate(flops=8 * C * C, bytes_accessed=7 * 2**20, transcendentals=0),
        name="stage",
    )(core, w_in, *early)


def gate_kernel(core_ref, back_ref, gate_ref, gg_ref, ggate_ref, gated_ref, send_ref):
    other = 1 - core_ref[0]
    flat = gate_ref.shape[1]
    att = back_ref[:, :DH, :].astype(F32).reshape(C, flat)
    gate = gate_ref[...]
    opened = att * gate
    gated = opened.astype(BF)
    gated_ref[...] = gated
    for q in range(4):
        send_ref[8 + q] = gated[q * 192 : (q + 1) * 192]
    ggate_ref[...] = (gg_ref[...].astype(F32) * opened * (1.0 - gate)).astype(BF).reshape(4, 4 * DH, flat)
    for n in range(8):
        send_ref[n] = head_rows(back_ref, ggate_ref, n, other)


def head_rows(back_ref, ggate_ref, n, core):
    kind = n // 2
    group = (n % 2) * 2 + core
    if kind == 3:
        return ggate_ref[group]
    flat = back_ref.shape[2]
    return back_ref[pl.ds(group * 4, 4), (kind + 1) * DH : (kind + 2) * DH, :].reshape(4 * DH, flat)


def gate_step(core, back, gate, ggated):
    def whole(shape):
        return pl.BlockSpec(shape, lambda t, core: (0,) * len(shape))

    flat = gate.shape[1]
    shapes = [(4, 4 * DH, flat), (C, flat), (12, 4 * DH, flat)]
    return pl.pallas_call(
        gate_kernel,
        grid_spec=pltpu.PrefetchScalarGridSpec(
            num_scalar_prefetch=1,
            grid=(1,),
            in_specs=[whole(back.shape), whole(gate.shape), whole(ggated.shape)],
            out_specs=[whole(s) for s in shapes],
        ),
        out_shape=[jax.ShapeDtypeStruct(s, BF) for s in shapes],
        compiler_params=params(20),
        cost_estimate=pl.CostEstimate(flops=6 * C * flat, bytes_accessed=6 * 2**20, transcendentals=0),
        name="gate",
    )(core, back, gate, ggated)


def input_grad_kernel(back_ref, ggate_ref, w_ref, act_ref, mean_ref, inv_ref, gain_ref, grad_ref, total_s):
    step = pl.program_id(0)
    flat = act_ref.shape[0]

    for kind in range(4):

        @pl.when(step == kind)
        def _(kind=kind):
            if kind == 3:
                total_s[...] += dot(w_ref[...], ggate_ref[...].reshape(C, flat))
            else:
                rows = back_ref[:, (kind + 1) * DH : (kind + 2) * DH, :].reshape(C, flat)
                part = dot(w_ref[...], rows)
                if kind == 0:
                    total_s[...] = part
                else:
                    total_s[...] += part

    @pl.when(step == 3)
    def _():
        normed = (act_ref[...].astype(F32) - mean_ref[...]) * inv_ref[...]
        grad_normed = total_s[...].T * gain_ref[...].reshape(1, C)
        grad_ref[...] = (
            inv_ref[...]
            * (
                grad_normed
                - jnp.mean(grad_normed, -1, keepdims=True)
                - normed * jnp.mean(grad_normed * normed, -1, keepdims=True)
            )
        ).astype(BF)


def input_grad(back, ggate, w_in, act, mean, inv_std, ln_gain):
    flat = act.shape[0]

    def whole(shape):
        return pl.BlockSpec(shape, lambda t: (0,) * len(shape))

    return pl.pallas_call(
        input_grad_kernel,
        grid=(4,),
        in_specs=[
            whole(back.shape),
            whole(ggate.shape),
            pl.BlockSpec((C, C), lambda t: (0, t)),
            whole((flat, C)),
            whole((flat, 1)),
            whole((flat, 1)),
            whole((C,)),
        ],
        out_specs=whole((flat, C)),
        out_shape=jax.ShapeDtypeStruct((flat, C), BF),
        scratch_shapes=[pltpu.VMEM((C, flat), F32)],
        compiler_params=params(60),
        cost_estimate=pl.CostEstimate(
            flops=2 * flat * C * 4 * C, bytes_accessed=8 * 2**20, transcendentals=0
        ),
        name="input_grad",
    )(back, ggate, w_in, act, mean, inv_std, ln_gain)


def weight_kernel(
    core_ref, back_ref, ggate_ref, o_ref, gated_ref, scaled_ref, dout_ref, wt_ref, gain_ref, out_ref, gated_s
):
    core = core_ref[0]
    flat = gated_ref.shape[1]
    gated_s[:flat] = gated_ref[...].T
    gated_s[flat:] = o_ref[8:12].reshape(C, flat).T
    sums = jnp.zeros((8, C), F32)
    for kind in range(4):
        blocks = [
            jnp.concatenate([head_rows(back_ref, ggate_ref, n, core), o_ref[n]], axis=1)
            for n in (2 * kind, 2 * kind + 1)
        ]
        win = dot(jnp.concatenate(blocks, axis=0), scaled_ref[...])
        wout = dot(dout_ref[2 * kind : 2 * kind + 2].reshape(128, 2 * flat), gated_s[...])
        weights = wt_ref[2 * kind : 2 * kind + 2].reshape(8 * DH, C).astype(F32)
        sums = sums + jnp.sum((win * weights).reshape(DH, 8, C), axis=0)
        for k in range(16):
            out_ref[kind * 16 + k] = jnp.concatenate(
                [win[k * 24 : k * 24 + 24], wout[k * 8 : k * 8 + 8]], axis=0
            ).astype(BF)
    gain = jnp.sum(sums, axis=0, keepdims=True) / gain_ref[...].reshape(1, C)
    gain_hi = gain.astype(BF).astype(F32)
    row = lax.broadcasted_iota(jnp.int32, (16, C), 0)
    extra = jnp.where(row == 14, gain_hi, gain - gain_hi).astype(BF)
    for k in range(64):
        out_ref[k, 16:] = jnp.where(row >= 14, extra, out_ref[k, 16:])


def weight_grads(core, operands):
    def whole(shape):
        return pl.BlockSpec(shape, lambda t, core: (0,) * len(shape))

    flat = operands[3].shape[1]
    return pl.pallas_call(
        weight_kernel,
        grid_spec=pltpu.PrefetchScalarGridSpec(
            num_scalar_prefetch=1,
            grid=(1,),
            in_specs=[whole(o.shape) for o in operands],
            out_specs=whole((64, 32, C)),
            scratch_shapes=[pltpu.VMEM((2 * flat, C), BF)],
        ),
        out_shape=jax.ShapeDtypeStruct((64, 32, C), BF),
        compiler_params=params(24),
        cost_estimate=pl.CostEstimate(
            flops=2 * 2 * flat * C * 2048, bytes_accessed=8 * 2**20, transcendentals=0
        ),
        name="weight_grads",
    )(core, *operands)


def per_device(act, pair_bias, ln_gain, w_in, w_out, d_out):
    sample_count, row_count, channels = act.shape
    flat = sample_count * row_count
    core = lax.axis_index("core")
    core_arg = jnp.full((1,), core, jnp.int32)
    own_x = lax.axis_index("x")
    place = jnp.stack([core, own_x]).astype(jnp.int32)
    zh = lax.axis_index("zh")

    bias = lax.dynamic_slice(pair_bias, (zh * 8, (own_x * 2 + core) * 16, 0), (8, 16, KEYS))
    bias = lax.all_to_all(bias, ("zl", "y"), 0, 0, tiled=True)

    rows_out = d_out.reshape(flat, channels)
    act = act.reshape(flat, channels)
    scaled, mean, inv_std, send, gate, ggated = front(
        act, ln_gain, w_in, w_out, rows_out
    )
    bias, send = lax.optimization_barrier((bias, send))
    pieces = [bias] + [lax.ppermute(bias, "x", turn(s)) for s in (1, 2, 3)]
    received = lax.all_to_all(send, PLANE, 0, 0, tiled=True)

    dout_t = jnp.pad(rows_out.T.reshape(128, 6, flat), ((0, 0), (0, 2), (0, 0)))
    dout_t = dout_t.reshape(8, 2, 64, flat)
    dout_mine = lax.dynamic_index_in_dim(dout_t, core, 1, keepdims=False)
    dout_send = lax.dynamic_index_in_dim(dout_t, 1 - core, 1, keepdims=False)
    scaled_other = lax.ppermute(scaled, "core", SWAP)

    pieces, dout_mine, dout_send = lax.optimization_barrier((pieces, dout_mine, dout_send))
    bias = jnp.stack(pieces)
    bias_other = lax.ppermute(bias, "core", SWAP)
    dout_other = lax.ppermute(dout_send, "core", SWAP)
    received, dout_other, scaled_other, bias_other = lax.optimization_barrier(
        (received, dout_other, scaled_other, bias_other)
    )
    result, keep, give = attention(place, received, bias, bias_other)
    back = lax.all_to_all(result, PLANE, 0, 0, tiled=True)

    keep, scaled, scaled_other, dout_mine, dout_other = lax.optimization_barrier(
        (keep, scaled, scaled_other, dout_mine, dout_other)
    )
    got = lax.ppermute(give, "core", SWAP)
    sums = [(keep[s].astype(F32) + got[s].astype(F32)).astype(BF) for s in range(4)]
    gb = sums[0].astype(F32)
    for s in (1, 2, 3):
        gb = gb + lax.ppermute(sums[s], "x", turn(s)).astype(F32)
    staged = stage(core_arg, w_in, scaled, scaled_other, dout_mine, dout_other)
    back, gb, staged = lax.optimization_barrier((back, gb.astype(BF), staged))
    gb = lax.all_to_all(gb, PLANE, 0, 0, tiled=True)

    ggate, gated, half = gate_step(core_arg, back, gate, ggated)
    other = lax.ppermute(half, "core", SWAP)
    chunks = weight_grads(
        core_arg,
        (back, ggate, other, gated, in_vmem(staged[1]), in_vmem(staged[2]), in_vmem(staged[0]), ln_gain),
    )
    chunks, gated, ggate, gb = lax.optimization_barrier((chunks, gated, ggate, gb))
    grad_act = input_grad(back, ggate, w_in, act, mean, inv_std, ln_gain)
    gb = gb.astype(F32)
    grad_bias = jnp.concatenate([gb[:, :, :64], gb[:, :, 64:]], axis=1)
    output = jnp.einsum("cr,cd->rd", gated, w_out, preferred_element_type=F32).astype(BF)
    chunks = lax.all_to_all(chunks, ("x", "zh", "zl", "y"), 0, 0, tiled=True)
    total = jnp.sum(chunks.astype(F32), axis=0)
    gain = total[30] + total[31]
    return (
        output.reshape(sample_count, row_count, channels),
        grad_act.reshape(sample_count, row_count, channels),
        grad_bias,
        gain + lax.ppermute(gain, "core", SWAP),
        total[:24].T,
        total[24:30].T,
    )


def solution(mesh):
    fine = Mesh(mesh.devices.reshape(4, 2, 2, 2, 4), ("x", "zh", "core", "zl", "y"))
    sample = ("x", "zh", "core")
    tok = ("zl", "y")
    return jax.shard_map(
        per_device,
        mesh=fine,
        in_specs=(
            P(sample, tok, None),
            P(None, tok, None),
            P(),
            P(),
            P(),
            P(sample, tok, None),
        ),
        out_specs=(
            P(sample, tok, None),
            P(sample, tok, None),
            P(None, tok, sample),
            P(),
            P(None, sample + tok),
            P(None, sample + tok),
        ),
        check_vma=False,
    )
```

```python
import functools
import math

import jax
import jax.numpy as jnp
from jax import lax
from jax.experimental import pallas as pl
from jax.experimental.pallas import tpu as pltpu
from jax.sharding import Mesh
from jax.sharding import PartitionSpec as P

EPS = 1e-05
LOG2E = math.log2(math.e)
BF = jnp.bfloat16
F32 = jnp.float32
C = 768
HEADS = 16
DH = 48
TOK = 128
KEYS = 1024
PLANE = ("zh", "zl", "y")
SWAP = [(0, 1), (1, 0)]
SCALE = 1.0 / math.sqrt(DH)
MIB = 1024 * 1024


def in_vmem(x):
    return pltpu.with_memory_space_constraint(x, pltpu.VMEM)


def dot(a, b):
    return jnp.dot(a, b, preferred_element_type=F32)


def dot_nt(a, b):
    return lax.dot_general(a, b, (((1,), (1,)), ((), ())), preferred_element_type=F32)


def turn(shift):
    return [(i, (i + shift) % 4) for i in range(4)]


def params(mib=20):
    return pltpu.CompilerParams(vmem_limit_bytes=mib * MIB)


def front_kernel(
    act_ref, gain_ref, w_ref, wout_ref, dout_ref, scaled_ref, mean_ref, inv_ref, send_ref, gate_ref, gg_ref
):
    step = pl.program_id(0)
    flat = act_ref.shape[0]

    @pl.when(step == 0)
    def _():
        values = act_ref[...].astype(F32)
        center = jnp.mean(values, -1, keepdims=True)
        shifted = values - center
        spread = jnp.mean(shifted * shifted, -1, keepdims=True)
        inv_std = lax.rsqrt(spread + EPS)
        mean_ref[...] = center
        inv_ref[...] = inv_std
        scaled_ref[...] = (shifted * inv_std * gain_ref[...].reshape(1, C)).astype(BF)

    block = dot(scaled_ref[...], w_ref[...])
    rows = pl.ds(pl.multiple_of(step * 4 * DH, 4 * DH), 4 * DH)
    gg_ref[rows, :] = dot_nt(wout_ref[...], dout_ref[...]).astype(BF)

    @pl.when(step < 3)
    def _():
        send_ref[...] = block.astype(BF).T.reshape(HEADS, DH, flat)

    @pl.when(step == 3)
    def _():
        gate = jax.nn.sigmoid(block.T)
        gate_ref[...] = gate
        send_ref[...] = (gg_ref[...].astype(F32) * gate).astype(BF).reshape(HEADS, DH, flat)


def front(act, ln_gain, w_in, w_out, d_out):
    flat = act.shape[0]

    def whole(shape):
        return pl.BlockSpec(shape, lambda t: (0,) * len(shape))

    outs = [
        ((flat, C), BF, whole((flat, C))),
        ((flat, 1), F32, whole((flat, 1))),
        ((flat, 1), F32, whole((flat, 1))),
        ((HEADS, 4 * DH, flat), BF, pl.BlockSpec((HEADS, DH, flat), lambda t: (0, t, 0))),
        ((C, flat), F32, whole((C, flat))),
        ((C, flat), BF, whole((C, flat))),
    ]
    return pl.pallas_call(
        front_kernel,
        grid=(4,),
        in_specs=[
            whole((flat, C)),
            whole((C,)),
            pl.BlockSpec((C, C), lambda t: (0, t)),
            pl.BlockSpec((4 * DH, C), lambda t: (t, 0)),
            whole((flat, C)),
        ],
        out_specs=[spec for _, _, spec in outs],
        out_shape=[jax.ShapeDtypeStruct(shape, kind) for shape, kind, _ in outs],
        compiler_params=params(60),
        cost_estimate=pl.CostEstimate(
            flops=2 * flat * C * 5 * C, bytes_accessed=11 * 2**20, transcendentals=flat * C
        ),
        name="front",
    )(act, ln_gain, w_in, w_out, d_out)


def attention_kernel(
    place_ref, x_ref, mine_ref, other_ref, out_ref, keep_ref, give_ref,
    qa_s, ka_s, va_s, vt_s, kn_s, gn_s, gb_s, bias_s, *, blocks,
):
    core = place_ref[0]
    own_x = place_ref[1]
    sample = pl.program_id(0)

    @pl.when(sample == 0)
    def _():
        for t in range(8):
            pieces = []
            for x in range(4):
                mine = mine_ref[(own_x - x + 4) % 4, t]
                other = other_ref[(own_x - x + 4) % 4, t]
                pieces += [jnp.where(core == 0, mine, other), jnp.where(core == 0, other, mine)]
            gb_s[t * TOK : (t + 1) * TOK] = jnp.zeros((TOK, KEYS), F32)
            bias_s[t * TOK : (t + 1) * TOK] = jnp.concatenate(pieces, axis=0).astype(F32) * LOG2E

    whole = jnp.concatenate([x_ref[t] for t in range(8)], axis=1)
    qt, kt, vt, gt = (whole[i * DH : (i + 1) * DH] for i in range(4))
    qs = qt.astype(F32) * (SCALE * LOG2E)
    q_hi = qs.astype(BF)
    q_lo = (qs - q_hi.astype(F32)).astype(BF)
    zeros32 = jnp.zeros((32, KEYS), BF)
    zeros64 = jnp.zeros((64, KEYS), BF)
    zeros80 = jnp.zeros((80, KEYS), BF)
    ones16 = jnp.ones((16, KEYS), BF)
    qa_s[...] = jnp.concatenate([q_hi, q_lo, zeros32], axis=0).T
    ka_s[...] = jnp.concatenate([kt, kt, zeros32], axis=0)
    v_one = jnp.concatenate([vt, ones16, zeros64], axis=0)
    va_s[...] = v_one
    vt_s[...] = v_one.T
    kn_s[...] = jnp.concatenate([kt, zeros80], axis=0).T
    gn_s[...] = jnp.concatenate([gt, zeros80], axis=0).T

    rows = KEYS // blocks
    every = [slice(i * rows, (i + 1) * rows) for i in range(blocks)]
    lane = lax.broadcasted_iota(jnp.int32, (rows, 128), 1)
    scores = [dot(qa_s[p], ka_s[...]) + bias_s[p] for p in every]
    expd = [jnp.exp2(s - jnp.max(s, axis=1, keepdims=True)) for s in scores]
    expd_low = [e.astype(BF) for e in expd]
    summed = [dot(e, vt_s[...]) for e in expd_low]
    inv = [1.0 / s[:, DH : DH + 1] for s in summed]
    out = [s * i for s, i in zip(summed, inv)]
    gscaled = [(gn_s[p].astype(F32) * i).astype(BF).astype(F32) for p, i in zip(every, inv)]
    left = []
    for o, g in zip(out, gscaled):
        delta = jnp.sum(o * g, axis=1, keepdims=True)
        high = delta.astype(BF).astype(F32)
        middle = (delta - high).astype(BF).astype(F32)
        low = delta - high - middle
        tail = jnp.where(lane == DH, high, jnp.where(lane == DH + 1, middle, low))
        left.append(jnp.where((lane >= DH) & (lane <= DH + 2), -tail, g).astype(BF))
    dscores = [e * dot(l, va_s[...]) for e, l in zip(expd, left)]
    dscores_low = [d.astype(BF) for d in dscores]

    for p, d in zip(every, dscores):
        gb_s[p] = gb_s[p] + d

    @pl.when(sample == 3)
    def _():
        for p, d in zip(every, dscores):
            total = gb_s[p].astype(BF)
            for t in range(rows // TOK):
                for n in range(8):
                    tile = total[t * TOK : (t + 1) * TOK, n * TOK : (n + 1) * TOK]
                    low = jnp.concatenate([tile[:64, :64], tile[64:, :64]], axis=1)
                    high = jnp.concatenate([tile[:64, 64:], tile[64:, 64:]], axis=1)
                    where = (n % 2) * 8 + p.start // TOK + t
                    ahead = (n // 2 - own_x + 4) % 4
                    keep_ref[ahead, where] = jnp.where(core == 0, low, high)
                    give_ref[ahead, where] = jnp.where(core == 0, high, low)

    all_low = jnp.concatenate(dscores_low, axis=0)
    gscaled_t = jnp.concatenate(gscaled, axis=0).T.astype(BF)
    out_t = jnp.concatenate(out, axis=0).T[:DH].astype(BF)
    dquery_t = (dot(all_low, kn_s[...]) * SCALE).T[:DH].astype(BF)
    dkey_t = (dot(qt, all_low) * SCALE).astype(BF)
    dvalue_t = dot(gscaled_t[:DH], jnp.concatenate(expd_low, axis=0)).astype(BF)
    for t in range(8):
        cols = slice(t * TOK, (t + 1) * TOK)
        for i, part in enumerate((out_t, dquery_t, dkey_t, dvalue_t)):
            out_ref[t, i * DH : (i + 1) * DH, :] = part[:, cols]


def attention(place, x, mine, other, blocks=4):
    def whole(shape):
        return pl.BlockSpec(shape, lambda s, place: (0,) * len(shape))

    one = pl.BlockSpec((8, 4 * DH, TOK), lambda s, place: (s // 2, 0, s % 2))
    half_sum = (4, HEADS, 64, 128)
    return pl.pallas_call(
        functools.partial(attention_kernel, blocks=blocks),
        grid_spec=pltpu.PrefetchScalarGridSpec(
            num_scalar_prefetch=1,
            grid=(4,),
            in_specs=[one, whole(mine.shape), whole(other.shape)],
            out_specs=[one, whole(half_sum), whole(half_sum)],
            scratch_shapes=[
                pltpu.VMEM((KEYS, 128), BF),
                pltpu.VMEM((128, KEYS), BF),
                pltpu.VMEM((128, KEYS), BF),
                pltpu.VMEM((KEYS, 128), BF),
                pltpu.VMEM((KEYS, 128), BF),
                pltpu.VMEM((KEYS, 128), BF),
                pltpu.VMEM((KEYS, KEYS), F32),
                pltpu.VMEM((KEYS, KEYS), F32),
            ],
        ),
        out_shape=[
            jax.ShapeDtypeStruct(x.shape, BF),
            jax.ShapeDtypeStruct(half_sum, BF),
            jax.ShapeDtypeStruct(half_sum, BF),
        ],
        compiler_params=params(60),
        cost_estimate=pl.CostEstimate(
            flops=4 * 6 * 2 * KEYS * KEYS * 256, bytes_accessed=8 * 2**20, transcendentals=4 * KEYS * KEYS
        ),
        name="attention",
    )(place, x, mine, other)


def stage_kernel(core_ref, w_ref, sc_ref, sco_ref, do_ref, doo_ref, wt_ref, scaled_ref, dout_ref, turned_s):
    n = pl.program_id(0)
    flat = sc_ref.shape[0]

    @pl.when(n == 0)
    def _():
        scaled_ref[:flat] = sc_ref[...]
        scaled_ref[flat:] = sco_ref[...]
        dout_ref[:, :, :flat] = do_ref[...]
        dout_ref[:, :, flat:] = doo_ref[...]

    turned_s[...] = w_ref[...].T
    wt_ref[n] = turned_s[pl.ds(pl.multiple_of(core_ref[0] * 4 * DH, 4 * DH), 4 * DH), :]


def stage(core, w_in, *early):
    def whole(shape):
        return pl.BlockSpec(shape, lambda t, core: (0,) * len(shape))

    flat = early[0].shape[0]
    shapes = [(8, 4 * DH, C), (2 * flat, C), (8, 64, 2 * flat)]
    return pl.pallas_call(
        stage_kernel,
        grid_spec=pltpu.PrefetchScalarGridSpec(
            num_scalar_prefetch=1,
            grid=(8,),
            in_specs=[pl.BlockSpec((C, 8 * DH), lambda n, core: (0, n))] + [whole(e.shape) for e in early],
            out_specs=[whole(s) for s in shapes],
            scratch_shapes=[pltpu.VMEM((8 * DH, C), BF)],
        ),
        out_shape=[pltpu.VMEM(s, BF) for s in shapes],
        compiler_params=params(24),
        cost_estimate=pl.CostEstimate(flops=8 * C * C, bytes_accessed=7 * 2**20, transcendentals=0),
        name="stage",
    )(core, w_in, *early)


def gate_kernel(core_ref, back_ref, gate_ref, gg_ref, ggate_ref, gated_ref, send_ref):
    other = 1 - core_ref[0]
    flat = gate_ref.shape[1]
    att = back_ref[:, :DH, :].astype(F32).reshape(C, flat)
    gate = gate_ref[...]
    opened = att * gate
    gated = opened.astype(BF)
    gated_ref[...] = gated
    for q in range(4):
        send_ref[8 + q] = gated[q * 192 : (q + 1) * 192]
    ggate_ref[...] = (gg_ref[...].astype(F32) * opened * (1.0 - gate)).astype(BF).reshape(4, 4 * DH, flat)
    for n in range(8):
        send_ref[n] = head_rows(back_ref, ggate_ref, n, other)


def head_rows(back_ref, ggate_ref, n, core):
    kind = n // 2
    group = (n % 2) * 2 + core
    if kind == 3:
        return ggate_ref[group]
    flat = back_ref.shape[2]
    return back_ref[pl.ds(group * 4, 4), (kind + 1) * DH : (kind + 2) * DH, :].reshape(4 * DH, flat)


def gate_step(core, back, gate, ggated):
    def whole(shape):
        return pl.BlockSpec(shape, lambda t, core: (0,) * len(shape))

    flat = gate.shape[1]
    shapes = [(4, 4 * DH, flat), (C, flat), (12, 4 * DH, flat)]
    return pl.pallas_call(
        gate_kernel,
        grid_spec=pltpu.PrefetchScalarGridSpec(
            num_scalar_prefetch=1,
            grid=(1,),
            in_specs=[whole(back.shape), whole(gate.shape), whole(ggated.shape)],
            out_specs=[whole(s) for s in shapes],
        ),
        out_shape=[jax.ShapeDtypeStruct(s, BF) for s in shapes],
        compiler_params=params(20),
        cost_estimate=pl.CostEstimate(flops=6 * C * flat, bytes_accessed=6 * 2**20, transcendentals=0),
        name="gate",
    )(core, back, gate, ggated)


def input_grad_kernel(back_ref, ggate_ref, w_ref, act_ref, mean_ref, inv_ref, gain_ref, grad_ref, total_s):
    step = pl.program_id(0)
    flat = act_ref.shape[0]

    for kind in range(4):

        @pl.when(step == kind)
        def _(kind=kind):
            if kind == 3:
                total_s[...] += dot(w_ref[...], ggate_ref[...].reshape(C, flat))
            else:
                rows = back_ref[:, (kind + 1) * DH : (kind + 2) * DH, :].reshape(C, flat)
                part = dot(w_ref[...], rows)
                if kind == 0:
                    total_s[...] = part
                else:
                    total_s[...] += part

    @pl.when(step == 3)
    def _():
        normed = (act_ref[...].astype(F32) - mean_ref[...]) * inv_ref[...]
        grad_normed = total_s[...].T * gain_ref[...].reshape(1, C)
        grad_ref[...] = (
            inv_ref[...]
            * (
                grad_normed
                - jnp.mean(grad_normed, -1, keepdims=True)
                - normed * jnp.mean(grad_normed * normed, -1, keepdims=True)
            )
        ).astype(BF)


def input_grad(back, ggate, w_in, act, mean, inv_std, ln_gain):
    flat = act.shape[0]

    def whole(shape):
        return pl.BlockSpec(shape, lambda t: (0,) * len(shape))

    return pl.pallas_call(
        input_grad_kernel,
        grid=(4,),
        in_specs=[
            whole(back.shape),
            whole(ggate.shape),
            pl.BlockSpec((C, C), lambda t: (0, t)),
            whole((flat, C)),
            whole((flat, 1)),
            whole((flat, 1)),
            whole((C,)),
        ],
        out_specs=whole((flat, C)),
        out_shape=jax.ShapeDtypeStruct((flat, C), BF),
        scratch_shapes=[pltpu.VMEM((C, flat), F32)],
        compiler_params=params(60),
        cost_estimate=pl.CostEstimate(
            flops=2 * flat * C * 4 * C, bytes_accessed=8 * 2**20, transcendentals=0
        ),
        name="input_grad",
    )(back, ggate, w_in, act, mean, inv_std, ln_gain)


def weight_kernel(
    core_ref, back_ref, ggate_ref, o_ref, gated_ref, scaled_ref, dout_ref, wt_ref, gain_ref, out_ref, gated_s
):
    core = core_ref[0]
    flat = gated_ref.shape[1]
    gated_s[:flat] = gated_ref[...].T
    gated_s[flat:] = o_ref[8:12].reshape(C, flat).T
    sums = jnp.zeros((8, C), F32)
    tails = []
    for kind in range(4):
        blocks = [
            jnp.concatenate([head_rows(back_ref, ggate_ref, n, core), o_ref[n]], axis=1)
            for n in (2 * kind, 2 * kind + 1)
        ]
        win = dot(jnp.concatenate(blocks, axis=0), scaled_ref[...])
        wout = dot(dout_ref[2 * kind : 2 * kind + 2].reshape(128, 2 * flat), gated_s[...])
        weights = wt_ref[2 * kind : 2 * kind + 2].reshape(8 * DH, C).astype(F32)
        sums = sums + jnp.sum((win * weights).reshape(DH, 8, C), axis=0)
        for k in range(16):
            out_ref[kind * 16 + k, :16] = win[k * 24 : k * 24 + 16].astype(BF)
            tails.append((win[k * 24 + 16 : k * 24 + 24], wout[k * 8 : k * 8 + 8]))
    gain = jnp.sum(sums, axis=0, keepdims=True) / gain_ref[...].reshape(1, C)
    gain_hi = gain.astype(BF).astype(F32)
    row = lax.broadcasted_iota(jnp.int32, (8, C), 0)
    extra = jnp.where(row == 6, gain_hi, gain - gain_hi)
    for k, (win, wout) in enumerate(tails):
        out_ref[k, 16:] = jnp.concatenate([win, jnp.where(row >= 6, extra, wout)], axis=0).astype(BF)


def weight_grads(core, operands):
    def whole(shape):
        return pl.BlockSpec(shape, lambda t, core: (0,) * len(shape))

    flat = operands[3].shape[1]
    return pl.pallas_call(
        weight_kernel,
        grid_spec=pltpu.PrefetchScalarGridSpec(
            num_scalar_prefetch=1,
            grid=(1,),
            in_specs=[whole(o.shape) for o in operands],
            out_specs=whole((64, 32, C)),
            scratch_shapes=[pltpu.VMEM((2 * flat, C), BF)],
        ),
        out_shape=jax.ShapeDtypeStruct((64, 32, C), BF),
        compiler_params=params(24),
        cost_estimate=pl.CostEstimate(
            flops=2 * 2 * flat * C * 2048, bytes_accessed=8 * 2**20, transcendentals=0
        ),
        name="weight_grads",
    )(core, *operands)


def per_device(act, pair_bias, ln_gain, w_in, w_out, d_out):
    sample_count, row_count, channels = act.shape
    flat = sample_count * row_count
    core = lax.axis_index("core")
    core_arg = jnp.full((1,), core, jnp.int32)
    own_x = lax.axis_index("x")
    place = jnp.stack([core, own_x]).astype(jnp.int32)
    zh = lax.axis_index("zh")

    bias = lax.dynamic_slice(pair_bias, (zh * 8, (own_x * 2 + core) * 16, 0), (8, 16, KEYS))
    bias = lax.all_to_all(bias, ("zl", "y"), 0, 0, tiled=True)

    rows_out = d_out.reshape(flat, channels)
    act = act.reshape(flat, channels)
    scaled, mean, inv_std, send, gate, ggated = front(
        act, ln_gain, w_in, w_out, rows_out
    )
    bias, send = lax.optimization_barrier((bias, send))
    pieces = [bias] + [lax.ppermute(bias, "x", turn(s)) for s in (1, 2, 3)]
    received = lax.all_to_all(send, PLANE, 0, 0, tiled=True)

    dout_t = jnp.pad(rows_out.T.reshape(128, 6, flat), ((0, 0), (0, 2), (0, 0)))
    dout_t = dout_t.reshape(8, 2, 64, flat)
    dout_mine = lax.dynamic_index_in_dim(dout_t, core, 1, keepdims=False)
    dout_send = lax.dynamic_index_in_dim(dout_t, 1 - core, 1, keepdims=False)
    scaled_other = lax.ppermute(scaled, "core", SWAP)

    pieces, dout_mine, dout_send = lax.optimization_barrier((pieces, dout_mine, dout_send))
    bias = jnp.stack(pieces)
    bias_other = lax.ppermute(bias, "core", SWAP)
    dout_other = lax.ppermute(dout_send, "core", SWAP)
    received, dout_other, scaled_other, bias_other = lax.optimization_barrier(
        (received, dout_other, scaled_other, bias_other)
    )
    result, keep, give = attention(place, received, bias, bias_other)
    back = lax.all_to_all(result, PLANE, 0, 0, tiled=True)

    keep, scaled, scaled_other, dout_mine, dout_other = lax.optimization_barrier(
        (keep, scaled, scaled_other, dout_mine, dout_other)
    )
    got = lax.ppermute(give, "core", SWAP)
    sums = [(keep[s].astype(F32) + got[s].astype(F32)).astype(BF) for s in range(4)]
    gb = sums[0].astype(F32)
    for s in (1, 2, 3):
        gb = gb + lax.ppermute(sums[s], "x", turn(s)).astype(F32)
    staged = stage(core_arg, w_in, scaled, scaled_other, dout_mine, dout_other)
    back, gb, staged = lax.optimization_barrier((back, gb.astype(BF), staged))
    gb = lax.all_to_all(gb, PLANE, 0, 0, tiled=True)

    ggate, gated, half = gate_step(core_arg, back, gate, ggated)
    other = lax.ppermute(half, "core", SWAP)
    chunks = weight_grads(
        core_arg,
        (back, ggate, other, gated, in_vmem(staged[1]), in_vmem(staged[2]), in_vmem(staged[0]), ln_gain),
    )
    chunks, gated, ggate, gb = lax.optimization_barrier((chunks, gated, ggate, gb))
    grad_act = input_grad(back, ggate, w_in, act, mean, inv_std, ln_gain)
    gb = gb.astype(F32)
    grad_bias = jnp.concatenate([gb[:, :, :64], gb[:, :, 64:]], axis=1)
    output = jnp.einsum("cr,cd->rd", gated, w_out, preferred_element_type=F32).astype(BF)
    chunks = lax.all_to_all(chunks, ("x", "zh", "zl", "y"), 0, 0, tiled=True)
    total = jnp.sum(chunks.astype(F32), axis=0)
    gain = total[30] + total[31]
    return (
        output.reshape(sample_count, row_count, channels),
        grad_act.reshape(sample_count, row_count, channels),
        grad_bias,
        gain + lax.ppermute(gain, "core", SWAP),
        total[:24].T,
        total[24:30].T,
    )


def solution(mesh):
    fine = Mesh(mesh.devices.reshape(4, 2, 2, 2, 4), ("x", "zh", "core", "zl", "y"))
    sample = ("x", "zh", "core")
    tok = ("zl", "y")
    return jax.shard_map(
        per_device,
        mesh=fine,
        in_specs=(
            P(sample, tok, None),
            P(None, tok, None),
            P(),
            P(),
            P(),
            P(sample, tok, None),
        ),
        out_specs=(
            P(sample, tok, None),
            P(sample, tok, None),
            P(None, tok, sample),
            P(),
            P(None, sample + tok),
            P(None, sample + tok),
        ),
        check_vma=False,
    )
```
